128 devices in a mesh: section: 2 (over z_lo), fsdp: 8 (over y, core), replica: 8 (over x, z_hi).
Axes of the slice: x: 4, y: 4, z: 4 (z_hi: 2, z_lo: 2; z = z_hi * 2 + z_lo), core: 2. Of those that a mesh axis runs over, the one named last changes fastest.
Arguments:
- ends_in: bfloat16 [2, 16384, 1024], P('section', ('fsdp', 'replica')), may hold values from -6 to 6
- segment_ids: int32 [16384], P(('fsdp', 'replica')), may hold values from 0 to 15, as said below
- w_qkv: bfloat16 [2, 1024, 3072], P('section', 'fsdp'), may hold values from -0.1875 to 0.1875
- w_out: bfloat16 [2, 1024, 1024], P('section', 'fsdp'), may hold values from -0.375 to 0.375
- w_in: bfloat16 [2, 1024, 4096], P('section', 'fsdp'), may hold values from -0.1875 to 0.1875
- w_down: bfloat16 [2, 4096, 1024], P('section', 'fsdp'), may hold values from -0.09375 to 0.09375
- biases: bfloat16 [2, 6, 1024], P('section', None, 'fsdp'), may hold values from -3 to 3
- gains: bfloat16 [2, 2, 1024], P('section', None, 'fsdp'), may hold values from 0.5 to 1.5
- bias_in: bfloat16 [2, 4096], P('section', 'fsdp'), may hold values from -3 to 3
Outputs:
- ends_out: bfloat16 [2, 16384, 1024], P('section', ('fsdp', 'replica'))
- grad_qkv: float32 [2, 1024, 3072], P('section', 'fsdp')
- grad_out: float32 [2, 1024, 1024], P('section', 'fsdp')
- grad_in: float32 [2, 1024, 4096], P('section', 'fsdp')
- grad_down: float32 [2, 4096, 1024], P('section', 'fsdp')
- grad_biases: float32 [2, 6, 1024], P('section', None, 'fsdp')
- grad_gains: float32 [2, 2, 1024], P('section', None, 'fsdp')
- grad_bias_in: float32 [2, 4096], P('section', 'fsdp')
The draws below stay inside these ranges and needn't reach their ends.
Inputs may be any that keep to these rules, and one draw needn't show every extreme that they name: `segment_ids`: within each aligned block of 64 rows the ids start at 0 and never fall; tokens of a block with equal ids form one sequence, of uneven length. In some block of every draw the ids reach 15.
All inputs are finite; a program needn't handle non-finite values.
Results may differ from the reference program's by a relative error of at most 0.013.
Values may be sent and summed in bfloat16 or wider, within the bound.
A program may use at most 320 MiB of HBM per device.

```python
import jax
import jax.numpy as jnp
from jax import lax

D = 1024
FF = 4096
HEADS = 16
HEAD_DIM = 64
SEQ = 64
MICRO = 4
TOKENS = 16384
N_SECTION = 2
N_FSDP = 8


def draw_segment_ids(key, part):
    blocks = TOKENS // SEQ
    starts = jax.random.randint(jax.random.fold_in(key, 11), (blocks, SEQ), 0, 24) == 0
    position = jnp.arange(SEQ, dtype=jnp.int32)[None, :]
    marked = jax.random.randint(jax.random.fold_in(key, 23), (), 0, blocks)
    marked_rows = jnp.arange(blocks, dtype=jnp.int32)[:, None] == marked
    quarter = position % 4 == 0
    starts = jnp.logical_or(starts, jnp.logical_and(marked_rows, quarter))
    starts = jnp.logical_or(starts, position == 0)
    labels = jnp.cumsum(starts.astype(jnp.int32), axis=1) - 1
    labels = jnp.minimum(labels, SEQ // 4 - 1)
    return labels.reshape(TOKENS).astype(jnp.int32)


def block_levels(own_key, shape, shards, low, top_value):
    level, own = 1.0, jax.random.fold_in(own_key, 6)
    for dim, blocks in shards:
        draws = jnp.exp(jax.random.uniform(jax.random.fold_in(own, dim), (blocks,), jnp.float32, low / len(shards), top_value / len(shards)))
        level = level * jnp.repeat(draws, shape[dim] // blocks).reshape([-1 if axis == dim else 1 for axis in range(len(shape))])
    return level


def bell_draw(key, shape, deviation, reach, split=(), kind=jnp.bfloat16):
    drawn = jax.random.normal(key, shape, jnp.float32) * deviation
    if len(split) > 0:
        drawn = block_levels(key, shape, split, -0.22, 0.18) * drawn
    return jnp.clip(drawn, min=-reach, max=reach).astype(kind)


def setup_inputs(seed: int = 0) -> dict:
    arg_keys = jax.random.split(jax.random.key(seed), 10)
    return {
        "ends_in": bell_draw(arg_keys[0], (N_SECTION, TOKENS, D), 1.0, 6.0, ((0, 2), (1, 64))),
        "segment_ids": draw_segment_ids(jax.random.fold_in(arg_keys[9], 71), 0),
        "w_qkv": bell_draw(arg_keys[2], (N_SECTION, D, 3 * D), D ** -0.5, 0.1875, ((0, 2), (1, 8))),
        "w_out": bell_draw(arg_keys[3], (N_SECTION, D, D), (D // 4) ** -0.5, 0.375, ((0, 2), (1, 8))),
        "w_in": bell_draw(arg_keys[4], (N_SECTION, D, FF), D ** -0.5, 0.1875, ((0, 2), (1, 8))),
        "w_down": bell_draw(arg_keys[5], (N_SECTION, FF, D), FF ** -0.5, 0.09375, ((0, 2), (1, 8))),
        "biases": bell_draw(arg_keys[6], (N_SECTION, 6, D), 0.5, 3.0, ((0, 2), (2, 8))),
        "gains": jnp.clip(1.0 + 0.1 * jax.random.normal(arg_keys[7], (N_SECTION, 2, D), jnp.float32), 0.5, 1.5).astype(jnp.bfloat16),
        "bias_in": bell_draw(arg_keys[8], (N_SECTION, FF), 0.5, 3.0, ((0, 2), (1, 8))),
    }


EPSILON = 1e-05

def to_float(array_in):
    return lax.optimization_barrier(array_in).astype(jnp.float32)

def norm_forward(summed, gain_row, offset):
    center = summed - lax.optimization_barrier(jnp.mean(summed, axis=-1, keepdims=True))
    inverse = lax.rsqrt(lax.optimization_barrier(jnp.mean(center * center, axis=-1, keepdims=True)) + EPSILON)
    normed = center * inverse
    return (normed * gain_row + offset, normed, inverse)

def norm_backward(grad_rows, normed, inverse, gain_row):
    scaled = grad_rows * gain_row
    return inverse * (scaled - lax.optimization_barrier(jnp.mean(scaled, axis=-1, keepdims=True)) - normed * lax.optimization_barrier(jnp.mean(scaled * normed, axis=-1, keepdims=True)))

def gelu_slope(pre_act):
    return 0.5 * (1.0 + lax.erf(pre_act * 0.7071067811865476)) + pre_act * jnp.exp(-0.5 * pre_act * pre_act) * 0.3989422804014327

def masked_scores(query_heads, key_heads, segment):
    score_scale = HEAD_DIM ** (-0.5)
    scores = jnp.einsum('qhd,khd->hqk', query_heads, key_heads) * score_scale
    same_block = segment[:, None] == segment[None, :]
    return jnp.where(same_block[None], scores, -1e+30)

def attend(query_rows, key_rows, value_rows, segment):
    row_count = query_rows.shape[0]
    query_heads = to_float(query_rows).reshape(row_count, HEADS, HEAD_DIM)
    key_heads = to_float(key_rows).reshape(row_count, HEADS, HEAD_DIM)
    value_heads = to_float(value_rows).reshape(row_count, HEADS, HEAD_DIM)
    scores = masked_scores(query_heads, key_heads, segment)
    row_peak = lax.optimization_barrier(jnp.max(scores, axis=-1, keepdims=True))
    exponent = jnp.exp(scores - row_peak)
    row_total = lax.optimization_barrier(jnp.sum(exponent, axis=-1, keepdims=True))
    weights = to_float((exponent / row_total).astype(jnp.bfloat16))
    log_total = row_peak + jnp.log(row_total)
    context = jnp.einsum('hqk,khd->qhd', weights, value_heads).reshape(row_count, HEADS * HEAD_DIM)
    return (context.astype(jnp.bfloat16), log_total)

def attend_backward(query_rows, key_rows, value_rows, log_total, context_grad, segment):
    row_count = query_rows.shape[0]
    query_heads = to_float(query_rows).reshape(row_count, HEADS, HEAD_DIM)
    key_heads = to_float(key_rows).reshape(row_count, HEADS, HEAD_DIM)
    value_heads = to_float(value_rows).reshape(row_count, HEADS, HEAD_DIM)
    grad_heads = to_float(context_grad).reshape(row_count, HEADS, HEAD_DIM)
    probabilities = jnp.exp(masked_scores(query_heads, key_heads, segment) - log_total)
    prob_low = to_float(probabilities.astype(jnp.bfloat16))
    value_grad = jnp.einsum('hqk,qhd->khd', prob_low, grad_heads)
    weight_grad = jnp.einsum('qhd,khd->hqk', grad_heads, value_heads)
    row_inner = lax.optimization_barrier(jnp.sum(probabilities * weight_grad, axis=-1, keepdims=True))
    score_grad = probabilities * (weight_grad - row_inner) * HEAD_DIM ** (-0.5)
    score_low = to_float(score_grad.astype(jnp.bfloat16))
    query_grad = jnp.einsum('hqk,khd->qhd', score_low, key_heads)
    key_grad = jnp.einsum('hqk,qhd->khd', score_low, query_heads)
    shape_out = (row_count, HEADS * HEAD_DIM)
    return (query_grad.reshape(shape_out), key_grad.reshape(shape_out), value_grad.reshape(shape_out))

def layer_forward(params, rows_in, segment):
    w_qkv, w_out, w_in, w_down, biases, gains, bias_in = params
    model_width = w_out.shape[0]
    group_count = segment.shape[0]

    def by_block(rows_flat):
        return rows_flat.reshape(group_count, SEQ, model_width)
    projected = jnp.dot(rows_in, w_qkv, preferred_element_type=jnp.float32)
    query_rows = (projected[:, :model_width] + biases[0]).astype(jnp.bfloat16)
    key_rows = projected[:, model_width:2 * model_width].astype(jnp.bfloat16)
    value_rows = (projected[:, 2 * model_width:] + biases[1]).astype(jnp.bfloat16)
    context, log_total = jax.vmap(attend)(by_block(query_rows), by_block(key_rows), by_block(value_rows), segment)
    context = context.reshape(rows_in.shape[0], model_width)
    first_sum = to_float(rows_in) + jnp.dot(context, w_out, preferred_element_type=jnp.float32) + biases[2]
    normed_out, first_normed, first_inverse = norm_forward(first_sum, gains[0], biases[3])
    normed_low = normed_out.astype(jnp.bfloat16)
    pre_act = jnp.dot(normed_low, w_in, preferred_element_type=jnp.float32) + bias_in
    activated = jax.nn.gelu(pre_act, approximate=False).astype(jnp.bfloat16)
    second_sum = normed_out + jnp.dot(activated, w_down, preferred_element_type=jnp.float32) + biases[4]
    result, second_normed, second_inverse = norm_forward(second_sum, gains[1], biases[5])
    kept_values = (rows_in, query_rows, key_rows, value_rows, log_total, context, first_normed, first_inverse, normed_low, pre_act, activated, second_normed, second_inverse, segment)
    return (result.astype(jnp.bfloat16), kept_values)

def layer_backward(params, kept_values, cotangent):
    w_qkv, w_out, w_in, w_down, biases, gains, bias_in = params
    rows_in, query_rows, key_rows, value_rows, log_total, context, first_normed, first_inverse, normed_low, pre_act, activated, second_normed, second_inverse, segment = kept_values
    model_width = w_out.shape[0]
    group_count = segment.shape[0]

    def by_block(rows_flat):
        return rows_flat.reshape(group_count, SEQ, model_width)
    second_grad = norm_backward(cotangent, second_normed, second_inverse, gains[1])
    second_low = second_grad.astype(jnp.bfloat16)
    grad_down = jnp.dot(activated.T, second_low, preferred_element_type=jnp.float32)
    act_grad = jnp.dot(second_low, w_down.T, preferred_element_type=jnp.float32)
    pre_grad = act_grad * gelu_slope(pre_act)
    pre_low = pre_grad.astype(jnp.bfloat16)
    grad_in = jnp.dot(normed_low.T, pre_low, preferred_element_type=jnp.float32)
    normed_grad = second_grad + jnp.dot(pre_low, w_in.T, preferred_element_type=jnp.float32)
    first_grad = norm_backward(normed_grad, first_normed, first_inverse, gains[0])
    first_low = first_grad.astype(jnp.bfloat16)
    grad_out = jnp.dot(context.T, first_low, preferred_element_type=jnp.float32)
    context_grad = jnp.dot(first_low, w_out.T, preferred_element_type=jnp.float32).astype(jnp.bfloat16)
    query_grad, key_grad, value_grad = jax.vmap(attend_backward)(by_block(query_rows), by_block(key_rows), by_block(value_rows), log_total, by_block(context_grad), segment)
    row_total = rows_in.shape[0]
    query_grad = query_grad.reshape(row_total, model_width)
    key_grad = key_grad.reshape(row_total, model_width)
    value_grad = value_grad.reshape(row_total, model_width)
    joined = jnp.concatenate([query_grad, key_grad, value_grad], axis=1).astype(jnp.bfloat16)
    grad_qkv = jnp.dot(rows_in.T, joined, preferred_element_type=jnp.float32)
    input_grad = first_grad + jnp.dot(joined, w_qkv.T, preferred_element_type=jnp.float32)
    bias_grads = jnp.stack([lax.optimization_barrier(jnp.sum(query_grad, axis=0)), lax.optimization_barrier(jnp.sum(value_grad, axis=0)), lax.optimization_barrier(jnp.sum(first_grad, axis=0)), lax.optimization_barrier(jnp.sum(normed_grad, axis=0)), lax.optimization_barrier(jnp.sum(second_grad, axis=0)), lax.optimization_barrier(jnp.sum(cotangent, axis=0))])
    gain_grads = jnp.stack([lax.optimization_barrier(jnp.sum(normed_grad * first_normed, axis=0)), lax.optimization_barrier(jnp.sum(cotangent * second_normed, axis=0))])
    return (input_grad, (grad_qkv, grad_out, grad_in, grad_down, bias_grads, gain_grads, lax.optimization_barrier(jnp.sum(pre_grad, axis=0))))

def reference(ends_in, segment_ids, w_qkv, w_out, w_in, w_down, biases, gains, bias_in):
    blocks = ends_in.shape[1] // SEQ
    group_blocks = MICRO * N_FSDP
    groups = blocks // group_blocks
    group_rows = group_blocks * SEQ
    inputs = ends_in[0].reshape(groups, group_rows, D)
    cotangents = ends_in[1].reshape(groups, group_rows, D)
    segments = segment_ids.reshape(groups, group_blocks, SEQ)
    stacks = (w_qkv, w_out, w_in, w_down, biases, gains, bias_in)
    layers = [tuple((member[layer_index] for member in stacks)) for layer_index in range(N_SECTION)]
    zero_totals = tuple((jnp.zeros(member.shape, jnp.float32) for member in stacks))

    def advance(totals, block_data):
        rows_in, cot_in, segment = block_data
        saved_values = []
        hidden = rows_in
        for layer_index in range(N_SECTION):
            hidden, kept_values = layer_forward(layers[layer_index], hidden, segment)
            saved_values.append(kept_values)
        cotangent = to_float(cot_in)
        updated = list(totals)
        backward_low = cot_in
        for layer_index in reversed(range(N_SECTION)):
            backward, gradients = layer_backward(layers[layer_index], saved_values[layer_index], cotangent)
            updated = [running.at[layer_index].add(increment) for running, increment in zip(updated, gradients)]
            backward_low = backward.astype(jnp.bfloat16)
            cotangent = to_float(backward_low)
        return (tuple(updated), (hidden, backward_low))
    totals, (outputs_last, inputs_grad) = lax.scan(advance, zero_totals, (inputs, cotangents, segments))
    ends_out = jnp.stack([inputs_grad.reshape(-1, D), outputs_last.reshape(-1, D)])
    return (ends_out, totals[0], totals[1], totals[2], totals[3], totals[4], totals[5], totals[6])
```

```python
import jax
import jax.numpy as jnp
from jax import lax
from jax.experimental import pallas as pl
from jax.experimental.pallas import tpu as pltpu
from jax.sharding import PartitionSpec as P

HEADS = 16
HEAD_DIM = 64
SEQ = 64
MICRO = 4


EPSILON = 1e-05


MESH = pl.DeviceIdType.MESH
N_F = 8
TILE = 128
SMALL_ROWS = 16
PAYLOAD = 97 * TILE
VMEM_CAP = 60 * 1024 * 1024

GATHER_PLAN = ((128, 3072, 16), (128, 1024, 16), (128, 4096, 16), (512, 1024, 128), (16, 256, 0))


def place():
    f = lax.axis_index("fsdp")
    r = lax.axis_index("replica")
    return f // 2, lax.rem(f, 2), r // 2, lax.rem(r, 2)


def device(y, c, x, z):
    return {"fsdp": y * 2 + c, "replica": x * 2 + z}


def step_on(index, distance):
    return lax.rem(index + distance + 4, 4)


def greet(peers):
    barrier = pltpu.get_barrier_semaphore()
    for peer in peers:
        pl.semaphore_signal(barrier, inc=1, device_id=peer, device_id_type=MESH)
    pl.semaphore_wait(barrier, len(peers))


class Copies:
    def __init__(self, send_sem, recv_sem):
        self.send_sem, self.recv_sem, self.started = send_sem, recv_sem, []

    def start(self, src, dst, peer):
        number = len(self.started)
        copy = pltpu.make_async_remote_copy(
            src_ref=src,
            dst_ref=dst,
            send_sem=self.send_sem.at[number],
            recv_sem=self.recv_sem.at[number],
            device_id=peer,
            device_id_type=MESH,
        )
        copy.start()
        self.started.append(copy)
        return copy

    def finish(self):
        for copy in self.started:
            copy.wait_send()


def gather_kernel(*refs):
    count = len(GATHER_PLAN)
    ins, outs = refs[:count], refs[count : 2 * count]
    send_sem, recv_sem, local_sem = refs[2 * count :]
    y, c, x, z = place()
    right_y, left_y = device(step_on(y, 1), c, x, z), device(step_on(y, -1), c, x, z)
    right_x, left_x = device(y, c, step_on(x, 1), z), device(y, c, step_on(x, -1), z)
    sibling = device(y, 1 - c, x, z)
    greet((right_y, left_y, right_x, left_x, sibling))
    copies = Copies(send_sem, recv_sem)

    def span(k, owner_y, first, rows, part=None):
        shard_rows, columns, _ = GATHER_PLAN[k]
        start = pl.multiple_of((owner_y * 2 + c) * shard_rows + first, 16)
        if part is None:
            return outs[k].at[pl.ds(start, rows), :]
        half = columns // 2
        return outs[k].at[pl.ds(start, rows), pl.ds(part * half, half)]

    def quarter(k, owner_x):
        return pl.multiple_of(owner_x * GATHER_PLAN[k][2], 16)

    relayed = [k for k in range(count) if GATHER_PLAN[k][2]]
    direct = [k for k in range(count) if GATHER_PLAN[k][0] > 4 * GATHER_PLAN[k][2]]
    first_right, first_left = {}, {}
    for kind, members in (("relay", relayed), ("direct", direct)):
        for k in members:
            shard_rows, _, piece = GATHER_PLAN[k]
            if kind == "relay":
                first, rows = quarter(k, x), piece
            else:
                first, rows = 4 * piece, shard_rows - 4 * piece
            src = ins[k].at[pl.ds(first, rows), :]
            first_right[kind, k] = copies.start(src, span(k, y, first, rows), right_y)
            first_left[kind, k] = copies.start(src, span(k, y, first, rows), left_y)
    own = []
    sibling_copies = []
    for k in range(count):
        shard_rows = GATHER_PLAN[k][0]
        own.append(pltpu.make_async_copy(ins[k], span(k, y, 0, shard_rows), local_sem.at[k]))
        own[-1].start()
        sibling_copies.append(copies.start(ins[k], span(k, y, 0, shard_rows), sibling))

    before, after, across = step_on(y, -1), step_on(y, 1), step_on(y, 2)
    second_right, second_left = {}, {}
    along_right, along_left = {}, {}
    for kind, members in (("relay", relayed), ("direct", direct)):
        for k in members:
            shard_rows, _, piece = GATHER_PLAN[k]
            if kind == "relay":
                first, rows = quarter(k, x), piece
            else:
                first, rows = 4 * piece, shard_rows - 4 * piece
            first_right[kind, k].wait_recv()
            block = span(k, before, first, rows, 0)
            second_right[kind, k] = copies.start(block, block, right_y)
            first_left[kind, k].wait_recv()
            block = span(k, after, first, rows, 1)
            second_left[kind, k] = copies.start(block, block, left_y)
            if kind == "relay":
                for n, owner in ((0, before), (1, after)):
                    block = span(k, owner, first, rows)
                    along_right[n, k] = copies.start(block, block, right_x)
                    along_left[n, k] = copies.start(block, block, left_x)
    for k in relayed:
        second_right["relay", k].wait_recv()
        second_left["relay", k].wait_recv()
        block = span(k, across, quarter(k, x), GATHER_PLAN[k][2])
        along_right[2, k] = copies.start(block, block, right_x)
        along_left[2, k] = copies.start(block, block, left_x)
    further = {}
    owners = (before, after, across)
    for n in range(3):
        for k in relayed:
            piece = GATHER_PLAN[k][2]
            along_right[n, k].wait_recv()
            block = span(k, owners[n], quarter(k, step_on(x, -1)), piece, 0)
            further[n, k, 0] = copies.start(block, block, right_x)
            along_left[n, k].wait_recv()
            block = span(k, owners[n], quarter(k, step_on(x, 1)), piece, 1)
            further[n, k, 1] = copies.start(block, block, left_x)
    for n in range(3):
        for k in range(count):
            shard_rows = GATHER_PLAN[k][0]
            if n == 2 and k in direct:
                second_right["direct", k].wait_recv()
                second_left["direct", k].wait_recv()
            if k in relayed:
                further[n, k, 0].wait_recv()
                further[n, k, 1].wait_recv()
            block = span(k, owners[n], 0, shard_rows)
            sibling_copies.append(copies.start(block, block, sibling))
    for copy in own:
        copy.wait()
    for copy in sibling_copies:
        copy.wait_recv()
    copies.finish()


def gather_weights(*shards):
    copies = 160
    return pl.pallas_call(
        gather_kernel,
        out_shape=[
            jax.ShapeDtypeStruct((N_F * rows, columns), jnp.bfloat16)
            for rows, columns, _ in GATHER_PLAN
        ],
        in_specs=[pl.BlockSpec(memory_space=pl.ANY)] * len(GATHER_PLAN),
        out_specs=[pl.BlockSpec(memory_space=pl.ANY)] * len(GATHER_PLAN),
        scratch_shapes=[
            pltpu.SemaphoreType.DMA((copies,)),
            pltpu.SemaphoreType.DMA((copies,)),
            pltpu.SemaphoreType.DMA((len(GATHER_PLAN),)),
        ],
        compiler_params=pltpu.CompilerParams(
            collective_id=0, has_side_effects=True, vmem_limit_bytes=4 * 1024 * 1024
        ),
        name="gather_weights",
    )(*shards)


REDUCE_PLAN = ((8, 8, "y"), (8, 8, "x"), (8, 8, "y"), (8, 8, "y"), (8, 8, "x"), (8, 9, "y"))


def stage_shape(plan, stage):
    part_a, part_b, leading = plan
    rows = {("y", 0): (1, 128), ("x", 0): (4, 32), ("y", 1): (1, 32), ("x", 1): (1, 32)}
    blocks, height = rows[leading, stage]
    return blocks, height, (part_a + part_b) * TILE


def add_into(target, rows, columns, sources, dest=None):
    blocks, first_block, height, first_row = rows
    first_column, width = columns

    def one(step, carry):
        block, row = step // (height // 16), lax.rem(step, height // 16) * 16
        here = (
            first_block + block,
            pl.ds(pl.multiple_of(first_row + row, 16), 16),
            pl.ds(first_column, width),
        )
        total = target[here].astype(jnp.float32)
        for ref, base, column in sources:
            total = total + ref[
                base + block, pl.ds(pl.multiple_of(row, 16), 16), pl.ds(column, width)
            ].astype(jnp.float32)
        if dest is None:
            target[here] = total.astype(jnp.bfloat16)
        else:
            dest[pl.ds(pl.multiple_of(row, 16), 16), pl.ds(first_column, width)] = total.astype(
                jnp.bfloat16
            )
        return carry

    lax.fori_loop(0, blocks * (height // 16), one, 0)


def reduce_kernel(parts, out, held, paired, final, crossed, *rest):
    stage_refs, (send_sem, recv_sem, local_sem) = rest[:-3], rest[-3:]
    y, c, x, z = place()
    ring = {
        "y": (y, device(step_on(y, 1), c, x, z), device(step_on(y, -1), c, x, z)),
        "x": (x, device(y, c, step_on(x, 1), z), device(y, c, step_on(x, -1), z)),
    }
    sibling = device(y, 1 - c, x, z)
    partner = device(y, c, x, 1 - z)
    greet((ring["y"][1], ring["y"][2], ring["x"][1], ring["x"][2], sibling, partner))
    copies = Copies(send_sem, recv_sem)
    own, from_sibling, from_here, offset = [], [], [], 0
    offsets = []
    for n, (part_a, part_b, _) in enumerate(REDUCE_PLAN):
        width = (part_a + part_b) * TILE
        columns = pl.ds(offset, width)
        from_sibling.append(
            copies.start(parts.at[:, 1 - c, :, columns], paired.at[:, :, columns], sibling)
        )
        local = pltpu.make_async_copy(
            parts.at[:, c, :, columns], held.at[:, :, columns], local_sem.at[n]
        )
        local.start()
        from_here.append(local)
        offsets.append(offset)
        offset += width

    def along(n, stage):
        part_a, part_b, leading = REDUCE_PLAN[n]
        wide_a, wide_b = part_a * TILE, part_b * TILE
        start_a, start_b = offsets[n], offsets[n] + wide_a
        axis = leading if stage == 0 else ("x" if leading == "y" else "y")
        index, right, left = ring[axis]
        blocks, height, _ = stage_shape(REDUCE_PLAN[n], stage)
        landing = stage_refs[2 * n + stage]

        def origin(at):
            if axis == "y":
                return at, (0 if stage == 0 else x * 32)
            return (0 if stage == 0 else y), at * 32

        def take(at, start, wide):
            block, row = origin(at)
            return held.at[
                pl.ds(block, blocks), pl.ds(pl.multiple_of(row, 16), height), pl.ds(start, wide)
            ]

        def land(slot, start, wide):
            return landing.at[pl.ds(slot * blocks, blocks), :, pl.ds(start - offsets[n], wide)]

        def add(at, start, wide, slots):
            block, row = origin(at)
            add_into(
                held,
                (blocks, block, height, row),
                (start, wide),
                [(landing, slot * blocks, start - offsets[n]) for slot in slots],
            )

        ahead, behind, across = step_on(index, 1), step_on(index, -1), step_on(index, 2)
        far_right = copies.start(take(across, start_a, wide_a), land(0, start_a, wide_a), right)
        far_left = copies.start(take(across, start_b, wide_b), land(0, start_b, wide_b), left)
        near = [
            copies.start(take(ahead, start_b, wide_b), land(1, start_b, wide_b), right),
            copies.start(take(behind, start_a, wide_a), land(2, start_a, wide_a), left),
        ]
        yield
        far_right.wait_recv()
        add(ahead, start_a, wide_a, (0,))
        near.append(copies.start(take(ahead, start_a, wide_a), land(1, start_a, wide_a), right))
        far_left.wait_recv()
        add(behind, start_b, wide_b, (0,))
        near.append(copies.start(take(behind, start_b, wide_b), land(2, start_b, wide_b), left))
        yield
        for copy in near:
            copy.wait_recv()
        add(index, start_a, wide_a + wide_b, (1, 2))

    def chunk(n):
        part_a, part_b, _ = REDUCE_PLAN[n]
        start, wide_a, wide = offsets[n], part_a * TILE, (part_a + part_b) * TILE
        columns = pl.ds(start, wide)
        from_here[n].wait()
        from_sibling[n].wait_recv()
        add_into(held, (4, 0, 128, 0), (start, wide), [(paired, 0, start)])
        yield from along(n, 0)
        yield from along(n, 1)
        rows = pl.ds(pl.multiple_of(x * 32, 16), 32)
        swap = copies.start(held.at[pl.ds(y, 1), rows, columns], crossed.at[:, :, columns], partner)
        yield
        swap.wait_recv()
        add_into(held, (1, y, 32, x * 32), (start, wide), [(crossed, 0, start)], dest=final)
        kept = pltpu.make_async_copy(
            final.at[:, columns], out.at[rows, columns], local_sem.at[len(REDUCE_PLAN) + n]
        )
        kept.start()
        own.append(kept)
        _, right, left = ring["x"]
        to_right = copies.start(final.at[:, columns], out.at[rows, columns], right)
        to_left = copies.start(final.at[:, columns], out.at[rows, columns], left)
        yield
        to_right.wait_recv()
        block = out.at[
            pl.ds(pl.multiple_of(step_on(x, -1) * 32, 16), 32), pl.ds(start, wide_a)
        ]
        last = [copies.start(block, block, right)]
        to_left.wait_recv()
        block = out.at[
            pl.ds(pl.multiple_of(step_on(x, 1) * 32, 16), 32), pl.ds(start + wide_a, wide - wide_a)
        ]
        last.append(copies.start(block, block, left))
        yield
        for copy in last:
            copy.wait_recv()

    waiting = [chunk(n) for n in range(len(REDUCE_PLAN))]
    running = []
    while waiting or running:
        if waiting:
            running.append(waiting.pop(0))
        for member in list(running):
            if next(member, "end") == "end":
                running.remove(member)
    for copy in own:
        copy.wait()
    copies.finish()


def reduce_parts(parts):
    chunks = len(REDUCE_PLAN)
    landing = []
    for plan in REDUCE_PLAN:
        for stage in (0, 1):
            blocks, height, width = stage_shape(plan, stage)
            landing.append(pltpu.VMEM((3 * blocks, height, width), jnp.bfloat16))
    return pl.pallas_call(
        reduce_kernel,
        out_shape=jax.ShapeDtypeStruct((128, PAYLOAD), jnp.bfloat16),
        in_specs=[pl.BlockSpec(memory_space=pl.ANY)],
        out_specs=pl.BlockSpec(memory_space=pl.ANY),
        scratch_shapes=[
            pltpu.VMEM((4, 128, PAYLOAD), jnp.bfloat16),
            pltpu.VMEM((4, 128, PAYLOAD), jnp.bfloat16),
            pltpu.VMEM((32, PAYLOAD), jnp.bfloat16),
            pltpu.VMEM((1, 32, PAYLOAD), jnp.bfloat16),
            *landing,
            pltpu.SemaphoreType.DMA((chunks * 18,)),
            pltpu.SemaphoreType.DMA((chunks * 18,)),
            pltpu.SemaphoreType.DMA((chunks * 2,)),
        ],
        compiler_params=pltpu.CompilerParams(
            collective_id=1, has_side_effects=True, vmem_limit_bytes=VMEM_CAP
        ),
        name="reduce_parts",
    )(parts)


def norm_forward(summed, gain_row, offset):
    center = summed - jnp.mean(summed, axis=-1, keepdims=True)
    inverse = lax.rsqrt(jnp.mean(center * center, axis=-1, keepdims=True) + EPSILON)
    normed = center * inverse
    return (normed * gain_row + offset, normed, inverse)


def norm_backward(grad_rows, normed, inverse, gain_row):
    scaled = grad_rows * gain_row
    return inverse * (
        scaled
        - jnp.mean(scaled, axis=-1, keepdims=True)
        - normed * jnp.mean(scaled * normed, axis=-1, keepdims=True)
    )


def gelu_slope(pre_act):
    return (
        0.5 * (1.0 + lax.erf(pre_act * 0.7071067811865476))
        + pre_act * jnp.exp(-0.5 * pre_act * pre_act) * 0.3989422804014327
    )


def masked_scores(query_heads, key_heads, segment):
    scores = jnp.einsum(
        "qhd,khd->hqk", query_heads, key_heads, preferred_element_type=jnp.float32
    ) * HEAD_DIM ** (-0.5)
    same_block = segment[:, None] == segment[None, :]
    return jnp.where(same_block[None], scores, -1e30)


def split_heads(rows_low):
    return rows_low.reshape(rows_low.shape[0], HEADS, HEAD_DIM)


def attend(query_rows, key_rows, value_rows, segment):
    scores = masked_scores(split_heads(query_rows), split_heads(key_rows), segment)
    row_peak = jnp.max(scores, axis=-1, keepdims=True)
    exponent = jnp.exp(scores - row_peak)
    row_total = jnp.sum(exponent, axis=-1, keepdims=True)
    weights = (exponent / row_total).astype(jnp.bfloat16)
    log_total = row_peak + jnp.log(row_total)
    context = jnp.einsum(
        "hqk,khd->qhd", weights, split_heads(value_rows), preferred_element_type=jnp.float32
    )
    return (context.reshape(query_rows.shape).astype(jnp.bfloat16), log_total)


def attend_backward(query_rows, key_rows, value_rows, log_total, context_grad, segment):
    query_heads = split_heads(query_rows)
    key_heads = split_heads(key_rows)
    grad_heads = split_heads(context_grad)
    probabilities = jnp.exp(masked_scores(query_heads, key_heads, segment) - log_total)
    prob_low = probabilities.astype(jnp.bfloat16)
    value_grad = jnp.einsum(
        "hqk,qhd->khd", prob_low, grad_heads, preferred_element_type=jnp.float32
    )
    weight_grad = jnp.einsum(
        "qhd,khd->hqk", grad_heads, split_heads(value_rows), preferred_element_type=jnp.float32
    )
    row_inner = jnp.sum(probabilities * weight_grad, axis=-1, keepdims=True)
    score_low = (probabilities * (weight_grad - row_inner) * HEAD_DIM ** (-0.5)).astype(
        jnp.bfloat16
    )
    query_grad = jnp.einsum(
        "hqk,khd->qhd", score_low, key_heads, preferred_element_type=jnp.float32
    )
    key_grad = jnp.einsum(
        "hqk,qhd->khd", score_low, query_heads, preferred_element_type=jnp.float32
    )
    shape_out = query_rows.shape
    return (
        query_grad.reshape(shape_out),
        key_grad.reshape(shape_out),
        value_grad.reshape(shape_out),
    )


def layer_forward(params, rows_in, segment):
    w_qkv, w_out, w_in, w_down, biases, gains, bias_in = params
    model_width = w_out.shape[0]
    projected = jnp.dot(rows_in, w_qkv, preferred_element_type=jnp.float32)
    query_rows = (projected[:, :model_width] + biases[0]).astype(jnp.bfloat16)
    key_rows = projected[:, model_width : 2 * model_width].astype(jnp.bfloat16)
    value_rows = (projected[:, 2 * model_width :] + biases[1]).astype(jnp.bfloat16)
    context, log_total = jax.vmap(attend)(
        by_block(query_rows), by_block(key_rows), by_block(value_rows), segment.reshape(MICRO, SEQ)
    )
    context = context.reshape(rows_in.shape)
    first_sum = (
        rows_in.astype(jnp.float32)
        + jnp.dot(context, w_out, preferred_element_type=jnp.float32)
        + biases[2]
    )
    normed_out, first_normed, first_inverse = norm_forward(first_sum, gains[0], biases[3])
    normed_low = normed_out.astype(jnp.bfloat16)
    pre_act = jnp.dot(normed_low, w_in, preferred_element_type=jnp.float32) + bias_in
    activated = jax.nn.gelu(pre_act, approximate=False).astype(jnp.bfloat16)
    second_sum = (
        normed_out + jnp.dot(activated, w_down, preferred_element_type=jnp.float32) + biases[4]
    )
    result, second_normed, second_inverse = norm_forward(second_sum, gains[1], biases[5])
    kept_values = (
        rows_in,
        query_rows,
        key_rows,
        value_rows,
        log_total,
        context,
        first_normed,
        first_inverse,
        normed_low,
        pre_act,
        activated,
        second_normed,
        second_inverse,
        segment,
    )
    return (result.astype(jnp.bfloat16), kept_values)


def layer_backward(params, kept_values, cotangent):
    w_qkv, w_out, w_in, w_down, biases, gains, bias_in = params
    (
        rows_in,
        query_rows,
        key_rows,
        value_rows,
        log_total,
        context,
        first_normed,
        first_inverse,
        normed_low,
        pre_act,
        activated,
        second_normed,
        second_inverse,
        segment,
    ) = kept_values
    second_grad = norm_backward(cotangent, second_normed, second_inverse, gains[1])
    second_low = second_grad.astype(jnp.bfloat16)
    act_grad = jnp.dot(second_low, w_down.T, preferred_element_type=jnp.float32)
    pre_grad = act_grad * gelu_slope(pre_act)
    pre_low = pre_grad.astype(jnp.bfloat16)
    normed_grad = second_grad + jnp.dot(pre_low, w_in.T, preferred_element_type=jnp.float32)
    first_grad = norm_backward(normed_grad, first_normed, first_inverse, gains[0])
    first_low = first_grad.astype(jnp.bfloat16)
    context_grad = jnp.dot(first_low, w_out.T, preferred_element_type=jnp.float32).astype(
        jnp.bfloat16
    )
    query_grad, key_grad, value_grad = jax.vmap(attend_backward)(
        by_block(query_rows),
        by_block(key_rows),
        by_block(value_rows),
        log_total,
        by_block(context_grad),
        segment.reshape(MICRO, SEQ),
    )
    query_grad, key_grad, value_grad = (
        member.reshape(first_low.shape) for member in (query_grad, key_grad, value_grad)
    )
    joined = jnp.concatenate([query_grad, key_grad, value_grad], axis=1).astype(jnp.bfloat16)
    input_grad = first_grad + jnp.dot(joined, w_qkv.T, preferred_element_type=jnp.float32)
    bias_grads = jnp.stack(
        [
            jnp.sum(query_grad, axis=0),
            jnp.sum(value_grad, axis=0),
            jnp.sum(first_grad, axis=0),
            jnp.sum(normed_grad, axis=0),
            jnp.sum(second_grad, axis=0),
            jnp.sum(cotangent, axis=0),
        ]
    )
    gain_grads = jnp.stack(
        [jnp.sum(normed_grad * first_normed, axis=0), jnp.sum(cotangent * second_normed, axis=0)]
    )
    low_parts = (joined, first_low, pre_low, second_low)
    return (input_grad, low_parts, (bias_grads, gain_grads, jnp.sum(pre_grad, axis=0)))


def by_block(rows):
    return rows.reshape(MICRO, SEQ, rows.shape[-1])


def pack_small(biases, gains, bias_in):
    rows = jnp.concatenate([biases, gains, bias_in.reshape(4, TILE)], axis=0)
    return jnp.pad(rows, ((0, 4), (0, TILE)))


def unpack_small(gathered):
    rows = gathered.reshape(N_F, SMALL_ROWS, 2 * TILE)[:, :12, :TILE]
    wide = jnp.swapaxes(rows[:, :8], 0, 1).reshape(8, N_F * TILE)
    return wide[:6], wide[6:], rows[:, 8:].reshape(N_F * 4 * TILE)


def join_parts(part_qkv, part_out, part_in, part_down, small_sums):
    bias_grads, gain_grads, bias_in_grads = small_sums
    wide = jnp.concatenate([bias_grads, gain_grads], axis=0)
    small = jnp.concatenate(
        [
            jnp.swapaxes(wide.reshape(8, N_F, TILE), 0, 1),
            bias_in_grads.reshape(N_F, 4, TILE),
            jnp.zeros((N_F, 116, TILE), jnp.float32),
        ],
        axis=1,
    )
    down = jnp.swapaxes(part_down.reshape(N_F, 4, TILE, 1024), 1, 2)
    parts = [
        part_qkv.reshape(N_F, TILE, 3072),
        part_out.reshape(N_F, TILE, 1024),
        part_in.reshape(N_F, TILE, 4096),
        down.reshape(N_F, TILE, 4096),
        small.astype(jnp.bfloat16),
    ]
    return jnp.concatenate(parts, axis=2).reshape(4, 2, TILE, PAYLOAD)


def split_total(total):
    small = total[:, 12288:]
    return (
        total[:, :3072],
        total[:, 3072:4096],
        total[:, 4096:8192],
        jnp.swapaxes(total[:, 8192:12288].reshape(TILE, 4, 1024), 0, 1).reshape(512, 1024),
        small[:6],
        small[6:8],
        small[8:12].reshape(512),
    )


def body(ends_in, segment_ids, w_qkv, w_out, w_in, w_down, biases, gains, bias_in):
    section_index = lax.axis_index("section")
    is_first = section_index == 0
    local_rows = ends_in[0]
    gathered = gather_weights(
        w_qkv[0], w_out[0], w_in[0], w_down[0], pack_small(biases[0], gains[0], bias_in[0])
    )
    params = (*gathered[:4], *unpack_small(gathered[4]))
    early, _ = layer_forward(params, local_rows, segment_ids)
    carried = lax.ppermute(early, "section", [(0, 1)])
    result, kept_values = layer_forward(
        params, jnp.where(is_first, local_rows, carried), segment_ids
    )
    early_grad, _, _ = layer_backward(params, kept_values, local_rows.astype(jnp.float32))
    carried = lax.ppermute(early_grad.astype(jnp.bfloat16), "section", [(1, 0)])
    cotangent = jnp.where(is_first, carried, local_rows).astype(jnp.float32)
    backward, low_parts, small_sums = layer_backward(params, kept_values, cotangent)
    joined, first_low, pre_low, second_low = low_parts
    def weight_grad(rows, grads):
        return jnp.einsum(
            "ta,tb->ab", rows, grads, preferred_element_type=jnp.float32
        ).astype(jnp.bfloat16)

    parts = join_parts(
        weight_grad(kept_values[0], joined),
        weight_grad(kept_values[5], first_low),
        weight_grad(kept_values[8], pre_low),
        weight_grad(kept_values[10], second_low),
        small_sums,
    )
    total = reduce_parts(parts).astype(jnp.float32)
    ends_out = jnp.where(is_first, backward.astype(jnp.bfloat16), result)
    return tuple(member[None] for member in (ends_out, *split_total(total)))


def solution(mesh):
    in_specs = (
        P("section", ("fsdp", "replica"), None),
        P(("fsdp", "replica")),
        P("section", "fsdp", None),
        P("section", "fsdp", None),
        P("section", "fsdp", None),
        P("section", "fsdp", None),
        P("section", None, "fsdp"),
        P("section", None, "fsdp"),
        P("section", "fsdp"),
    )
    out_specs = (
        P("section", ("fsdp", "replica"), None),
        P("section", "fsdp", None),
        P("section", "fsdp", None),
        P("section", "fsdp", None),
        P("section", "fsdp", None),
        P("section", None, "fsdp"),
        P("section", None, "fsdp"),
        P("section", "fsdp"),
    )
    return jax.shard_map(body, mesh=mesh, in_specs=in_specs, out_specs=out_specs, check_vma=False)
```

```python
import jax
import jax.numpy as jnp
from jax import lax
from jax.experimental import pallas as pl
from jax.experimental.pallas import tpu as pltpu
from jax.sharding import PartitionSpec as P

HEADS = 16
HEAD_DIM = 64
SEQ = 64


MESH = pl.DeviceIdType.MESH
N_F = 8
TILE = 128
SMALL_ROWS = 16
PAYLOAD = 97 * TILE
VMEM_CAP = 60 * 1024 * 1024

GATHER_PLAN = ((128, 3072, 16), (128, 1024, 16), (128, 4096, 16), (512, 1024, 128), (16, 256, 0))


def place():
    f = lax.axis_index("fsdp")
    r = lax.axis_index("replica")
    return f // 2, lax.rem(f, 2), r // 2, lax.rem(r, 2)


def device(y, c, x, z):
    return {"fsdp": y * 2 + c, "replica": x * 2 + z}


def step_on(index, distance):
    return lax.rem(index + distance + 4, 4)


def greet(peers):
    barrier = pltpu.get_barrier_semaphore()
    for peer in peers:
        pl.semaphore_signal(barrier, inc=1, device_id=peer, device_id_type=MESH)
    pl.semaphore_wait(barrier, len(peers))


class Copies:
    def __init__(self, send_sem, recv_sem):
        self.send_sem, self.recv_sem, self.started = send_sem, recv_sem, []

    def start(self, src, dst, peer):
        number = len(self.started)
        copy = pltpu.make_async_remote_copy(
            src_ref=src,
            dst_ref=dst,
            send_sem=self.send_sem.at[number],
            recv_sem=self.recv_sem.at[number],
            device_id=peer,
            device_id_type=MESH,
        )
        copy.start()
        self.started.append(copy)
        return copy

    def finish(self):
        for copy in self.started:
            copy.wait_send()


def gather_kernel(*refs):
    count = len(GATHER_PLAN)
    ins, outs = refs[:count], refs[count : 2 * count]
    send_sem, recv_sem, local_sem = refs[2 * count :]
    y, c, x, z = place()
    right_y, left_y = device(step_on(y, 1), c, x, z), device(step_on(y, -1), c, x, z)
    right_x, left_x = device(y, c, step_on(x, 1), z), device(y, c, step_on(x, -1), z)
    sibling = device(y, 1 - c, x, z)
    greet((right_y, left_y, right_x, left_x, sibling))
    copies = Copies(send_sem, recv_sem)

    def span(k, owner_y, first, rows, part=None):
        shard_rows, columns, _ = GATHER_PLAN[k]
        start = pl.multiple_of((owner_y * 2 + c) * shard_rows + first, 16)
        if part is None:
            return outs[k].at[pl.ds(start, rows), :]
        half = columns // 2
        return outs[k].at[pl.ds(start, rows), pl.ds(part * half, half)]

    def quarter(k, owner_x):
        return pl.multiple_of(owner_x * GATHER_PLAN[k][2], 16)

    relayed = [k for k in range(count) if GATHER_PLAN[k][2]]
    direct = [k for k in range(count) if GATHER_PLAN[k][0] > 4 * GATHER_PLAN[k][2]]
    first_right, first_left = {}, {}
    for kind, members in (("relay", relayed), ("direct", direct)):
        for k in members:
            shard_rows, _, piece = GATHER_PLAN[k]
            if kind == "relay":
                first, rows = quarter(k, x), piece
            else:
                first, rows = 4 * piece, shard_rows - 4 * piece
            src = ins[k].at[pl.ds(first, rows), :]
            first_right[kind, k] = copies.start(src, span(k, y, first, rows), right_y)
            first_left[kind, k] = copies.start(src, span(k, y, first, rows), left_y)
    own = []
    sibling_copies = []
    for k in range(count):
        shard_rows = GATHER_PLAN[k][0]
        own.append(pltpu.make_async_copy(ins[k], span(k, y, 0, shard_rows), local_sem.at[k]))
        own[-1].start()
        sibling_copies.append(copies.start(ins[k], span(k, y, 0, shard_rows), sibling))

    before, after, across = step_on(y, -1), step_on(y, 1), step_on(y, 2)
    second_right, second_left = {}, {}
    along_right, along_left = {}, {}
    for kind, members in (("relay", relayed), ("direct", direct)):
        for k in members:
            shard_rows, _, piece = GATHER_PLAN[k]
            if kind == "relay":
                first, rows = quarter(k, x), piece
            else:
                first, rows = 4 * piece, shard_rows - 4 * piece
            first_right[kind, k].wait_recv()
            block = span(k, before, first, rows, 0)
            second_right[kind, k] = copies.start(block, block, right_y)
            first_left[kind, k].wait_recv()
            block = span(k, after, first, rows, 1)
            second_left[kind, k] = copies.start(block, block, left_y)
            if kind == "relay":
                for n, owner in ((0, before), (1, after)):
                    block = span(k, owner, first, rows)
                    along_right[n, k] = copies.start(block, block, right_x)
                    along_left[n, k] = copies.start(block, block, left_x)
    for k in relayed:
        second_right["relay", k].wait_recv()
        second_left["relay", k].wait_recv()
        block = span(k, across, quarter(k, x), GATHER_PLAN[k][2])
        along_right[2, k] = copies.start(block, block, right_x)
        along_left[2, k] = copies.start(block, block, left_x)
    further = {}
    owners = (before, after, across)
    for n in range(3):
        for k in relayed:
            piece = GATHER_PLAN[k][2]
            along_right[n, k].wait_recv()
            block = span(k, owners[n], quarter(k, step_on(x, -1)), piece, 0)
            further[n, k, 0] = copies.start(block, block, right_x)
            along_left[n, k].wait_recv()
            block = span(k, owners[n], quarter(k, step_on(x, 1)), piece, 1)
            further[n, k, 1] = copies.start(block, block, left_x)
    for n in range(3):
        for k in range(count):
            shard_rows = GATHER_PLAN[k][0]
            if n == 2 and k in direct:
                second_right["direct", k].wait_recv()
                second_left["direct", k].wait_recv()
            if k in relayed:
                further[n, k, 0].wait_recv()
                further[n, k, 1].wait_recv()
            block = span(k, owners[n], 0, shard_rows)
            sibling_copies.append(copies.start(block, block, sibling))
    for copy in own:
        copy.wait()
    for copy in sibling_copies:
        copy.wait_recv()
    copies.finish()


def gather_weights(*shards):
    copies = 160
    return pl.pallas_call(
        gather_kernel,
        out_shape=[
            jax.ShapeDtypeStruct((N_F * rows, columns), jnp.bfloat16)
            for rows, columns, _ in GATHER_PLAN
        ],
        in_specs=[pl.BlockSpec(memory_space=pl.ANY)] * len(GATHER_PLAN),
        out_specs=[pl.BlockSpec(memory_space=pl.ANY)] * len(GATHER_PLAN),
        scratch_shapes=[
            pltpu.SemaphoreType.DMA((copies,)),
            pltpu.SemaphoreType.DMA((copies,)),
            pltpu.SemaphoreType.DMA((len(GATHER_PLAN),)),
        ],
        compiler_params=pltpu.CompilerParams(
            collective_id=0, has_side_effects=True, vmem_limit_bytes=4 * 1024 * 1024
        ),
        name="gather_weights",
    )(*shards)


REDUCE_PLAN = ((8, 8, "y"), (8, 8, "x"), (8, 8, "y"), (8, 8, "y"), (8, 8, "x"), (8, 9, "y"))


def stage_shape(plan, stage):
    part_a, part_b, leading = plan
    rows = {("y", 0): (1, 128), ("x", 0): (4, 32), ("y", 1): (1, 32), ("x", 1): (1, 32)}
    blocks, height = rows[leading, stage]
    return blocks, height, (part_a + part_b) * TILE


def add_into(target, rows, columns, sources, dest=None):
    blocks, first_block, height, first_row = rows
    first_column, width = columns

    def one(step, carry):
        block, row = step // (height // 16), lax.rem(step, height // 16) * 16
        here = (
            first_block + block,
            pl.ds(pl.multiple_of(first_row + row, 16), 16),
            pl.ds(first_column, width),
        )
        total = target[here].astype(jnp.float32)
        for ref, base, column in sources:
            total = total + ref[
                base + block, pl.ds(pl.multiple_of(row, 16), 16), pl.ds(column, width)
            ].astype(jnp.float32)
        if dest is None:
            target[here] = total.astype(jnp.bfloat16)
        else:
            dest[pl.ds(pl.multiple_of(row, 16), 16), pl.ds(first_column, width)] = total.astype(
                jnp.bfloat16
            )
        return carry

    lax.fori_loop(0, blocks * (height // 16), one, 0)


def reduce_kernel(parts, out, held, paired, final, crossed, *rest):
    stage_refs, (send_sem, recv_sem, local_sem) = rest[:-3], rest[-3:]
    y, c, x, z = place()
    ring = {
        "y": (y, device(step_on(y, 1), c, x, z), device(step_on(y, -1), c, x, z)),
        "x": (x, device(y, c, step_on(x, 1), z), device(y, c, step_on(x, -1), z)),
    }
    sibling = device(y, 1 - c, x, z)
    partner = device(y, c, x, 1 - z)
    greet((ring["y"][1], ring["y"][2], ring["x"][1], ring["x"][2], sibling, partner))
    copies = Copies(send_sem, recv_sem)
    own, from_sibling, from_here, offset = [], [], [], 0
    offsets = []
    for n, (part_a, part_b, _) in enumerate(REDUCE_PLAN):
        width = (part_a + part_b) * TILE
        columns = pl.ds(offset, width)
        from_sibling.append(
            copies.start(parts.at[:, 1 - c, :, columns], paired.at[:, :, columns], sibling)
        )
        local = pltpu.make_async_copy(
            parts.at[:, c, :, columns], held.at[:, :, columns], local_sem.at[n]
        )
        local.start()
        from_here.append(local)
        offsets.append(offset)
        offset += width

    def along(n, stage):
        part_a, part_b, leading = REDUCE_PLAN[n]
        wide_a, wide_b = part_a * TILE, part_b * TILE
        start_a, start_b = offsets[n], offsets[n] + wide_a
        axis = leading if stage == 0 else ("x" if leading == "y" else "y")
        index, right, left = ring[axis]
        blocks, height, _ = stage_shape(REDUCE_PLAN[n], stage)
        landing = stage_refs[2 * n + stage]

        def origin(at):
            if axis == "y":
                return at, (0 if stage == 0 else x * 32)
            return (0 if stage == 0 else y), at * 32

        def take(at, start, wide):
            block, row = origin(at)
            return held.at[
                pl.ds(block, blocks), pl.ds(pl.multiple_of(row, 16), height), pl.ds(start, wide)
            ]

        def land(slot, start, wide):
            return landing.at[pl.ds(slot * blocks, blocks), :, pl.ds(start - offsets[n], wide)]

        def add(at, start, wide, slots):
            block, row = origin(at)
            add_into(
                held,
                (blocks, block, height, row),
                (start, wide),
                [(landing, slot * blocks, start - offsets[n]) for slot in slots],
            )

        ahead, behind, across = step_on(index, 1), step_on(index, -1), step_on(index, 2)
        far_right = copies.start(take(across, start_a, wide_a), land(0, start_a, wide_a), right)
        far_left = copies.start(take(across, start_b, wide_b), land(0, start_b, wide_b), left)
        near = [
            copies.start(take(ahead, start_b, wide_b), land(1, start_b, wide_b), right),
            copies.start(take(behind, start_a, wide_a), land(2, start_a, wide_a), left),
        ]
        yield
        far_right.wait_recv()
        add(ahead, start_a, wide_a, (0,))
        near.append(copies.start(take(ahead, start_a, wide_a), land(1, start_a, wide_a), right))
        far_left.wait_recv()
        add(behind, start_b, wide_b, (0,))
        near.append(copies.start(take(behind, start_b, wide_b), land(2, start_b, wide_b), left))
        yield
        for copy in near:
            copy.wait_recv()
        add(index, start_a, wide_a + wide_b, (1, 2))

    def chunk(n):
        part_a, part_b, _ = REDUCE_PLAN[n]
        start, wide_a, wide = offsets[n], part_a * TILE, (part_a + part_b) * TILE
        columns = pl.ds(start, wide)
        from_here[n].wait()
        from_sibling[n].wait_recv()
        add_into(held, (4, 0, 128, 0), (start, wide), [(paired, 0, start)])
        yield from along(n, 0)
        yield from along(n, 1)
        rows = pl.ds(pl.multiple_of(x * 32, 16), 32)
        swap = copies.start(held.at[pl.ds(y, 1), rows, columns], crossed.at[:, :, columns], partner)
        yield
        swap.wait_recv()
        add_into(held, (1, y, 32, x * 32), (start, wide), [(crossed, 0, start)], dest=final)
        kept = pltpu.make_async_copy(
            final.at[:, columns], out.at[rows, columns], local_sem.at[len(REDUCE_PLAN) + n]
        )
        kept.start()
        own.append(kept)
        _, right, left = ring["x"]
        to_right = copies.start(final.at[:, columns], out.at[rows, columns], right)
        to_left = copies.start(final.at[:, columns], out.at[rows, columns], left)
        yield
        to_right.wait_recv()
        block = out.at[
            pl.ds(pl.multiple_of(step_on(x, -1) * 32, 16), 32), pl.ds(start, wide_a)
        ]
        last = [copies.start(block, block, right)]
        to_left.wait_recv()
        block = out.at[
            pl.ds(pl.multiple_of(step_on(x, 1) * 32, 16), 32), pl.ds(start + wide_a, wide - wide_a)
        ]
        last.append(copies.start(block, block, left))
        yield
        for copy in last:
            copy.wait_recv()

    waiting = [chunk(n) for n in range(len(REDUCE_PLAN))]
    running = []
    while waiting or running:
        if waiting:
            running.append(waiting.pop(0))
        for member in list(running):
            if next(member, "end") == "end":
                running.remove(member)
    for copy in own:
        copy.wait()
    copies.finish()


def reduce_parts(parts):
    chunks = len(REDUCE_PLAN)
    landing = []
    for plan in REDUCE_PLAN:
        for stage in (0, 1):
            blocks, height, width = stage_shape(plan, stage)
            landing.append(pltpu.VMEM((3 * blocks, height, width), jnp.bfloat16))
    return pl.pallas_call(
        reduce_kernel,
        out_shape=jax.ShapeDtypeStruct((128, PAYLOAD), jnp.bfloat16),
        in_specs=[pl.BlockSpec(memory_space=pl.ANY)],
        out_specs=pl.BlockSpec(memory_space=pl.ANY),
        scratch_shapes=[
            pltpu.VMEM((4, 128, PAYLOAD), jnp.bfloat16),
            pltpu.VMEM((4, 128, PAYLOAD), jnp.bfloat16),
            pltpu.VMEM((32, PAYLOAD), jnp.bfloat16),
            pltpu.VMEM((1, 32, PAYLOAD), jnp.bfloat16),
            *landing,
            pltpu.SemaphoreType.DMA((chunks * 18,)),
            pltpu.SemaphoreType.DMA((chunks * 18,)),
            pltpu.SemaphoreType.DMA((chunks * 2,)),
        ],
        compiler_params=pltpu.CompilerParams(
            collective_id=1, has_side_effects=True, vmem_limit_bytes=VMEM_CAP
        ),
        name="reduce_parts",
    )(parts)


EPSILON = 1e-05
ROWS = 256
WIDTH = 1024
FF_WIDTH = 4096
STRIP = 32
FF_STEP = 512


def dot(a, b):
    return jnp.dot(a, b, preferred_element_type=jnp.float32)


def dot_last(a, b):
    return lax.dot_general(a, b, (((1,), (1,)), ((), ())), preferred_element_type=jnp.float32)


def dot_first(a, b):
    return lax.dot_general(a, b, (((0,), (0,)), ((), ())), preferred_element_type=jnp.float32)


def row_mean(rows):
    return jnp.mean(rows, axis=-1, keepdims=True)


def norm_forward(summed):
    center = summed - row_mean(summed)
    inverse = lax.rsqrt(row_mean(center * center) + EPSILON)
    return center * inverse, inverse


def norm_backward(grad_rows, normed, inverse, gain_row):
    scaled = grad_rows * gain_row
    return inverse * (scaled - row_mean(scaled) - normed * row_mean(scaled * normed))


def strips(body):
    def one(n, carry):
        body(pl.ds(pl.multiple_of(n * STRIP, STRIP), STRIP))
        return carry

    lax.fori_loop(0, ROWS // STRIP, one, 0)


def layer_kernel(
    ends,
    id_column,
    id_row,
    w_qkv_far,
    w_out_far,
    w_in_far,
    w_down_far,
    small,
    ends_out,
    parts,
    w_qkv,
    w_out,
    w_in,
    w_down,
    vec,
    sums,
    rows_in,
    cotangent,
    leaving,
    qkv,
    context,
    first_normed,
    first_inverse,
    normed_out,
    normed_low,
    activated,
    slope,
    second_normed,
    second_inverse,
    chances,
    second_low,
    pre_low,
    first_low,
    joined,
    total,
    tiles,
    small_rows,
    small_tile,
    load_sem,
    store_sem,
    send_sem,
    recv_sem,
):
    section = lax.axis_index("section")
    loads = [
        pltpu.make_async_copy(far, near, load_sem.at[n])
        for n, (far, near) in enumerate(
            ((w_qkv_far, w_qkv), (w_out_far, w_out), (w_in_far, w_in), (w_down_far, w_down))
        )
    ]
    for load in loads:
        load.start()
    other = {"section": 1 - section}
    greet((other,))
    onward = pltpu.make_async_remote_copy(
        src_ref=leaving, dst_ref=rows_in, send_sem=send_sem.at[0], recv_sem=recv_sem.at[0],
        device_id=other, device_id_type=MESH,
    )
    back = pltpu.make_async_remote_copy(
        src_ref=leaving, dst_ref=cotangent, send_sem=send_sem.at[1], recv_sem=recv_sem.at[1],
        device_id=other, device_id_type=MESH,
    )
    for f in range(N_F):
        shard = small[f * SMALL_ROWS : (f + 1) * SMALL_ROWS, :TILE].astype(jnp.float32)
        vec[0:8, f * TILE : (f + 1) * TILE] = shard[0:8]
        for i in range(4):
            first = (f % 2) * 512 + i * TILE
            vec[8 + f // 2 : 9 + f // 2, first : first + TILE] = shard[8 + i : 9 + i]
    sums[...] = jnp.zeros_like(sums)
    lane = lax.broadcasted_iota(jnp.int32, (1, TILE), 1)
    head_masks = [
        jnp.where((lane < HEAD_DIM) == (h == 0), 1.0, 0.0).astype(jnp.bfloat16) for h in (0, 1)
    ]

    @pl.when(section == 0)
    def _():
        rows_in[...] = ends[...]

    @pl.when(section == 1)
    def _():
        cotangent[...] = ends[...]
        onward.wait_recv()

    loads[0].wait()
    for j in range(6):
        columns = slice(j * 512, (j + 1) * 512)
        projected = dot(rows_in[...], w_qkv[:, columns])
        if j // 2 != 1:
            row = 0 if j < 2 else 1
            first = (j % 2) * 512
            projected = projected + vec[row : row + 1, first : first + 512]
        qkv[:, columns] = projected.astype(jnp.bfloat16)

    def head_columns(p, part):
        return pl.ds(pl.multiple_of(part * WIDTH + p * TILE, TILE), TILE)

    def attend(p, carry):
        for b in (0, 1):
            rows = slice(b * TILE, (b + 1) * TILE)
            query = qkv[rows, head_columns(p, 0)]
            key = qkv[rows, head_columns(p, 1)]
            value = qkv[rows, head_columns(p, 2)]
            same = id_column[rows, :] == id_row[:, rows]
            mixed = None
            for h in (0, 1):
                scores = dot_last(query * head_masks[h], key) * HEAD_DIM ** (-0.5)
                scores = jnp.where(same, scores, -1e30)
                exponent = jnp.exp(scores - jnp.max(scores, axis=-1, keepdims=True))
                share = exponent / jnp.sum(exponent, axis=-1, keepdims=True)
                low = share.astype(jnp.bfloat16)
                chances[p * 4 + b * 2 + h] = low
                part = dot(low, value * head_masks[h])
                mixed = part if mixed is None else mixed + part
            context[rows, head_columns(p, 0)] = mixed.astype(jnp.bfloat16)
        return carry

    lax.fori_loop(0, HEADS // 2, attend, 0)
    loads[1].wait()
    total[...] = dot(context[...], w_out[...])

    def first_norm(rows):
        summed = rows_in[rows, :].astype(jnp.float32) + total[rows, :] + vec[2:3, :]
        normed, inverse = norm_forward(summed)
        first_normed[rows, :] = normed
        first_inverse[rows, :] = jnp.broadcast_to(inverse, (STRIP, TILE))
        shifted = normed * vec[6:7, :] + vec[3:4, :]
        normed_out[rows, :] = shifted
        normed_low[rows, :] = shifted.astype(jnp.bfloat16)

    strips(first_norm)
    loads[2].wait()
    loads[3].wait()

    def widen(j):
        columns = slice(j * FF_STEP, (j + 1) * FF_STEP)
        row, first = j * FF_STEP // WIDTH, j * FF_STEP % WIDTH
        pre_act = dot(normed_low[...], w_in[:, columns])
        pre_act = pre_act + vec[8 + row : 9 + row, first : first + FF_STEP]
        phi = 0.5 * (1.0 + lax.erf(pre_act * 0.7071067811865476))
        activated[:, columns] = (pre_act * phi).astype(jnp.bfloat16)
        density = jnp.exp(-0.5 * pre_act * pre_act) * 0.3989422804014327
        slope[:, columns] = (phi + pre_act * density).astype(jnp.bfloat16)

    for j in range(FF_WIDTH // FF_STEP):
        widen(j)
    for n in range(2):
        columns = slice(n * 512, (n + 1) * 512)
        total[:, columns] = dot(activated[...], w_down[:, columns])

    def second_norm(rows):
        summed = normed_out[rows, :] + total[rows, :] + vec[4:5, :]
        normed, inverse = norm_forward(summed)
        second_normed[rows, :] = normed
        second_inverse[rows, :] = jnp.broadcast_to(inverse, (STRIP, TILE))
        leaving[rows, :] = (normed * vec[7:8, :] + vec[5:6, :]).astype(jnp.bfloat16)

    strips(second_norm)

    @pl.when(section == 0)
    def _():
        onward.start()
        onward.wait_send()
        back.wait_recv()

    @pl.when(section == 1)
    def _():
        ends_out[...] = leaving[...]

    def add_sum(row, values):
        sums[row : row + 1, :] += jnp.sum(values, axis=0, keepdims=True)

    def second_back(rows):
        grad = cotangent[rows, :].astype(jnp.float32)
        normed = second_normed[rows, :]
        add_sum(5, grad)
        add_sum(7, grad * normed)
        grad = norm_backward(grad, normed, second_inverse[rows, 0:1], vec[7:8, :])
        add_sum(4, grad)
        normed_out[rows, :] = grad
        second_low[rows, :] = grad.astype(jnp.bfloat16)

    strips(second_back)
    for j in range(FF_WIDTH // FF_STEP):
        columns = slice(j * FF_STEP, (j + 1) * FF_STEP)
        row, first = j * FF_STEP // WIDTH, j * FF_STEP % WIDTH
        grad = dot_last(second_low[...], w_down[columns, :]) * slope[:, columns].astype(jnp.float32)
        sums[8 + row : 9 + row, first : first + FF_STEP] = jnp.sum(grad, axis=0, keepdims=True)
        pre_low[:, columns] = grad.astype(jnp.bfloat16)
    for n in range(2):
        columns = slice(n * 512, (n + 1) * 512)
        total[:, columns] = dot_last(pre_low[...], w_in[columns, :])

    def first_back(rows):
        grad = normed_out[rows, :] + total[rows, :]
        normed = first_normed[rows, :]
        add_sum(3, grad)
        add_sum(6, grad * normed)
        grad = norm_backward(grad, normed, first_inverse[rows, 0:1], vec[6:7, :])
        add_sum(2, grad)
        normed_out[rows, :] = grad
        first_low[rows, :] = grad.astype(jnp.bfloat16)

    strips(first_back)
    context_grad = leaving
    for n in range(2):
        columns = slice(n * 512, (n + 1) * 512)
        context_grad[:, columns] = dot_last(first_low[...], w_out[columns, :]).astype(jnp.bfloat16)

    def attend_back(p, carry):
        for b in (0, 1):
            rows = slice(b * TILE, (b + 1) * TILE)
            query = qkv[rows, head_columns(p, 0)]
            key = qkv[rows, head_columns(p, 1)]
            value = qkv[rows, head_columns(p, 2)]
            grads = context_grad[rows, head_columns(p, 0)]
            results = [0.0, 0.0, 0.0]
            for h in (0, 1):
                own = grads * head_masks[h]
                low = chances[p * 4 + b * 2 + h]
                share = low.astype(jnp.float32)
                weight_grad = dot_last(own, value)
                inner = jnp.sum(share * weight_grad, axis=-1, keepdims=True)
                score = (share * (weight_grad - inner) * HEAD_DIM ** (-0.5)).astype(jnp.bfloat16)
                results[0] += dot(score, key * head_masks[h])
                results[1] += dot_first(score, query * head_masks[h])
                results[2] += dot_first(low, own)
            for part in range(3):
                joined[rows, head_columns(p, part)] = results[part].astype(jnp.bfloat16)
            for row, part in ((0, 0), (1, 2)):
                here = head_columns(p, 0)
                sums[row : row + 1, here] += jnp.sum(results[part], axis=0, keepdims=True)
        return carry

    lax.fori_loop(0, HEADS // 2, attend_back, 0)
    for n in range(2):
        columns = slice(n * 512, (n + 1) * 512)
        grad = normed_out[:, columns] + dot_last(joined[...], w_qkv[columns, :])
        leaving[:, columns] = grad.astype(jnp.bfloat16)

    @pl.when(section == 1)
    def _():
        back.start()

    @pl.when(section == 0)
    def _():
        ends_out[...] = leaving[...]

    for f in range(N_F):
        small_rows[f, 0:8, :] = sums[0:8, f * TILE : (f + 1) * TILE]
        for i in range(4):
            first = (f % 2) * 512 + i * TILE
            small_rows[f, 8 + i : 9 + i, :] = sums[8 + f // 2 : 9 + f // 2, first : first + TILE]
        small_rows[f, 12:16, :] = jnp.zeros((4, TILE), jnp.float32)
    small_tile[...] = jnp.zeros_like(small_tile)
    for f in range(N_F):
        small_tile[f // 2, f % 2, 0:16, :] = small_rows[f].astype(jnp.bfloat16)
    small_copy = pltpu.make_async_copy(
        small_tile, parts.at[:, :, :, 12 * WIDTH : 12 * WIDTH + TILE], store_sem.at[12]
    )
    small_copy.start()

    def store(slot, y):
        return pltpu.make_async_copy(
            tiles.at[slot],
            parts.at[y, :, :, slot * WIDTH : (slot + 1) * WIDTH],
            store_sem.at[slot],
        )

    def weight_grads(y, carry):
        block = pl.ds(pl.multiple_of(y * 256, 256), 256)

        @pl.when(y > 0)
        def _():
            for slot in range(12):
                store(slot, y - 1).wait()

        for slot in range(8):
            if slot < 3:
                left, right, column = rows_in, joined, slot
            elif slot == 3:
                left, right, column = context, first_low, 0
            else:
                left, right, column = normed_low, pre_low, slot - 4
            tile = dot_first(left[:, block], right[:, column * WIDTH : (column + 1) * WIDTH])
            tiles[slot] = tile.astype(jnp.bfloat16).reshape(2, TILE, WIDTH)
            store(slot, y).start()
        for core in (0, 1):
            for pair in (0, 1):
                first = pl.multiple_of(y * WIDTH + core * 512 + pair * 256, 256)
                tile = dot_first(activated[:, pl.ds(first, 256)], second_low[...])
                low = tile.astype(jnp.bfloat16)
                tiles[8 + 2 * pair, core] = low[:TILE]
                tiles[9 + 2 * pair, core] = low[TILE:]
        for slot in range(8, 12):
            store(slot, y).start()
        return carry

    lax.fori_loop(0, 4, weight_grads, 0)
    for slot in range(12):
        store(slot, 3).wait()
    small_copy.wait()

    @pl.when(section == 1)
    def _():
        back.wait_send()


def run_layer(ends, ids, weights, small):
    low, full = jnp.bfloat16, jnp.float32
    scratch = [
        ((1024, 3072), low),
        ((1024, 1024), low),
        ((1024, 4096), low),
        ((4096, 1024), low),
        ((16, WIDTH), full),
        ((16, WIDTH), full),
        ((ROWS, WIDTH), low),
        ((ROWS, WIDTH), low),
        ((ROWS, WIDTH), low),
        ((ROWS, 3 * WIDTH), low),
        ((ROWS, WIDTH), low),
        ((ROWS, WIDTH), full),
        ((ROWS, TILE), full),
        ((ROWS, WIDTH), full),
        ((ROWS, WIDTH), low),
        ((ROWS, FF_WIDTH), low),
        ((ROWS, FF_WIDTH), low),
        ((ROWS, WIDTH), full),
        ((ROWS, TILE), full),
        ((2 * HEADS, TILE, TILE), low),
        ((ROWS, WIDTH), low),
        ((ROWS, FF_WIDTH), low),
        ((ROWS, WIDTH), low),
        ((ROWS, 3 * WIDTH), low),
        ((ROWS, WIDTH), full),
        ((12, 2, TILE, WIDTH), low),
        ((N_F, SMALL_ROWS, TILE), full),
        ((4, 2, TILE, TILE), low),
    ]
    near = pl.BlockSpec(memory_space=pltpu.VMEM)
    far = pl.BlockSpec(memory_space=pl.ANY)
    return pl.pallas_call(
        layer_kernel,
        out_shape=[
            jax.ShapeDtypeStruct((ROWS, WIDTH), low),
            jax.ShapeDtypeStruct((4, 2, TILE, PAYLOAD), low),
        ],
        in_specs=[near, near, near, far, far, far, far, near],
        out_specs=[near, far],
        scratch_shapes=[
            *[pltpu.VMEM(shape, kind) for shape, kind in scratch],
            pltpu.SemaphoreType.DMA((4,)),
            pltpu.SemaphoreType.DMA((13,)),
            pltpu.SemaphoreType.DMA((2,)),
            pltpu.SemaphoreType.DMA((2,)),
        ],
        compiler_params=pltpu.CompilerParams(
            collective_id=2, has_side_effects=True, vmem_limit_bytes=VMEM_CAP
        ),
        name="run_layer",
    )(ends, ids[:, None], ids[None, :], *weights, small)


def pack_small(biases, gains, bias_in):
    rows = jnp.concatenate([biases, gains, bias_in.reshape(4, TILE)], axis=0)
    return jnp.pad(rows, ((0, 4), (0, TILE)))


def split_total(total):
    small = total[:, 12288:]
    return (
        total[:, :3072],
        total[:, 3072:4096],
        total[:, 4096:8192],
        jnp.swapaxes(total[:, 8192:12288].reshape(TILE, 4, 1024), 0, 1).reshape(512, 1024),
        small[:6],
        small[6:8],
        small[8:12].reshape(512),
    )


def body(ends_in, segment_ids, w_qkv, w_out, w_in, w_down, biases, gains, bias_in):
    gathered = gather_weights(
        w_qkv[0], w_out[0], w_in[0], w_down[0], pack_small(biases[0], gains[0], bias_in[0])
    )
    ids = segment_ids + (lax.iota(jnp.int32, ROWS) // SEQ) * 16
    ends_out, parts = run_layer(ends_in[0], ids, gathered[:4], gathered[4])
    total = reduce_parts(parts).astype(jnp.float32)
    return tuple(member[None] for member in (ends_out, *split_total(total)))


def solution(mesh):
    in_specs = (
        P("section", ("fsdp", "replica"), None),
        P(("fsdp", "replica")),
        P("section", "fsdp", None),
        P("section", "fsdp", None),
        P("section", "fsdp", None),
        P("section", "fsdp", None),
        P("section", None, "fsdp"),
        P("section", None, "fsdp"),
        P("section", "fsdp"),
    )
    out_specs = (
        P("section", ("fsdp", "replica"), None),
        P("section", "fsdp", None),
        P("section", "fsdp", None),
        P("section", "fsdp", None),
        P("section", "fsdp", None),
        P("section", None, "fsdp"),
        P("section", None, "fsdp"),
        P("section", "fsdp"),
    )
    return jax.shard_map(body, mesh=mesh, in_specs=in_specs, out_specs=out_specs, check_vma=False)
```

```python
import jax
import jax.numpy as jnp
from jax import lax
from jax.experimental import pallas as pl
from jax.experimental.pallas import tpu as pltpu
from jax.sharding import PartitionSpec as P

HEADS = 16
HEAD_DIM = 64
SEQ = 64
EPSILON = 1e-05
ROWS = 256
WIDTH = 1024
FF_WIDTH = 4096
STRIP = 32
FF_STEP = 512


def dot(a, b):
    return jnp.dot(a, b, preferred_element_type=jnp.float32)


def dot_last(a, b):
    return lax.dot_general(a, b, (((1,), (1,)), ((), ())), preferred_element_type=jnp.float32)


def dot_first(a, b):
    return lax.dot_general(a, b, (((0,), (0,)), ((), ())), preferred_element_type=jnp.float32)


MESH = pl.DeviceIdType.MESH
N_F = 8
TILE = 128
SMALL_ROWS = 16
GATHER_COPIES = 112
PAYLOAD = 97 * TILE
VMEM_CAP = 60 * 1024 * 1024

GATHER_PLAN = ((128, 3072, 16), (128, 1024, 16), (128, 4096, 16), (512, 1024, 128), (16, 256, 0))


def place():
    f = lax.axis_index("fsdp")
    r = lax.axis_index("replica")
    return f // 2, lax.rem(f, 2), r // 2, lax.rem(r, 2)


def device(y, c, x, z):
    return {"fsdp": y * 2 + c, "replica": x * 2 + z}


def step_on(index, distance):
    return lax.rem(index + distance + 4, 4)


def greet(peers):
    barrier = pltpu.get_barrier_semaphore()
    for peer in peers:
        pl.semaphore_signal(barrier, inc=1, device_id=peer, device_id_type=MESH)
    pl.semaphore_wait(barrier, len(peers))


class Copies:
    def __init__(self, send_sem, recv_sem):
        self.send_sem, self.recv_sem, self.count, self.unsent = send_sem, recv_sem, 0, []

    def start(self, src, dst, peer):
        copy = pltpu.make_async_remote_copy(
            src_ref=src,
            dst_ref=dst,
            send_sem=self.send_sem.at[self.count],
            recv_sem=self.recv_sem.at[self.count],
            device_id=peer,
            device_id_type=MESH,
        )
        copy.start()
        self.count += 1
        self.unsent.append(copy)
        return copy

    def sent(self, copy):
        copy.wait_send()
        self.unsent = [member for member in self.unsent if member is not copy]

    def finish(self):
        for copy in self.unsent:
            copy.wait_send()


def gather_into(ins, outs, copies, local_sem, others):
    count = len(GATHER_PLAN)
    y, c, x, z = place()
    right_y, left_y = device(step_on(y, 1), c, x, z), device(step_on(y, -1), c, x, z)
    right_x, left_x = device(y, c, step_on(x, 1), z), device(y, c, step_on(x, -1), z)
    sibling = device(y, 1 - c, x, z)
    own = []
    for k in range(count):
        start = pl.multiple_of((y * 2 + c) * GATHER_PLAN[k][0], 16)
        here = outs[k].at[pl.ds(start, GATHER_PLAN[k][0]), :]
        own.append(pltpu.make_async_copy(ins[k], here, local_sem.at[k]))
        own[-1].start()
    greet((right_y, left_y, right_x, left_x, sibling, *others))

    def span(k, owner_y, first, rows, part=None):
        shard_rows, columns, _ = GATHER_PLAN[k]
        start = pl.multiple_of((owner_y * 2 + c) * shard_rows + first, 16)
        if part is None:
            return outs[k].at[pl.ds(start, rows), :]
        half = columns // 2
        return outs[k].at[pl.ds(start, rows), pl.ds(part * half, half)]

    def quarter(k, owner_x):
        return pl.multiple_of(owner_x * GATHER_PLAN[k][2], 16)

    relayed = [k for k in range(count) if GATHER_PLAN[k][2]]
    direct = [k for k in range(count) if GATHER_PLAN[k][0] > 4 * GATHER_PLAN[k][2]]
    first_right, first_left, loaded = {}, {}, []
    for kind, members in (("relay", relayed), ("direct", direct)):
        for k in members:
            shard_rows, _, piece = GATHER_PLAN[k]
            if kind == "relay":
                first, rows = quarter(k, x), piece
            else:
                first, rows = 4 * piece, shard_rows - 4 * piece
            if k not in loaded:
                own[k].wait()
                loaded.append(k)
            src = span(k, y, first, rows)
            first_right[kind, k] = copies.start(src, src, right_y)
            first_left[kind, k] = copies.start(src, src, left_y)
    sibling_copies = {}
    for k in range(count):
        block = span(k, y, 0, GATHER_PLAN[k][0])
        sibling_copies[3, k] = copies.start(block, block, sibling)

    before, after, across = step_on(y, -1), step_on(y, 1), step_on(y, 2)
    second_right, second_left = {}, {}
    along_right, along_left = {}, {}
    for kind, members in (("relay", relayed), ("direct", direct)):
        for k in members:
            shard_rows, _, piece = GATHER_PLAN[k]
            if kind == "relay":
                first, rows = quarter(k, x), piece
            else:
                first, rows = 4 * piece, shard_rows - 4 * piece
            first_right[kind, k].wait_recv()
            block = span(k, before, first, rows, 0)
            second_right[kind, k] = copies.start(block, block, right_y)
            first_left[kind, k].wait_recv()
            block = span(k, after, first, rows, 1)
            second_left[kind, k] = copies.start(block, block, left_y)
            if kind == "relay":
                for n, owner in ((0, before), (1, after)):
                    block = span(k, owner, first, rows)
                    along_right[n, k] = copies.start(block, block, right_x)
                    along_left[n, k] = copies.start(block, block, left_x)
    for k in relayed:
        second_right["relay", k].wait_recv()
        second_left["relay", k].wait_recv()
        block = span(k, across, quarter(k, x), GATHER_PLAN[k][2])
        along_right[2, k] = copies.start(block, block, right_x)
        along_left[2, k] = copies.start(block, block, left_x)
    further = {}
    owners = (before, after, across)
    for n in range(3):
        for k in relayed:
            piece = GATHER_PLAN[k][2]
            along_right[n, k].wait_recv()
            block = span(k, owners[n], quarter(k, step_on(x, -1)), piece, 0)
            further[n, k, 0] = copies.start(block, block, right_x)
            along_left[n, k].wait_recv()
            block = span(k, owners[n], quarter(k, step_on(x, 1)), piece, 1)
            further[n, k, 1] = copies.start(block, block, left_x)
    for k in range(count):
        for n in range(3):
            if n == 2 and k in direct:
                second_right["direct", k].wait_recv()
                second_left["direct", k].wait_recv()
            if k in relayed:
                further[n, k, 0].wait_recv()
                further[n, k, 1].wait_recv()
            block = span(k, owners[n], 0, GATHER_PLAN[k][0])
            sibling_copies[n, k] = copies.start(block, block, sibling)

    def arrived(k):
        for n in range(4):
            sibling_copies[n, k].wait_recv()

    return arrived


REDUCE_PLAN = ((4, 2, "y"), (6, 2, "x"), (0, 2, "y"), (2, 2, "y"), (8, 2, "x"), (10, 2, "y"))
UNITS = 12


def chunk_width(plan):
    first, units, _ = plan
    return units * WIDTH + (TILE if first + units == UNITS else 0)


def stage_shape(plan, stage):
    shapes = {("y", 0): (1, 128), ("x", 0): (4, 32), ("y", 1): (1, 32), ("x", 1): (1, 32)}
    blocks, height = shapes[plan[2], stage]
    return blocks, height, chunk_width(plan)


def add_rows(blocks, height, reads, write):
    def one(step, carry):
        block = step // (height // 16)
        row = pl.multiple_of(lax.rem(step, height // 16) * 16, 16)
        total = reads[0](block, row).astype(jnp.float32)
        for read in reads[1:]:
            total = total + read(block, row).astype(jnp.float32)
        write(block, row, total.astype(jnp.bfloat16))
        return carry

    lax.fori_loop(0, blocks * (height // 16), one, 0)


def reduce_kernel(*refs):
    far, out = refs[:9], refs[9]
    near, (staged, held, crossed, gathered) = refs[10:19], refs[19:23]
    stage_refs, (load_sem, store_sem, send_sem, recv_sem) = refs[23:-4], refs[-4:]
    rows_in, context, normed_low, activated, joined, first_low, pre_low, second_low, small = near
    loads = [pltpu.make_async_copy(a, b, load_sem.at[n]) for n, (a, b) in enumerate(zip(far, near))]
    needs = {0: (0, 4), 3: (1, 5), 4: (2, 6), 8: (3, 7), 12: (8,)}
    sources = lambda unit: needs[max(key for key in needs if key <= unit)]
    pending = []
    for first, units, _ in REDUCE_PLAN:
        for unit in (first, first + units - 1):
            pending += [n for n in sources(unit) if n not in pending]
    pending.append(8)
    for n in pending:
        loads[n].start()
    y, c, x, z = place()
    ring = {
        "y": (y, device(step_on(y, 1), c, x, z), device(step_on(y, -1), c, x, z)),
        "x": (x, device(y, c, step_on(x, 1), z), device(y, c, step_on(x, -1), z)),
    }
    sibling = device(y, 1 - c, x, z)
    partner = device(y, c, x, 1 - z)
    greet((ring["y"][1], ring["y"][2], ring["x"][1], ring["x"][2], sibling, partner))
    copies = Copies(send_sem, recv_sem)
    to_sibling, stores = [], []

    def ready(numbers):
        for n in numbers:
            if n in pending:
                loads[n].wait()
                pending.remove(n)

    def produce(n):
        first, units, _ = REDUCE_PLAN[n]
        slot = n % 2
        for unit in range(first, first + units):
            ready(sources(unit))

        def block_rows(at, carry):
            for unit in range(first, min(first + units, 8)):
                if unit < 3:
                    left, right, column = rows_in, joined, unit
                elif unit == 3:
                    left, right, column = context, first_low, 0
                else:
                    left, right, column = normed_low, pre_low, unit - 4
                tile = dot_first(
                    left[:, pl.ds(pl.multiple_of(at * 256, 256), 256)],
                    right[:, column * WIDTH : (column + 1) * WIDTH],
                ).astype(jnp.bfloat16)
                place_at = slice((unit - first) * WIDTH, (unit - first + 1) * WIDTH)
                staged[slot, at, :, :, place_at] = tile.reshape(2, TILE, WIDTH)
            if first >= 8:
                for core in (0, 1):
                    start = at * WIDTH + core * 512 + (first - 8) * TILE
                    rows = activated[:, pl.ds(pl.multiple_of(start, TILE), units * TILE)]
                    tile = dot_first(rows, second_low[...]).astype(jnp.bfloat16)
                    for unit in range(units):
                        place_at = slice(unit * WIDTH, (unit + 1) * WIDTH)
                        staged[slot, at, core, :, place_at] = tile[unit * TILE : (unit + 1) * TILE]
            return carry

        lax.fori_loop(0, 4, block_rows, 0)
        if first + units == UNITS:
            ready((8,))
            for at in range(4):
                for core in (0, 1):
                    staged[slot, at, core, :, units * WIDTH : units * WIDTH + TILE] = small[at, core]

    def along(n, stage):
        first, _, leading = REDUCE_PLAN[n]
        offset, wide_a = first * WIDTH, REDUCE_PLAN[n][1] * WIDTH // 2
        wide_b = chunk_width(REDUCE_PLAN[n]) - wide_a
        start_a, start_b = offset, offset + wide_a
        axis = leading if stage == 0 else ("x" if leading == "y" else "y")
        index, right, left = ring[axis]
        blocks, height, _ = stage_shape(REDUCE_PLAN[n], stage)
        landing = stage_refs[2 * n + stage]

        def origin(at):
            if axis == "y":
                return at, (0 if stage == 0 else x * 32)
            return (0 if stage == 0 else y), at * 32

        def take(at, start, wide):
            block, row = origin(at)
            return held.at[
                pl.ds(block, blocks), pl.ds(pl.multiple_of(row, 16), height), pl.ds(start, wide)
            ]

        def land(slot, start, wide):
            return landing.at[pl.ds(slot * blocks, blocks), :, pl.ds(start - offset, wide)]

        def add(at, start, wide, slots):
            first_block, first_row = origin(at)

            def own(block, row):
                return first_block + block, pl.ds(
                    pl.multiple_of(first_row + row, 16), 16
                ), pl.ds(start, wide)

            def write(block, row, total):
                held[own(block, row)] = total

            def landed(slot):
                return lambda block, row: landing[
                    slot * blocks + block, pl.ds(row, 16), pl.ds(start - offset, wide)
                ]

            reads = [lambda block, row: held[own(block, row)], *[landed(slot) for slot in slots]]
            add_rows(blocks, height, reads, write)

        ahead, behind, across = step_on(index, 1), step_on(index, -1), step_on(index, 2)
        far_right = copies.start(take(across, start_a, wide_a), land(0, start_a, wide_a), right)
        far_left = copies.start(take(across, start_b, wide_b), land(0, start_b, wide_b), left)
        near_copies = [
            copies.start(take(ahead, start_b, wide_b), land(1, start_b, wide_b), right),
            copies.start(take(behind, start_a, wide_a), land(2, start_a, wide_a), left),
        ]
        yield
        far_right.wait_recv()
        add(ahead, start_a, wide_a, (0,))
        near_copies.append(
            copies.start(take(ahead, start_a, wide_a), land(1, start_a, wide_a), right)
        )
        far_left.wait_recv()
        add(behind, start_b, wide_b, (0,))
        near_copies.append(
            copies.start(take(behind, start_b, wide_b), land(2, start_b, wide_b), left)
        )
        yield
        for copy in near_copies:
            copy.wait_recv()
        add(index, start_a, wide_a + wide_b, (1, 2))

    def chunk(n):
        plan = REDUCE_PLAN[n]
        start, wide, slot = plan[0] * WIDTH, chunk_width(plan), n % 2
        wide_a = plan[1] * WIDTH // 2
        columns = pl.ds(start, wide)
        if n >= 2:
            copies.sent(to_sibling[n - 2])
        produce(n)
        to_sibling.append(
            copies.start(
                staged.at[slot, :, 1 - c, :, pl.ds(0, wide)], held.at[:, :, columns], sibling
            )
        )
        yield
        to_sibling[n].wait_recv()

        def write(block, row, total):
            held[block, pl.ds(row, 16), columns] = total

        add_rows(
            4,
            128,
            [
                lambda block, row: held[block, pl.ds(row, 16), columns],
                lambda block, row: staged[slot, block, c, pl.ds(row, 16), pl.ds(0, wide)],
            ],
            write,
        )
        yield from along(n, 0)
        yield from along(n, 1)

        def rows_of(at, first=start, width=wide):
            return gathered.at[pl.ds(pl.multiple_of(at * 32, 16), 32), pl.ds(first, width)]

        swap = copies.start(
            held.at[pl.ds(y, 1), pl.ds(pl.multiple_of(x * 32, 16), 32), columns],
            crossed.at[:, :, columns],
            partner,
        )
        yield
        swap.wait_recv()

        def finish(block, row, total):
            gathered[pl.ds(pl.multiple_of(x * 32 + row, 16), 16), columns] = total

        add_rows(
            1,
            32,
            [
                lambda block, row: held[y, pl.ds(pl.multiple_of(x * 32 + row, 16), 16), columns],
                lambda block, row: crossed[0, pl.ds(row, 16), columns],
            ],
            finish,
        )
        _, right, left = ring["x"]
        to_right = copies.start(rows_of(x), rows_of(x), right)
        to_left = copies.start(rows_of(x), rows_of(x), left)
        yield
        to_right.wait_recv()
        block = rows_of(step_on(x, -1), start, wide_a)
        last = [copies.start(block, block, right)]
        to_left.wait_recv()
        block = rows_of(step_on(x, 1), start + wide_a, wide - wide_a)
        last.append(copies.start(block, block, left))
        yield
        for copy in last:
            copy.wait_recv()
        stores.append(
            pltpu.make_async_copy(gathered.at[:, columns], out.at[:, columns], store_sem.at[n])
        )
        stores[-1].start()

    waiting = [chunk(n) for n in range(len(REDUCE_PLAN))]
    running = []
    while waiting or running:
        if waiting:
            running.append(waiting.pop(0))
        for member in list(running):
            if next(member, "end") == "end":
                running.remove(member)
    for copy in stores:
        copy.wait()
    copies.finish()


def reduce_grads(*operands):
    chunks = len(REDUCE_PLAN)
    widest = max(chunk_width(plan) for plan in REDUCE_PLAN)
    landing = []
    for plan in REDUCE_PLAN:
        for stage in (0, 1):
            blocks, height, width = stage_shape(plan, stage)
            landing.append(pltpu.VMEM((3 * blocks, height, width), jnp.bfloat16))
    far = pl.BlockSpec(memory_space=pl.ANY)
    return pl.pallas_call(
        reduce_kernel,
        out_shape=jax.ShapeDtypeStruct((TILE, PAYLOAD), jnp.bfloat16),
        in_specs=[far] * len(operands),
        out_specs=far,
        scratch_shapes=[
            *[pltpu.VMEM(operand.shape, operand.dtype) for operand in operands],
            pltpu.VMEM((2, 4, 2, TILE, widest), jnp.bfloat16),
            pltpu.VMEM((4, TILE, PAYLOAD), jnp.bfloat16),
            pltpu.VMEM((1, 32, PAYLOAD), jnp.bfloat16),
            pltpu.VMEM((TILE, PAYLOAD), jnp.bfloat16),
            *landing,
            pltpu.SemaphoreType.DMA((len(operands),)),
            pltpu.SemaphoreType.DMA((chunks,)),
            pltpu.SemaphoreType.DMA((chunks * 18,)),
            pltpu.SemaphoreType.DMA((chunks * 18,)),
        ],
        compiler_params=pltpu.CompilerParams(
            collective_id=1, has_side_effects=True, vmem_limit_bytes=VMEM_CAP
        ),
        name="reduce_grads",
    )(*operands)


def widen_kernel(low, qkv, out, into, down, bias, gain, hidden):
    total = low[...].astype(jnp.float32)
    qkv[...] = total[:, :3072]
    out[...] = total[:, 3072:4096]
    into[...] = total[:, 4096:8192]
    for j in range(4):
        down[j] = total[:, 8192 + j * WIDTH : 8192 + (j + 1) * WIDTH]

    @pl.when(pl.program_id(0) == 0)
    def _():
        bias[...] = total[0:6, 12288:]
        gain[...] = total[6:8, 12288:]
        hidden[...] = total[8:12, 12288:]


def widen_outputs(total):
    step = 32
    shapes = [(TILE, 3072), (TILE, WIDTH), (TILE, 4096), (4, TILE, WIDTH), (6, TILE), (2, TILE), (4, TILE)]
    specs = [pl.BlockSpec((step, shape[1]), lambda i: (i, 0)) for shape in shapes[:3]]
    specs.append(pl.BlockSpec((4, step, WIDTH), lambda i: (0, i, 0)))
    specs += [pl.BlockSpec(shape, lambda i: (0, 0)) for shape in shapes[4:]]
    outs = pl.pallas_call(
        widen_kernel,
        grid=(TILE // step,),
        out_shape=[jax.ShapeDtypeStruct(shape, jnp.float32) for shape in shapes],
        in_specs=[pl.BlockSpec((step, PAYLOAD), lambda i: (i, 0))],
        out_specs=specs,
        name="widen_outputs",
    )(total)
    return (*outs[:3], outs[3].reshape(512, WIDTH), outs[4], outs[5], outs[6].reshape(512))


def row_mean(rows):
    return jnp.mean(rows, axis=-1, keepdims=True)


def norm_forward(summed):
    center = summed - row_mean(summed)
    inverse = lax.rsqrt(row_mean(center * center) + EPSILON)
    return center * inverse, inverse


def norm_backward(grad_rows, normed, inverse, gain_row):
    scaled = grad_rows * gain_row
    return inverse * (scaled - row_mean(scaled) - normed * row_mean(scaled * normed))


def strips(body):
    def one(n, carry):
        body(pl.ds(pl.multiple_of(n * STRIP, STRIP), STRIP))
        return carry

    lax.fori_loop(0, ROWS // STRIP, one, 0)


def layer_kernel(
    ends,
    id_column,
    id_row,
    w_qkv_shard,
    w_out_shard,
    w_in_shard,
    w_down_shard,
    small_shard,
    ends_out,
    rows_in_far,
    context_far,
    normed_low_far,
    activated_far,
    joined_far,
    first_low_far,
    pre_low_far,
    second_low_far,
    small_far,
    w_qkv,
    w_out,
    w_in,
    w_down,
    small,
    vec,
    sums,
    rows_in,
    cotangent,
    leaving,
    qkv,
    context,
    first_normed,
    first_inverse,
    normed_out,
    normed_low,
    activated,
    slope,
    second_normed,
    second_inverse,
    chances,
    second_low,
    pre_low,
    first_low,
    joined,
    total,
    small_rows,
    small_tile,
    load_sem,
    store_sem,
    send_sem,
    recv_sem,
    gather_send_sem,
    gather_recv_sem,
):
    section = lax.axis_index("section")
    other = {"section": 1 - section}
    copies = Copies(gather_send_sem, gather_recv_sem)
    arrived = gather_into(
        (w_qkv_shard, w_out_shard, w_in_shard, w_down_shard, small_shard),
        (w_qkv, w_out, w_in, w_down, small),
        copies,
        load_sem,
        (other,),
    )
    stores = []

    def store(near, far):
        copy = pltpu.make_async_copy(near, far, store_sem.at[len(stores)])
        copy.start()
        stores.append(copy)

    onward = pltpu.make_async_remote_copy(
        src_ref=leaving, dst_ref=rows_in, send_sem=send_sem.at[0], recv_sem=recv_sem.at[0],
        device_id=other, device_id_type=MESH,
    )
    back = pltpu.make_async_remote_copy(
        src_ref=leaving, dst_ref=cotangent, send_sem=send_sem.at[1], recv_sem=recv_sem.at[1],
        device_id=other, device_id_type=MESH,
    )
    arrived(4)
    for f in range(N_F):
        shard = small[f * SMALL_ROWS : (f + 1) * SMALL_ROWS, :TILE].astype(jnp.float32)
        vec[0:8, f * TILE : (f + 1) * TILE] = shard[0:8]
        for i in range(4):
            first = (f % 2) * 512 + i * TILE
            vec[8 + f // 2 : 9 + f // 2, first : first + TILE] = shard[8 + i : 9 + i]
    sums[...] = jnp.zeros_like(sums)
    lane = lax.broadcasted_iota(jnp.int32, (1, TILE), 1)
    head_masks = [
        jnp.where((lane < HEAD_DIM) == (h == 0), 1.0, 0.0).astype(jnp.bfloat16) for h in (0, 1)
    ]

    @pl.when(section == 0)
    def _():
        rows_in[...] = ends[...]

    @pl.when(section == 1)
    def _():
        cotangent[...] = ends[...]
        onward.wait_recv()

    arrived(0)
    store(rows_in, rows_in_far)
    for j in range(6):
        columns = slice(j * 512, (j + 1) * 512)
        projected = dot(rows_in[...], w_qkv[:, columns])
        if j // 2 != 1:
            row = 0 if j < 2 else 1
            first = (j % 2) * 512
            projected = projected + vec[row : row + 1, first : first + 512]
        qkv[:, columns] = projected.astype(jnp.bfloat16)

    def head_columns(p, part):
        return pl.ds(pl.multiple_of(part * WIDTH + p * TILE, TILE), TILE)

    def attend(p, carry):
        for b in (0, 1):
            rows = slice(b * TILE, (b + 1) * TILE)
            query = qkv[rows, head_columns(p, 0)]
            key = qkv[rows, head_columns(p, 1)]
            value = qkv[rows, head_columns(p, 2)]
            same = id_column[rows, :] == id_row[:, rows]
            mixed = None
            for h in (0, 1):
                scores = dot_last(query * head_masks[h], key) * HEAD_DIM ** (-0.5)
                scores = jnp.where(same, scores, -1e30)
                exponent = jnp.exp(scores - jnp.max(scores, axis=-1, keepdims=True))
                share = exponent / jnp.sum(exponent, axis=-1, keepdims=True)
                low = share.astype(jnp.bfloat16)
                chances[p * 4 + b * 2 + h] = low
                part = dot(low, value * head_masks[h])
                mixed = part if mixed is None else mixed + part
            context[rows, head_columns(p, 0)] = mixed.astype(jnp.bfloat16)
        return carry

    lax.fori_loop(0, HEADS // 2, attend, 0)
    arrived(1)
    store(context, context_far)
    total[...] = dot(context[...], w_out[...])

    def first_norm(rows):
        summed = rows_in[rows, :].astype(jnp.float32) + total[rows, :] + vec[2:3, :]
        normed, inverse = norm_forward(summed)
        first_normed[rows, :] = normed
        first_inverse[rows, :] = jnp.broadcast_to(inverse, (STRIP, TILE))
        shifted = normed * vec[6:7, :] + vec[3:4, :]
        normed_out[rows, :] = shifted
        normed_low[rows, :] = shifted.astype(jnp.bfloat16)

    strips(first_norm)
    store(normed_low, normed_low_far)
    arrived(2)
    arrived(3)

    def widen(j):
        columns = slice(j * FF_STEP, (j + 1) * FF_STEP)
        row, first = j * FF_STEP // WIDTH, j * FF_STEP % WIDTH
        pre_act = dot(normed_low[...], w_in[:, columns])
        pre_act = pre_act + vec[8 + row : 9 + row, first : first + FF_STEP]
        phi = 0.5 * (1.0 + lax.erf(pre_act * 0.7071067811865476))
        activated[:, columns] = (pre_act * phi).astype(jnp.bfloat16)
        density = jnp.exp(-0.5 * pre_act * pre_act) * 0.3989422804014327
        slope[:, columns] = (phi + pre_act * density).astype(jnp.bfloat16)

    for j in range(FF_WIDTH // FF_STEP):
        widen(j)
    for n in range(2):
        columns = slice(n * 512, (n + 1) * 512)
        total[:, columns] = dot(activated[...], w_down[:, columns])

    store(activated, activated_far)

    def second_norm(rows):
        summed = normed_out[rows, :] + total[rows, :] + vec[4:5, :]
        normed, inverse = norm_forward(summed)
        second_normed[rows, :] = normed
        second_inverse[rows, :] = jnp.broadcast_to(inverse, (STRIP, TILE))
        leaving[rows, :] = (normed * vec[7:8, :] + vec[5:6, :]).astype(jnp.bfloat16)

    strips(second_norm)

    @pl.when(section == 0)
    def _():
        onward.start()
        onward.wait_send()
        back.wait_recv()

    @pl.when(section == 1)
    def _():
        ends_out[...] = leaving[...]

    def add_sum(row, values):
        sums[row : row + 1, :] += jnp.sum(values, axis=0, keepdims=True)

    def second_back(rows):
        grad = cotangent[rows, :].astype(jnp.float32)
        normed = second_normed[rows, :]
        add_sum(5, grad)
        add_sum(7, grad * normed)
        grad = norm_backward(grad, normed, second_inverse[rows, 0:1], vec[7:8, :])
        add_sum(4, grad)
        normed_out[rows, :] = grad
        second_low[rows, :] = grad.astype(jnp.bfloat16)

    strips(second_back)
    store(second_low, second_low_far)
    for j in range(FF_WIDTH // FF_STEP):
        columns = slice(j * FF_STEP, (j + 1) * FF_STEP)
        row, first = j * FF_STEP // WIDTH, j * FF_STEP % WIDTH
        grad = dot_last(second_low[...], w_down[columns, :]) * slope[:, columns].astype(jnp.float32)
        sums[8 + row : 9 + row, first : first + FF_STEP] = jnp.sum(grad, axis=0, keepdims=True)
        pre_low[:, columns] = grad.astype(jnp.bfloat16)
    for n in range(2):
        columns = slice(n * 512, (n + 1) * 512)
        total[:, columns] = dot_last(pre_low[...], w_in[columns, :])

    store(pre_low, pre_low_far)

    def first_back(rows):
        grad = normed_out[rows, :] + total[rows, :]
        normed = first_normed[rows, :]
        add_sum(3, grad)
        add_sum(6, grad * normed)
        grad = norm_backward(grad, normed, first_inverse[rows, 0:1], vec[6:7, :])
        add_sum(2, grad)
        normed_out[rows, :] = grad
        first_low[rows, :] = grad.astype(jnp.bfloat16)

    strips(first_back)
    store(first_low, first_low_far)
    context_grad = leaving
    for n in range(2):
        columns = slice(n * 512, (n + 1) * 512)
        context_grad[:, columns] = dot_last(first_low[...], w_out[columns, :]).astype(jnp.bfloat16)

    def attend_back(p, carry):
        for b in (0, 1):
            rows = slice(b * TILE, (b + 1) * TILE)
            query = qkv[rows, head_columns(p, 0)]
            key = qkv[rows, head_columns(p, 1)]
            value = qkv[rows, head_columns(p, 2)]
            grads = context_grad[rows, head_columns(p, 0)]
            results = [0.0, 0.0, 0.0]
            for h in (0, 1):
                own = grads * head_masks[h]
                low = chances[p * 4 + b * 2 + h]
                share = low.astype(jnp.float32)
                weight_grad = dot_last(own, value)
                inner = jnp.sum(share * weight_grad, axis=-1, keepdims=True)
                score = (share * (weight_grad - inner) * HEAD_DIM ** (-0.5)).astype(jnp.bfloat16)
                results[0] += dot(score, key * head_masks[h])
                results[1] += dot_first(score, query * head_masks[h])
                results[2] += dot_first(low, own)
            for part in range(3):
                joined[rows, head_columns(p, part)] = results[part].astype(jnp.bfloat16)
            for row, part in ((0, 0), (1, 2)):
                here = head_columns(p, 0)
                sums[row : row + 1, here] += jnp.sum(results[part], axis=0, keepdims=True)
        return carry

    lax.fori_loop(0, HEADS // 2, attend_back, 0)
    store(joined, joined_far)
    for n in range(2):
        columns = slice(n * 512, (n + 1) * 512)
        grad = normed_out[:, columns] + dot_last(joined[...], w_qkv[columns, :])
        leaving[:, columns] = grad.astype(jnp.bfloat16)

    @pl.when(section == 1)
    def _():
        back.start()

    @pl.when(section == 0)
    def _():
        ends_out[...] = leaving[...]

    for f in range(N_F):
        small_rows[f, 0:8, :] = sums[0:8, f * TILE : (f + 1) * TILE]
        for i in range(4):
            first = (f % 2) * 512 + i * TILE
            small_rows[f, 8 + i : 9 + i, :] = sums[8 + f // 2 : 9 + f // 2, first : first + TILE]
        small_rows[f, 12:16, :] = jnp.zeros((4, TILE), jnp.float32)
    small_tile[...] = jnp.zeros_like(small_tile)
    for f in range(N_F):
        small_tile[f // 2, f % 2, 0:16, :] = small_rows[f].astype(jnp.bfloat16)
    store(small_tile, small_far)
    for copy in stores:
        copy.wait()
    copies.finish()

    @pl.when(section == 1)
    def _():
        back.wait_send()


def run_layer(ends, ids, shards):
    low, full = jnp.bfloat16, jnp.float32
    scratch = [
        ((1024, 3072), low),
        ((1024, 1024), low),
        ((1024, 4096), low),
        ((4096, 1024), low),
        ((N_F * SMALL_ROWS, 2 * TILE), low),
        ((16, WIDTH), full),
        ((16, WIDTH), full),
        ((ROWS, WIDTH), low),
        ((ROWS, WIDTH), low),
        ((ROWS, WIDTH), low),
        ((ROWS, 3 * WIDTH), low),
        ((ROWS, WIDTH), low),
        ((ROWS, WIDTH), full),
        ((ROWS, TILE), full),
        ((ROWS, WIDTH), full),
        ((ROWS, WIDTH), low),
        ((ROWS, FF_WIDTH), low),
        ((ROWS, FF_WIDTH), low),
        ((ROWS, WIDTH), full),
        ((ROWS, TILE), full),
        ((2 * HEADS, TILE, TILE), low),
        ((ROWS, WIDTH), low),
        ((ROWS, FF_WIDTH), low),
        ((ROWS, WIDTH), low),
        ((ROWS, 3 * WIDTH), low),
        ((ROWS, WIDTH), full),
        ((N_F, SMALL_ROWS, TILE), full),
        ((4, 2, TILE, TILE), low),
    ]
    near = pl.BlockSpec(memory_space=pltpu.VMEM)
    far = pl.BlockSpec(memory_space=pl.ANY)
    return pl.pallas_call(
        layer_kernel,
        out_shape=[
            jax.ShapeDtypeStruct((ROWS, WIDTH), low),
            *[jax.ShapeDtypeStruct((ROWS, columns * WIDTH), low) for columns in (1, 1, 1, 4, 3, 1, 4, 1)],
            jax.ShapeDtypeStruct((4, 2, TILE, TILE), low),
        ],
        in_specs=[near, near, near, far, far, far, far, far],
        out_specs=[near, *[far] * 9],
        scratch_shapes=[
            *[pltpu.VMEM(shape, kind) for shape, kind in scratch],
            pltpu.SemaphoreType.DMA((5,)),
            pltpu.SemaphoreType.DMA((9,)),
            pltpu.SemaphoreType.DMA((2,)),
            pltpu.SemaphoreType.DMA((2,)),
            pltpu.SemaphoreType.DMA((GATHER_COPIES,)),
            pltpu.SemaphoreType.DMA((GATHER_COPIES,)),
        ],
        compiler_params=pltpu.CompilerParams(
            collective_id=2, has_side_effects=True, vmem_limit_bytes=VMEM_CAP
        ),
        name="run_layer",
    )(ends, ids[:, None], ids[None, :], *shards)


def pack_small(biases, gains, bias_in):
    rows = jnp.concatenate([biases, gains, bias_in.reshape(4, TILE)], axis=0)
    return jnp.pad(rows, ((0, 4), (0, TILE)))


def body(ends_in, segment_ids, w_qkv, w_out, w_in, w_down, biases, gains, bias_in):
    shards = (w_qkv[0], w_out[0], w_in[0], w_down[0], pack_small(biases[0], gains[0], bias_in[0]))
    ids = segment_ids + (lax.iota(jnp.int32, ROWS) // SEQ) * 16
    ends_out, *operands = run_layer(ends_in[0], ids, shards)
    outs = widen_outputs(reduce_grads(*operands))
    return tuple(member[None] for member in (ends_out, *outs))


def solution(mesh):
    in_specs = (
        P("section", ("fsdp", "replica"), None),
        P(("fsdp", "replica")),
        P("section", "fsdp", None),
        P("section", "fsdp", None),
        P("section", "fsdp", None),
        P("section", "fsdp", None),
        P("section", None, "fsdp"),
        P("section", None, "fsdp"),
        P("section", "fsdp"),
    )
    out_specs = (
        P("section", ("fsdp", "replica"), None),
        P("section", "fsdp", None),
        P("section", "fsdp", None),
        P("section", "fsdp", None),
        P("section", "fsdp", None),
        P("section", None, "fsdp"),
        P("section", None, "fsdp"),
        P("section", "fsdp"),
    )
    return jax.shard_map(body, mesh=mesh, in_specs=in_specs, out_specs=out_specs, check_vma=False)
```

```python
import jax
import jax.numpy as jnp
from jax import lax
from jax.experimental import pallas as pl
from jax.experimental.pallas import tpu as pltpu
from jax.sharding import PartitionSpec as P

HEADS = 16
HEAD_DIM = 64
SEQ = 64
EPSILON = 1e-05
ROWS = 256
WIDTH = 1024
FF_WIDTH = 4096
STRIP = 32
FF_STEP = 512


def dot(a, b):
    return jnp.dot(a, b, preferred_element_type=jnp.float32)


def dot_last(a, b):
    return lax.dot_general(a, b, (((1,), (1,)), ((), ())), preferred_element_type=jnp.float32)


def dot_first(a, b):
    return lax.dot_general(a, b, (((0,), (0,)), ((), ())), preferred_element_type=jnp.float32)


MESH = pl.DeviceIdType.MESH
N_F = 8
TILE = 128
SMALL_ROWS = 16
GATHER_COPIES = 112
PAYLOAD = 97 * TILE
VMEM_CAP = 60 * 1024 * 1024

GATHER_PLAN = ((128, 3072, 16), (128, 1024, 16), (128, 4096, 16), (512, 1024, 128), (16, 256, 0))


def place():
    f = lax.axis_index("fsdp")
    r = lax.axis_index("replica")
    return f // 2, lax.rem(f, 2), r // 2, lax.rem(r, 2)


def device(y, c, x, z):
    return {"fsdp": y * 2 + c, "replica": x * 2 + z}


def step_on(index, distance):
    return lax.rem(index + distance + 4, 4)


def greet(peers):
    barrier = pltpu.get_barrier_semaphore()
    for peer in peers:
        pl.semaphore_signal(barrier, inc=1, device_id=peer, device_id_type=MESH)
    pl.semaphore_wait(barrier, len(peers))


class Copies:
    def __init__(self, send_sem, recv_sem):
        self.send_sem, self.recv_sem, self.count, self.unsent = send_sem, recv_sem, 0, []

    def start(self, src, dst, peer):
        copy = pltpu.make_async_remote_copy(
            src_ref=src,
            dst_ref=dst,
            send_sem=self.send_sem.at[self.count],
            recv_sem=self.recv_sem.at[self.count],
            device_id=peer,
            device_id_type=MESH,
        )
        copy.start()
        self.count += 1
        self.unsent.append(copy)
        return copy

    def sent(self, copy):
        copy.wait_send()
        self.unsent = [member for member in self.unsent if member is not copy]

    def finish(self):
        for copy in self.unsent:
            copy.wait_send()


def gather_into(ins, outs, copies, local_sem, others):
    count = len(GATHER_PLAN)
    y, c, x, z = place()
    right_y, left_y = device(step_on(y, 1), c, x, z), device(step_on(y, -1), c, x, z)
    right_x, left_x = device(y, c, step_on(x, 1), z), device(y, c, step_on(x, -1), z)
    sibling = device(y, 1 - c, x, z)
    own = []
    for k in range(count):
        start = pl.multiple_of((y * 2 + c) * GATHER_PLAN[k][0], 16)
        here = outs[k].at[pl.ds(start, GATHER_PLAN[k][0]), :]
        own.append(pltpu.make_async_copy(ins[k], here, local_sem.at[k]))
        own[-1].start()
    greet((right_y, left_y, right_x, left_x, sibling, *others))

    def span(k, owner_y, first, rows, part=None):
        shard_rows, columns, _ = GATHER_PLAN[k]
        start = pl.multiple_of((owner_y * 2 + c) * shard_rows + first, 16)
        if part is None:
            return outs[k].at[pl.ds(start, rows), :]
        half = columns // 2
        return outs[k].at[pl.ds(start, rows), pl.ds(part * half, half)]

    def quarter(k, owner_x):
        return pl.multiple_of(owner_x * GATHER_PLAN[k][2], 16)

    relayed = [k for k in range(count) if GATHER_PLAN[k][2]]
    direct = [k for k in range(count) if GATHER_PLAN[k][0] > 4 * GATHER_PLAN[k][2]]
    first_right, first_left, second_right, second_left = {}, {}, {}, {}
    along_right, along_left, sibling_copies, further = {}, {}, {}, {}
    before, after, across = owners = (step_on(y, -1), step_on(y, 1), step_on(y, 2))

    def extent(kind, k):
        shard_rows, _, piece = GATHER_PLAN[k]
        return (quarter(k, x), piece) if kind == "relay" else (4 * piece, shard_rows - 4 * piece)

    def send_own(kind, k):
        block = span(k, y, *extent(kind, k))
        first_right[kind, k] = copies.start(block, block, right_y)
        first_left[kind, k] = copies.start(block, block, left_y)

    def send_on(kind, k):
        first_right[kind, k].wait_recv()
        block = span(k, before, *extent(kind, k), 0)
        second_right[kind, k] = copies.start(block, block, right_y)
        first_left[kind, k].wait_recv()
        block = span(k, after, *extent(kind, k), 1)
        second_left[kind, k] = copies.start(block, block, left_y)

    def send_along(n, k):
        block = span(k, owners[n], *extent("relay", k))
        along_right[n, k] = copies.start(block, block, right_x)
        along_left[n, k] = copies.start(block, block, left_x)

    def send_further(n, k):
        piece = GATHER_PLAN[k][2]
        along_right[n, k].wait_recv()
        block = span(k, owners[n], quarter(k, step_on(x, -1)), piece, 0)
        further[n, k, 0] = copies.start(block, block, right_x)
        along_left[n, k].wait_recv()
        block = span(k, owners[n], quarter(k, step_on(x, 1)), piece, 1)
        further[n, k, 1] = copies.start(block, block, left_x)

    for k in relayed:
        own[k].wait()
        send_own("relay", k)
    for k in range(count):
        if k not in relayed:
            own[k].wait()
        block = span(k, y, 0, GATHER_PLAN[k][0])
        sibling_copies[3, k] = copies.start(block, block, sibling)
    for k in relayed:
        send_on("relay", k)
        send_along(0, k)
        send_along(1, k)
    for k in direct[::-1]:
        send_own("direct", k)
    for k in relayed:
        second_right["relay", k].wait_recv()
        second_left["relay", k].wait_recv()
        send_along(2, k)
    for n in (0, 1):
        for k in relayed:
            send_further(n, k)
    for k in direct[::-1]:
        send_on("direct", k)
    for k in relayed:
        send_further(2, k)
    for k in range(count):
        for n in range(3):
            if n == 2 and k in direct:
                second_right["direct", k].wait_recv()
                second_left["direct", k].wait_recv()
            if k in relayed:
                further[n, k, 0].wait_recv()
                further[n, k, 1].wait_recv()
            block = span(k, owners[n], 0, GATHER_PLAN[k][0])
            sibling_copies[n, k] = copies.start(block, block, sibling)

    def arrived(k):
        for n in range(4):
            sibling_copies[n, k].wait_recv()

    return arrived


REDUCE_PLAN = tuple(
    (unit, 1, "yxy"[n % 3]) for n, unit in enumerate((4, 5, 6, 7, 0, 1, 2, 3, 8, 9, 10, 11))
)
UNITS = 12


def chunk_width(plan):
    first, units, _ = plan
    return units * WIDTH + (TILE if first + units == UNITS else 0)


def stage_shape(plan, stage):
    shapes = {("y", 0): (1, 128), ("x", 0): (4, 32), ("y", 1): (1, 32), ("x", 1): (1, 32)}
    blocks, height = shapes[plan[2], stage]
    return blocks, height, chunk_width(plan)


def add_rows(blocks, height, reads, write):
    def one(step, carry):
        block = step // (height // 16)
        row = pl.multiple_of(lax.rem(step, height // 16) * 16, 16)
        total = reads[0](block, row).astype(jnp.float32)
        for read in reads[1:]:
            total = total + read(block, row).astype(jnp.float32)
        write(block, row, total.astype(jnp.bfloat16))
        return carry

    lax.fori_loop(0, blocks * (height // 16), one, 0)


def reduce_kernel(*refs):
    far, out = refs[:9], refs[9]
    near, (staged, held, crossed, gathered) = refs[10:19], refs[19:23]
    stage_refs, (load_sem, store_sem, send_sem, recv_sem) = refs[23:-4], refs[-4:]
    rows_in, context, normed_low, activated, joined, first_low, pre_low, second_low, small = near
    loads = [pltpu.make_async_copy(a, b, load_sem.at[n]) for n, (a, b) in enumerate(zip(far, near))]
    needs = {0: (0, 4), 3: (1, 5), 4: (2, 6), 8: (3, 7), 12: (8,)}
    sources = lambda unit: needs[max(key for key in needs if key <= unit)]
    pending = []
    for first, units, _ in REDUCE_PLAN:
        for unit in (first, first + units - 1):
            pending += [n for n in sources(unit) if n not in pending]
    pending.append(8)
    for n in pending:
        loads[n].start()
    y, c, x, z = place()
    ring = {
        "y": (y, device(step_on(y, 1), c, x, z), device(step_on(y, -1), c, x, z)),
        "x": (x, device(y, c, step_on(x, 1), z), device(y, c, step_on(x, -1), z)),
    }
    sibling = device(y, 1 - c, x, z)
    partner = device(y, c, x, 1 - z)
    greet((ring["y"][1], ring["y"][2], ring["x"][1], ring["x"][2], sibling, partner))
    copies = Copies(send_sem, recv_sem)
    to_sibling, stores = [], []

    def ready(numbers):
        for n in numbers:
            if n in pending:
                loads[n].wait()
                pending.remove(n)

    def produce(n):
        first, units, _ = REDUCE_PLAN[n]
        slot = n % 2
        for unit in range(first, first + units):
            ready(sources(unit))

        def block_rows(at, carry):
            for unit in range(first, min(first + units, 8)):
                if unit < 3:
                    left, right, column = rows_in, joined, unit
                elif unit == 3:
                    left, right, column = context, first_low, 0
                else:
                    left, right, column = normed_low, pre_low, unit - 4
                tile = dot_first(
                    left[:, pl.ds(pl.multiple_of(at * 256, 256), 256)],
                    right[:, column * WIDTH : (column + 1) * WIDTH],
                ).astype(jnp.bfloat16)
                place_at = slice((unit - first) * WIDTH, (unit - first + 1) * WIDTH)
                staged[slot, at, :, :, place_at] = tile.reshape(2, TILE, WIDTH)
            if first >= 8:
                for core in (0, 1):
                    start = at * WIDTH + core * 512 + (first - 8) * TILE
                    rows = activated[:, pl.ds(pl.multiple_of(start, TILE), units * TILE)]
                    tile = dot_first(rows, second_low[...]).astype(jnp.bfloat16)
                    for unit in range(units):
                        place_at = slice(unit * WIDTH, (unit + 1) * WIDTH)
                        staged[slot, at, core, :, place_at] = tile[unit * TILE : (unit + 1) * TILE]
            return carry

        lax.fori_loop(0, 4, block_rows, 0)
        if first + units == UNITS:
            ready((8,))
            for at in range(4):
                for core in (0, 1):
                    staged[slot, at, core, :, units * WIDTH : units * WIDTH + TILE] = small[at, core]

    def along(n, stage):
        first, _, leading = REDUCE_PLAN[n]
        offset, wide_a = first * WIDTH, REDUCE_PLAN[n][1] * WIDTH // 2
        wide_b = chunk_width(REDUCE_PLAN[n]) - wide_a
        start_a, start_b = offset, offset + wide_a
        axis = leading if stage == 0 else ("x" if leading == "y" else "y")
        index, right, left = ring[axis]
        blocks, height, _ = stage_shape(REDUCE_PLAN[n], stage)
        landing = stage_refs[2 * n + stage]

        def origin(at):
            if axis == "y":
                return at, (0 if stage == 0 else x * 32)
            return (0 if stage == 0 else y), at * 32

        def take(at, start, wide):
            block, row = origin(at)
            return held.at[
                pl.ds(block, blocks), pl.ds(pl.multiple_of(row, 16), height), pl.ds(start, wide)
            ]

        def land(slot, start, wide):
            return landing.at[pl.ds(slot * blocks, blocks), :, pl.ds(start - offset, wide)]

        def add(at, start, wide, slots):
            first_block, first_row = origin(at)

            def own(block, row):
                return first_block + block, pl.ds(
                    pl.multiple_of(first_row + row, 16), 16
                ), pl.ds(start, wide)

            def write(block, row, total):
                held[own(block, row)] = total

            def landed(slot):
                return lambda block, row: landing[
                    slot * blocks + block, pl.ds(row, 16), pl.ds(start - offset, wide)
                ]

            reads = [lambda block, row: held[own(block, row)], *[landed(slot) for slot in slots]]
            add_rows(blocks, height, reads, write)

        ahead, behind, across = step_on(index, 1), step_on(index, -1), step_on(index, 2)
        far_right = copies.start(take(across, start_a, wide_a), land(0, start_a, wide_a), right)
        far_left = copies.start(take(across, start_b, wide_b), land(0, start_b, wide_b), left)
        near_copies = [
            copies.start(take(ahead, start_b, wide_b), land(1, start_b, wide_b), right),
            copies.start(take(behind, start_a, wide_a), land(2, start_a, wide_a), left),
        ]
        yield
        far_right.wait_recv()
        add(ahead, start_a, wide_a, (0,))
        near_copies.append(
            copies.start(take(ahead, start_a, wide_a), land(1, start_a, wide_a), right)
        )
        far_left.wait_recv()
        add(behind, start_b, wide_b, (0,))
        near_copies.append(
            copies.start(take(behind, start_b, wide_b), land(2, start_b, wide_b), left)
        )
        yield
        for copy in near_copies:
            copy.wait_recv()
        add(index, start_a, wide_a + wide_b, (1, 2))

    def chunk(n):
        plan = REDUCE_PLAN[n]
        start, wide, slot = plan[0] * WIDTH, chunk_width(plan), n % 2
        wide_a = plan[1] * WIDTH // 2
        columns = pl.ds(start, wide)
        if n >= 2:
            copies.sent(to_sibling[n - 2])
        produce(n)
        to_sibling.append(
            copies.start(
                staged.at[slot, :, 1 - c, :, pl.ds(0, wide)], held.at[:, :, columns], sibling
            )
        )
        yield
        to_sibling[n].wait_recv()

        def write(block, row, total):
            held[block, pl.ds(row, 16), columns] = total

        add_rows(
            4,
            128,
            [
                lambda block, row: held[block, pl.ds(row, 16), columns],
                lambda block, row: staged[slot, block, c, pl.ds(row, 16), pl.ds(0, wide)],
            ],
            write,
        )
        yield from along(n, 0)
        yield from along(n, 1)

        def rows_of(at, first=start, width=wide):
            return gathered.at[pl.ds(pl.multiple_of(at * 32, 16), 32), pl.ds(first, width)]

        swap = copies.start(
            held.at[pl.ds(y, 1), pl.ds(pl.multiple_of(x * 32, 16), 32), columns],
            crossed.at[:, :, columns],
            partner,
        )
        yield
        swap.wait_recv()

        def finish(block, row, total):
            gathered[pl.ds(pl.multiple_of(x * 32 + row, 16), 16), columns] = total

        add_rows(
            1,
            32,
            [
                lambda block, row: held[y, pl.ds(pl.multiple_of(x * 32 + row, 16), 16), columns],
                lambda block, row: crossed[0, pl.ds(row, 16), columns],
            ],
            finish,
        )
        _, right, left = ring["x"]
        to_right = copies.start(rows_of(x), rows_of(x), right)
        to_left = copies.start(rows_of(x), rows_of(x), left)
        yield
        to_right.wait_recv()
        block = rows_of(step_on(x, -1), start, wide_a)
        last = [copies.start(block, block, right)]
        to_left.wait_recv()
        block = rows_of(step_on(x, 1), start + wide_a, wide - wide_a)
        last.append(copies.start(block, block, left))
        yield
        for copy in last:
            copy.wait_recv()
        stores.append(
            pltpu.make_async_copy(gathered.at[:, columns], out.at[:, columns], store_sem.at[n])
        )
        stores[-1].start()

    waiting = [chunk(n) for n in range(len(REDUCE_PLAN))]
    running = []
    while waiting or running:
        if waiting:
            running.append(waiting.pop(0))
        for member in running[::-1]:
            if next(member, "end") == "end":
                running.remove(member)
    for copy in stores:
        copy.wait()
    copies.finish()


def reduce_grads(*operands):
    chunks = len(REDUCE_PLAN)
    widest = max(chunk_width(plan) for plan in REDUCE_PLAN)
    landing = []
    for plan in REDUCE_PLAN:
        for stage in (0, 1):
            blocks, height, width = stage_shape(plan, stage)
            landing.append(pltpu.VMEM((3 * blocks, height, width), jnp.bfloat16))
    far = pl.BlockSpec(memory_space=pl.ANY)
    return pl.pallas_call(
        reduce_kernel,
        out_shape=jax.ShapeDtypeStruct((TILE, PAYLOAD), jnp.bfloat16),
        in_specs=[far] * len(operands),
        out_specs=far,
        scratch_shapes=[
            *[pltpu.VMEM(operand.shape, operand.dtype) for operand in operands],
            pltpu.VMEM((2, 4, 2, TILE, widest), jnp.bfloat16),
            pltpu.VMEM((4, TILE, PAYLOAD), jnp.bfloat16),
            pltpu.VMEM((1, 32, PAYLOAD), jnp.bfloat16),
            pltpu.VMEM((TILE, PAYLOAD), jnp.bfloat16),
            *landing,
            pltpu.SemaphoreType.DMA((len(operands),)),
            pltpu.SemaphoreType.DMA((chunks,)),
            pltpu.SemaphoreType.DMA((chunks * 18,)),
            pltpu.SemaphoreType.DMA((chunks * 18,)),
        ],
        compiler_params=pltpu.CompilerParams(
            collective_id=1, has_side_effects=True, vmem_limit_bytes=VMEM_CAP
        ),
        name="reduce_grads",
    )(*operands)


def widen_kernel(low, qkv, out, into, down, bias, gain, hidden):
    total = low[...].astype(jnp.float32)
    qkv[...] = total[:, :3072]
    out[...] = total[:, 3072:4096]
    into[...] = total[:, 4096:8192]
    for j in range(4):
        down[j] = total[:, 8192 + j * WIDTH : 8192 + (j + 1) * WIDTH]

    @pl.when(pl.program_id(0) == 0)
    def _():
        bias[...] = total[0:6, 12288:]
        gain[...] = total[6:8, 12288:]
        hidden[...] = total[8:12, 12288:]


def widen_outputs(total):
    step = 32
    shapes = [(TILE, 3072), (TILE, WIDTH), (TILE, 4096), (4, TILE, WIDTH), (6, TILE), (2, TILE), (4, TILE)]
    specs = [pl.BlockSpec((step, shape[1]), lambda i: (i, 0)) for shape in shapes[:3]]
    specs.append(pl.BlockSpec((4, step, WIDTH), lambda i: (0, i, 0)))
    specs += [pl.BlockSpec(shape, lambda i: (0, 0)) for shape in shapes[4:]]
    outs = pl.pallas_call(
        widen_kernel,
        grid=(TILE // step,),
        out_shape=[jax.ShapeDtypeStruct(shape, jnp.float32) for shape in shapes],
        in_specs=[pl.BlockSpec((step, PAYLOAD), lambda i: (i, 0))],
        out_specs=specs,
        name="widen_outputs",
    )(total)
    return (*outs[:3], outs[3].reshape(512, WIDTH), outs[4], outs[5], outs[6].reshape(512))


def row_mean(rows):
    return jnp.mean(rows, axis=-1, keepdims=True)


def norm_forward(summed):
    center = summed - row_mean(summed)
    inverse = lax.rsqrt(row_mean(center * center) + EPSILON)
    return center * inverse, inverse


def norm_backward(grad_rows, normed, inverse, gain_row):
    scaled = grad_rows * gain_row
    return inverse * (scaled - row_mean(scaled) - normed * row_mean(scaled * normed))


def strips(body):
    def one(n, carry):
        body(pl.ds(pl.multiple_of(n * STRIP, STRIP), STRIP))
        return carry

    lax.fori_loop(0, ROWS // STRIP, one, 0)


def layer_kernel(
    ends,
    id_column,
    id_row,
    w_qkv_shard,
    w_out_shard,
    w_in_shard,
    w_down_shard,
    small_shard,
    ends_out,
    rows_in_far,
    context_far,
    normed_low_far,
    activated_far,
    joined_far,
    first_low_far,
    pre_low_far,
    second_low_far,
    small_far,
    w_qkv,
    w_out,
    w_in,
    w_down,
    small,
    vec,
    sums,
    rows_in,
    cotangent,
    leaving,
    qkv,
    context,
    first_normed,
    first_inverse,
    normed_out,
    normed_low,
    activated,
    slope,
    second_normed,
    second_inverse,
    chances,
    second_low,
    pre_low,
    first_low,
    joined,
    total,
    small_rows,
    small_tile,
    load_sem,
    store_sem,
    send_sem,
    recv_sem,
    gather_send_sem,
    gather_recv_sem,
):
    section = lax.axis_index("section")
    other = {"section": 1 - section}
    copies = Copies(gather_send_sem, gather_recv_sem)
    arrived = gather_into(
        (w_qkv_shard, w_out_shard, w_in_shard, w_down_shard, small_shard),
        (w_qkv, w_out, w_in, w_down, small),
        copies,
        load_sem,
        (other,),
    )
    stores = []

    def store(near, far):
        copy = pltpu.make_async_copy(near, far, store_sem.at[len(stores)])
        copy.start()
        stores.append(copy)

    onward = pltpu.make_async_remote_copy(
        src_ref=leaving, dst_ref=rows_in, send_sem=send_sem.at[0], recv_sem=recv_sem.at[0],
        device_id=other, device_id_type=MESH,
    )
    back = pltpu.make_async_remote_copy(
        src_ref=leaving, dst_ref=cotangent, send_sem=send_sem.at[1], recv_sem=recv_sem.at[1],
        device_id=other, device_id_type=MESH,
    )
    arrived(4)
    for f in range(N_F):
        shard = small[f * SMALL_ROWS : (f + 1) * SMALL_ROWS, :TILE].astype(jnp.float32)
        vec[0:8, f * TILE : (f + 1) * TILE] = shard[0:8]
        for i in range(4):
            first = (f % 2) * 512 + i * TILE
            vec[8 + f // 2 : 9 + f // 2, first : first + TILE] = shard[8 + i : 9 + i]
    sums[...] = jnp.zeros_like(sums)
    lane = lax.broadcasted_iota(jnp.int32, (1, TILE), 1)
    head_masks = [
        jnp.where((lane < HEAD_DIM) == (h == 0), 1.0, 0.0).astype(jnp.bfloat16) for h in (0, 1)
    ]

    @pl.when(section == 0)
    def _():
        rows_in[...] = ends[...]

    @pl.when(section == 1)
    def _():
        cotangent[...] = ends[...]
        onward.wait_recv()

    arrived(0)
    store(rows_in, rows_in_far)
    for j in range(6):
        columns = slice(j * 512, (j + 1) * 512)
        projected = dot(rows_in[...], w_qkv[:, columns])
        if j // 2 != 1:
            row = 0 if j < 2 else 1
            first = (j % 2) * 512
            projected = projected + vec[row : row + 1, first : first + 512]
        qkv[:, columns] = projected.astype(jnp.bfloat16)

    def head_columns(p, part):
        return pl.ds(pl.multiple_of(part * WIDTH + p * TILE, TILE), TILE)

    def attend(p, carry):
        for b in (0, 1):
            rows = slice(b * TILE, (b + 1) * TILE)
            query = qkv[rows, head_columns(p, 0)]
            key = qkv[rows, head_columns(p, 1)]
            value = qkv[rows, head_columns(p, 2)]
            same = id_column[rows, :] == id_row[:, rows]
            mixed = None
            for h in (0, 1):
                scores = dot_last(query * head_masks[h], key) * HEAD_DIM ** (-0.5)
                scores = jnp.where(same, scores, -1e30)
                exponent = jnp.exp(scores - jnp.max(scores, axis=-1, keepdims=True))
                share = exponent / jnp.sum(exponent, axis=-1, keepdims=True)
                low = share.astype(jnp.bfloat16)
                chances[p * 4 + b * 2 + h] = low
                part = dot(low, value * head_masks[h])
                mixed = part if mixed is None else mixed + part
            context[rows, head_columns(p, 0)] = mixed.astype(jnp.bfloat16)
        return carry

    lax.fori_loop(0, HEADS // 2, attend, 0)
    arrived(1)
    store(context, context_far)
    total[...] = dot(context[...], w_out[...])

    def first_norm(rows):
        summed = rows_in[rows, :].astype(jnp.float32) + total[rows, :] + vec[2:3, :]
        normed, inverse = norm_forward(summed)
        first_normed[rows, :] = normed
        first_inverse[rows, :] = jnp.broadcast_to(inverse, (STRIP, TILE))
        shifted = normed * vec[6:7, :] + vec[3:4, :]
        normed_out[rows, :] = shifted
        normed_low[rows, :] = shifted.astype(jnp.bfloat16)

    strips(first_norm)
    store(normed_low, normed_low_far)
    arrived(2)
    arrived(3)

    def widen(j):
        columns = slice(j * FF_STEP, (j + 1) * FF_STEP)
        row, first = j * FF_STEP // WIDTH, j * FF_STEP % WIDTH
        pre_act = dot(normed_low[...], w_in[:, columns])
        pre_act = pre_act + vec[8 + row : 9 + row, first : first + FF_STEP]
        phi = 0.5 * (1.0 + lax.erf(pre_act * 0.7071067811865476))
        activated[:, columns] = (pre_act * phi).astype(jnp.bfloat16)
        density = jnp.exp(-0.5 * pre_act * pre_act) * 0.3989422804014327
        slope[:, columns] = (phi + pre_act * density).astype(jnp.bfloat16)

    for j in range(FF_WIDTH // FF_STEP):
        widen(j)
    for n in range(2):
        columns = slice(n * 512, (n + 1) * 512)
        total[:, columns] = dot(activated[...], w_down[:, columns])

    store(activated, activated_far)

    def second_norm(rows):
        summed = normed_out[rows, :] + total[rows, :] + vec[4:5, :]
        normed, inverse = norm_forward(summed)
        second_normed[rows, :] = normed
        second_inverse[rows, :] = jnp.broadcast_to(inverse, (STRIP, TILE))
        leaving[rows, :] = (normed * vec[7:8, :] + vec[5:6, :]).astype(jnp.bfloat16)

    strips(second_norm)

    @pl.when(section == 0)
    def _():
        onward.start()
        onward.wait_send()
        back.wait_recv()

    @pl.when(section == 1)
    def _():
        ends_out[...] = leaving[...]

    def add_sum(row, values):
        sums[row : row + 1, :] += jnp.sum(values, axis=0, keepdims=True)

    def second_back(rows):
        grad = cotangent[rows, :].astype(jnp.float32)
        normed = second_normed[rows, :]
        add_sum(5, grad)
        add_sum(7, grad * normed)
        grad = norm_backward(grad, normed, second_inverse[rows, 0:1], vec[7:8, :])
        add_sum(4, grad)
        normed_out[rows, :] = grad
        second_low[rows, :] = grad.astype(jnp.bfloat16)

    strips(second_back)
    store(second_low, second_low_far)
    for j in range(FF_WIDTH // FF_STEP):
        columns = slice(j * FF_STEP, (j + 1) * FF_STEP)
        row, first = j * FF_STEP // WIDTH, j * FF_STEP % WIDTH
        grad = dot_last(second_low[...], w_down[columns, :]) * slope[:, columns].astype(jnp.float32)
        sums[8 + row : 9 + row, first : first + FF_STEP] = jnp.sum(grad, axis=0, keepdims=True)
        pre_low[:, columns] = grad.astype(jnp.bfloat16)
    for n in range(2):
        columns = slice(n * 512, (n + 1) * 512)
        total[:, columns] = dot_last(pre_low[...], w_in[columns, :])

    store(pre_low, pre_low_far)

    def first_back(rows):
        grad = normed_out[rows, :] + total[rows, :]
        normed = first_normed[rows, :]
        add_sum(3, grad)
        add_sum(6, grad * normed)
        grad = norm_backward(grad, normed, first_inverse[rows, 0:1], vec[6:7, :])
        add_sum(2, grad)
        normed_out[rows, :] = grad
        first_low[rows, :] = grad.astype(jnp.bfloat16)

    strips(first_back)
    store(first_low, first_low_far)
    context_grad = leaving
    for n in range(2):
        columns = slice(n * 512, (n + 1) * 512)
        context_grad[:, columns] = dot_last(first_low[...], w_out[columns, :]).astype(jnp.bfloat16)

    def attend_back(p, carry):
        for b in (0, 1):
            rows = slice(b * TILE, (b + 1) * TILE)
            query = qkv[rows, head_columns(p, 0)]
            key = qkv[rows, head_columns(p, 1)]
            value = qkv[rows, head_columns(p, 2)]
            grads = context_grad[rows, head_columns(p, 0)]
            results = [0.0, 0.0, 0.0]
            for h in (0, 1):
                own = grads * head_masks[h]
                low = chances[p * 4 + b * 2 + h]
                share = low.astype(jnp.float32)
                weight_grad = dot_last(own, value)
                inner = jnp.sum(share * weight_grad, axis=-1, keepdims=True)
                score = (share * (weight_grad - inner) * HEAD_DIM ** (-0.5)).astype(jnp.bfloat16)
                results[0] += dot(score, key * head_masks[h])
                results[1] += dot_first(score, query * head_masks[h])
                results[2] += dot_first(low, own)
            for part in range(3):
                joined[rows, head_columns(p, part)] = results[part].astype(jnp.bfloat16)
            for row, part in ((0, 0), (1, 2)):
                here = head_columns(p, 0)
                sums[row : row + 1, here] += jnp.sum(results[part], axis=0, keepdims=True)
        return carry

    lax.fori_loop(0, HEADS // 2, attend_back, 0)
    store(joined, joined_far)
    for n in range(2):
        columns = slice(n * 512, (n + 1) * 512)
        grad = normed_out[:, columns] + dot_last(joined[...], w_qkv[columns, :])
        leaving[:, columns] = grad.astype(jnp.bfloat16)

    @pl.when(section == 1)
    def _():
        back.start()

    @pl.when(section == 0)
    def _():
        ends_out[...] = leaving[...]

    for f in range(N_F):
        small_rows[f, 0:8, :] = sums[0:8, f * TILE : (f + 1) * TILE]
        for i in range(4):
            first = (f % 2) * 512 + i * TILE
            small_rows[f, 8 + i : 9 + i, :] = sums[8 + f // 2 : 9 + f // 2, first : first + TILE]
        small_rows[f, 12:16, :] = jnp.zeros((4, TILE), jnp.float32)
    small_tile[...] = jnp.zeros_like(small_tile)
    for f in range(N_F):
        small_tile[f // 2, f % 2, 0:16, :] = small_rows[f].astype(jnp.bfloat16)
    store(small_tile, small_far)
    for copy in stores:
        copy.wait()
    copies.finish()

    @pl.when(section == 1)
    def _():
        back.wait_send()


def run_layer(ends, ids, shards):
    low, full = jnp.bfloat16, jnp.float32
    scratch = [
        ((1024, 3072), low),
        ((1024, 1024), low),
        ((1024, 4096), low),
        ((4096, 1024), low),
        ((N_F * SMALL_ROWS, 2 * TILE), low),
        ((16, WIDTH), full),
        ((16, WIDTH), full),
        ((ROWS, WIDTH), low),
        ((ROWS, WIDTH), low),
        ((ROWS, WIDTH), low),
        ((ROWS, 3 * WIDTH), low),
        ((ROWS, WIDTH), low),
        ((ROWS, WIDTH), full),
        ((ROWS, TILE), full),
        ((ROWS, WIDTH), full),
        ((ROWS, WIDTH), low),
        ((ROWS, FF_WIDTH), low),
        ((ROWS, FF_WIDTH), low),
        ((ROWS, WIDTH), full),
        ((ROWS, TILE), full),
        ((2 * HEADS, TILE, TILE), low),
        ((ROWS, WIDTH), low),
        ((ROWS, FF_WIDTH), low),
        ((ROWS, WIDTH), low),
        ((ROWS, 3 * WIDTH), low),
        ((ROWS, WIDTH), full),
        ((N_F, SMALL_ROWS, TILE), full),
        ((4, 2, TILE, TILE), low),
    ]
    near = pl.BlockSpec(memory_space=pltpu.VMEM)
    far = pl.BlockSpec(memory_space=pl.ANY)
    return pl.pallas_call(
        layer_kernel,
        out_shape=[
            jax.ShapeDtypeStruct((ROWS, WIDTH), low),
            *[jax.ShapeDtypeStruct((ROWS, columns * WIDTH), low) for columns in (1, 1, 1, 4, 3, 1, 4, 1)],
            jax.ShapeDtypeStruct((4, 2, TILE, TILE), low),
        ],
        in_specs=[near, near, near, far, far, far, far, far],
        out_specs=[near, *[far] * 9],
        scratch_shapes=[
            *[pltpu.VMEM(shape, kind) for shape, kind in scratch],
            pltpu.SemaphoreType.DMA((5,)),
            pltpu.SemaphoreType.DMA((9,)),
            pltpu.SemaphoreType.DMA((2,)),
            pltpu.SemaphoreType.DMA((2,)),
            pltpu.SemaphoreType.DMA((GATHER_COPIES,)),
            pltpu.SemaphoreType.DMA((GATHER_COPIES,)),
        ],
        compiler_params=pltpu.CompilerParams(
            collective_id=2, has_side_effects=True, vmem_limit_bytes=VMEM_CAP
        ),
        name="run_layer",
    )(ends, ids[:, None], ids[None, :], *shards)


def pack_small(biases, gains, bias_in):
    rows = jnp.concatenate([biases, gains, bias_in.reshape(4, TILE)], axis=0)
    return jnp.pad(rows, ((0, 4), (0, TILE)))


def body(ends_in, segment_ids, w_qkv, w_out, w_in, w_down, biases, gains, bias_in):
    shards = (w_qkv[0], w_out[0], w_in[0], w_down[0], pack_small(biases[0], gains[0], bias_in[0]))
    ids = segment_ids + (lax.iota(jnp.int32, ROWS) // SEQ) * 16
    ends_out, *operands = run_layer(ends_in[0], ids, shards)
    outs = widen_outputs(reduce_grads(*operands))
    return tuple(member[None] for member in (ends_out, *outs))


def solution(mesh):
    in_specs = (
        P("section", ("fsdp", "replica"), None),
        P(("fsdp", "replica")),
        P("section", "fsdp", None),
        P("section", "fsdp", None),
        P("section", "fsdp", None),
        P("section", "fsdp", None),
        P("section", None, "fsdp"),
        P("section", None, "fsdp"),
        P("section", "fsdp"),
    )
    out_specs = (
        P("section", ("fsdp", "replica"), None),
        P("section", "fsdp", None),
        P("section", "fsdp", None),
        P("section", "fsdp", None),
        P("section", "fsdp", None),
        P("section", None, "fsdp"),
        P("section", None, "fsdp"),
        P("section", "fsdp"),
    )
    return jax.shard_map(body, mesh=mesh, in_specs=in_specs, out_specs=out_specs, check_vma=False)
```

```python
import jax
import jax.numpy as jnp
from jax import lax
from jax.experimental import pallas as pl
from jax.experimental.pallas import tpu as pltpu
from jax.sharding import PartitionSpec as P

HEADS = 16
HEAD_DIM = 64
SEQ = 64
EPSILON = 1e-05
ROWS = 256
WIDTH = 1024
FF_WIDTH = 4096
STRIP = 32
HALF = 128
FF_STEP = 512


def dot(a, b):
    return jnp.dot(a, b, preferred_element_type=jnp.float32)


def dot_last(a, b):
    return lax.dot_general(a, b, (((1,), (1,)), ((), ())), preferred_element_type=jnp.float32)


def dot_first(a, b):
    return lax.dot_general(a, b, (((0,), (0,)), ((), ())), preferred_element_type=jnp.float32)


MESH = pl.DeviceIdType.MESH
N_F = 8
TILE = 128
SMALL_ROWS = 16
GATHER_COPIES = 112
PAYLOAD = 97 * TILE
VMEM_CAP = 60 * 1024 * 1024

GATHER_PLAN = ((128, 3072, 16), (128, 1024, 16), (128, 4096, 16), (512, 1024, 128), (16, 256, 0))


def place():
    f = lax.axis_index("fsdp")
    r = lax.axis_index("replica")
    return f // 2, lax.rem(f, 2), r // 2, lax.rem(r, 2)


def device(y, c, x, z):
    return {"fsdp": y * 2 + c, "replica": x * 2 + z}


def step_on(index, distance):
    return lax.rem(index + distance + 4, 4)


def greet(peers):
    barrier = pltpu.get_barrier_semaphore()
    for peer in peers:
        pl.semaphore_signal(barrier, inc=1, device_id=peer, device_id_type=MESH)
    pl.semaphore_wait(barrier, len(peers))


class Copies:
    def __init__(self, send_sem, recv_sem):
        self.send_sem, self.recv_sem, self.count, self.unsent = send_sem, recv_sem, 0, []

    def start(self, src, dst, peer):
        copy = pltpu.make_async_remote_copy(
            src_ref=src,
            dst_ref=dst,
            send_sem=self.send_sem.at[self.count],
            recv_sem=self.recv_sem.at[self.count],
            device_id=peer,
            device_id_type=MESH,
        )
        copy.start()
        self.count += 1
        self.unsent.append(copy)
        return copy

    def sent(self, copy):
        copy.wait_send()
        self.unsent = [member for member in self.unsent if member is not copy]

    def finish(self):
        for copy in self.unsent:
            copy.wait_send()


def gather_into(ins, outs, copies, local_sem, others):
    count = len(GATHER_PLAN)
    y, c, x, z = place()
    right_y, left_y = device(step_on(y, 1), c, x, z), device(step_on(y, -1), c, x, z)
    right_x, left_x = device(y, c, step_on(x, 1), z), device(y, c, step_on(x, -1), z)
    sibling = device(y, 1 - c, x, z)
    own = []
    for k in range(count):
        start = pl.multiple_of((y * 2 + c) * GATHER_PLAN[k][0], 16)
        here = outs[k].at[pl.ds(start, GATHER_PLAN[k][0]), :]
        own.append(pltpu.make_async_copy(ins[k], here, local_sem.at[k]))
        own[-1].start()
    greet((right_y, left_y, right_x, left_x, sibling, *others))

    def span(k, owner_y, first, rows, part=None):
        shard_rows, columns, _ = GATHER_PLAN[k]
        start = pl.multiple_of((owner_y * 2 + c) * shard_rows + first, 16)
        if part is None:
            return outs[k].at[pl.ds(start, rows), :]
        half = columns // 2
        return outs[k].at[pl.ds(start, rows), pl.ds(part * half, half)]

    def quarter(k, owner_x):
        return pl.multiple_of(owner_x * GATHER_PLAN[k][2], 16)

    relayed = [k for k in range(count) if GATHER_PLAN[k][2]]
    direct = [k for k in range(count) if GATHER_PLAN[k][0] > 4 * GATHER_PLAN[k][2]]
    first_right, first_left, second_right, second_left = {}, {}, {}, {}
    along_right, along_left, sibling_copies, further = {}, {}, {}, {}
    before, after, across = owners = (step_on(y, -1), step_on(y, 1), step_on(y, 2))

    def extent(kind, k):
        shard_rows, _, piece = GATHER_PLAN[k]
        return (quarter(k, x), piece) if kind == "relay" else (4 * piece, shard_rows - 4 * piece)

    def send_own(kind, k):
        block = span(k, y, *extent(kind, k))
        first_right[kind, k] = copies.start(block, block, right_y)
        first_left[kind, k] = copies.start(block, block, left_y)

    def send_on(kind, k):
        first_right[kind, k].wait_recv()
        block = span(k, before, *extent(kind, k), 0)
        second_right[kind, k] = copies.start(block, block, right_y)
        first_left[kind, k].wait_recv()
        block = span(k, after, *extent(kind, k), 1)
        second_left[kind, k] = copies.start(block, block, left_y)

    def send_along(n, k):
        block = span(k, owners[n], *extent("relay", k))
        along_right[n, k] = copies.start(block, block, right_x)
        along_left[n, k] = copies.start(block, block, left_x)

    def send_further(n, k):
        piece = GATHER_PLAN[k][2]
        along_right[n, k].wait_recv()
        block = span(k, owners[n], quarter(k, step_on(x, -1)), piece, 0)
        further[n, k, 0] = copies.start(block, block, right_x)
        along_left[n, k].wait_recv()
        block = span(k, owners[n], quarter(k, step_on(x, 1)), piece, 1)
        further[n, k, 1] = copies.start(block, block, left_x)

    for k in relayed:
        own[k].wait()
        send_own("relay", k)
    for k in range(count):
        if k not in relayed:
            own[k].wait()
        block = span(k, y, 0, GATHER_PLAN[k][0])
        sibling_copies[3, k] = copies.start(block, block, sibling)
    for k in relayed:
        send_on("relay", k)
        send_along(0, k)
        send_along(1, k)
    for k in direct[::-1]:
        send_own("direct", k)
    for k in relayed:
        second_right["relay", k].wait_recv()
        second_left["relay", k].wait_recv()
        send_along(2, k)
    for n in (0, 1):
        for k in relayed:
            send_further(n, k)
    for k in direct[::-1]:
        send_on("direct", k)
    for k in relayed:
        send_further(2, k)
    for k in range(count):
        for n in range(3):
            if n == 2 and k in direct:
                second_right["direct", k].wait_recv()
                second_left["direct", k].wait_recv()
            if k in relayed:
                further[n, k, 0].wait_recv()
                further[n, k, 1].wait_recv()
            block = span(k, owners[n], 0, GATHER_PLAN[k][0])
            sibling_copies[n, k] = copies.start(block, block, sibling)

    def arrived(k):
        for n in range(4):
            sibling_copies[n, k].wait_recv()

    return arrived


REDUCE_PLAN = tuple(
    (unit, 1, "yxy"[n % 3]) for n, unit in enumerate((4, 5, 6, 7, 0, 1, 2, 3, 8, 9, 10, 11))
)
UNITS = 12


def chunk_width(plan):
    first, units, _ = plan
    return units * WIDTH + (TILE if first + units == UNITS else 0)


def stage_shape(plan, stage):
    shapes = {("y", 0): (1, 128), ("x", 0): (4, 32), ("y", 1): (1, 32), ("x", 1): (1, 32)}
    blocks, height = shapes[plan[2], stage]
    return blocks, height, chunk_width(plan)


def add_rows(blocks, height, reads, write):
    def one(step, carry):
        block = step // (height // 16)
        row = pl.multiple_of(lax.rem(step, height // 16) * 16, 16)
        total = reads[0](block, row).astype(jnp.float32)
        for read in reads[1:]:
            total = total + read(block, row).astype(jnp.float32)
        write(block, row, total.astype(jnp.bfloat16))
        return carry

    lax.fori_loop(0, blocks * (height // 16), one, 0)


def reduce_kernel(*refs):
    far, out = refs[:9], refs[9]
    near, (staged, held, crossed, gathered) = refs[10:19], refs[19:23]
    stage_refs, (load_sem, store_sem, send_sem, recv_sem) = refs[23:-4], refs[-4:]
    rows_in, context, normed_low, activated, joined, first_low, pre_low, second_low, small = near
    loads = [pltpu.make_async_copy(a, b, load_sem.at[n]) for n, (a, b) in enumerate(zip(far, near))]
    needs = {0: (0, 4), 3: (1, 5), 4: (2, 6), 8: (3, 7), 12: (8,)}
    sources = lambda unit: needs[max(key for key in needs if key <= unit)]
    pending = []
    for first, units, _ in REDUCE_PLAN:
        for unit in (first, first + units - 1):
            pending += [n for n in sources(unit) if n not in pending]
    pending.append(8)
    for n in pending:
        loads[n].start()
    y, c, x, z = place()
    ring = {
        "y": (y, device(step_on(y, 1), c, x, z), device(step_on(y, -1), c, x, z)),
        "x": (x, device(y, c, step_on(x, 1), z), device(y, c, step_on(x, -1), z)),
    }
    sibling = device(y, 1 - c, x, z)
    partner = device(y, c, x, 1 - z)
    greet((ring["y"][1], ring["y"][2], ring["x"][1], ring["x"][2], sibling, partner))
    copies = Copies(send_sem, recv_sem)
    to_sibling, stores = [], []

    def ready(numbers):
        for n in numbers:
            if n in pending:
                loads[n].wait()
                pending.remove(n)

    def produce(n):
        first, units, _ = REDUCE_PLAN[n]
        slot = n % 2
        for unit in range(first, first + units):
            ready(sources(unit))

        def block_rows(at, carry):
            for unit in range(first, min(first + units, 8)):
                if unit < 3:
                    left, right, column = rows_in, joined, unit
                elif unit == 3:
                    left, right, column = context, first_low, 0
                else:
                    left, right, column = normed_low, pre_low, unit - 4
                tile = dot_first(
                    left[:, pl.ds(pl.multiple_of(at * 256, 256), 256)],
                    right[:, column * WIDTH : (column + 1) * WIDTH],
                ).astype(jnp.bfloat16)
                place_at = slice((unit - first) * WIDTH, (unit - first + 1) * WIDTH)
                staged[slot, at, :, :, place_at] = tile.reshape(2, TILE, WIDTH)
            if first >= 8:
                for core in (0, 1):
                    start = at * WIDTH + core * 512 + (first - 8) * TILE
                    rows = activated[:, pl.ds(pl.multiple_of(start, TILE), units * TILE)]
                    tile = dot_first(rows, second_low[...]).astype(jnp.bfloat16)
                    for unit in range(units):
                        place_at = slice(unit * WIDTH, (unit + 1) * WIDTH)
                        staged[slot, at, core, :, place_at] = tile[unit * TILE : (unit + 1) * TILE]
            return carry

        lax.fori_loop(0, 4, block_rows, 0)
        if first + units == UNITS:
            ready((8,))
            for at in range(4):
                for core in (0, 1):
                    staged[slot, at, core, :, units * WIDTH : units * WIDTH + TILE] = small[at, core]

    def along(n, stage):
        first, _, leading = REDUCE_PLAN[n]
        offset, wide_a = first * WIDTH, REDUCE_PLAN[n][1] * WIDTH // 2
        wide_b = chunk_width(REDUCE_PLAN[n]) - wide_a
        start_a, start_b = offset, offset + wide_a
        axis = leading if stage == 0 else ("x" if leading == "y" else "y")
        index, right, left = ring[axis]
        blocks, height, _ = stage_shape(REDUCE_PLAN[n], stage)
        landing = stage_refs[2 * n + stage]

        def origin(at):
            if axis == "y":
                return at, (0 if stage == 0 else x * 32)
            return (0 if stage == 0 else y), at * 32

        def take(at, start, wide):
            block, row = origin(at)
            return held.at[
                pl.ds(block, blocks), pl.ds(pl.multiple_of(row, 16), height), pl.ds(start, wide)
            ]

        def land(slot, start, wide):
            return landing.at[pl.ds(slot * blocks, blocks), :, pl.ds(start - offset, wide)]

        def add(at, start, wide, slots):
            first_block, first_row = origin(at)

            def own(block, row):
                return first_block + block, pl.ds(
                    pl.multiple_of(first_row + row, 16), 16
                ), pl.ds(start, wide)

            def write(block, row, total):
                held[own(block, row)] = total

            def landed(slot):
                return lambda block, row: landing[
                    slot * blocks + block, pl.ds(row, 16), pl.ds(start - offset, wide)
                ]

            reads = [lambda block, row: held[own(block, row)], *[landed(slot) for slot in slots]]
            add_rows(blocks, height, reads, write)

        ahead, behind, across = step_on(index, 1), step_on(index, -1), step_on(index, 2)
        far_right = copies.start(take(across, start_a, wide_a), land(0, start_a, wide_a), right)
        far_left = copies.start(take(across, start_b, wide_b), land(0, start_b, wide_b), left)
        near_copies = [
            copies.start(take(ahead, start_b, wide_b), land(1, start_b, wide_b), right),
            copies.start(take(behind, start_a, wide_a), land(2, start_a, wide_a), left),
        ]
        yield
        far_right.wait_recv()
        add(ahead, start_a, wide_a, (0,))
        near_copies.append(
            copies.start(take(ahead, start_a, wide_a), land(1, start_a, wide_a), right)
        )
        far_left.wait_recv()
        add(behind, start_b, wide_b, (0,))
        near_copies.append(
            copies.start(take(behind, start_b, wide_b), land(2, start_b, wide_b), left)
        )
        yield
        for copy in near_copies:
            copy.wait_recv()
        add(index, start_a, wide_a + wide_b, (1, 2))

    def chunk(n):
        plan = REDUCE_PLAN[n]
        start, wide, slot = plan[0] * WIDTH, chunk_width(plan), n % 2
        wide_a = plan[1] * WIDTH // 2
        columns = pl.ds(start, wide)
        if n >= 2:
            copies.sent(to_sibling[n - 2])
        produce(n)
        to_sibling.append(
            copies.start(
                staged.at[slot, :, 1 - c, :, pl.ds(0, wide)], held.at[:, :, columns], sibling
            )
        )
        yield
        to_sibling[n].wait_recv()

        def write(block, row, total):
            held[block, pl.ds(row, 16), columns] = total

        add_rows(
            4,
            128,
            [
                lambda block, row: held[block, pl.ds(row, 16), columns],
                lambda block, row: staged[slot, block, c, pl.ds(row, 16), pl.ds(0, wide)],
            ],
            write,
        )
        yield from along(n, 0)
        yield from along(n, 1)

        def rows_of(at, first=start, width=wide):
            return gathered.at[pl.ds(pl.multiple_of(at * 32, 16), 32), pl.ds(first, width)]

        swap = copies.start(
            held.at[pl.ds(y, 1), pl.ds(pl.multiple_of(x * 32, 16), 32), columns],
            crossed.at[:, :, columns],
            partner,
        )
        yield
        swap.wait_recv()

        def finish(block, row, total):
            gathered[pl.ds(pl.multiple_of(x * 32 + row, 16), 16), columns] = total

        add_rows(
            1,
            32,
            [
                lambda block, row: held[y, pl.ds(pl.multiple_of(x * 32 + row, 16), 16), columns],
                lambda block, row: crossed[0, pl.ds(row, 16), columns],
            ],
            finish,
        )
        _, right, left = ring["x"]
        to_right = copies.start(rows_of(x), rows_of(x), right)
        to_left = copies.start(rows_of(x), rows_of(x), left)
        yield
        to_right.wait_recv()
        block = rows_of(step_on(x, -1), start, wide_a)
        last = [copies.start(block, block, right)]
        to_left.wait_recv()
        block = rows_of(step_on(x, 1), start + wide_a, wide - wide_a)
        last.append(copies.start(block, block, left))
        yield
        for copy in last:
            copy.wait_recv()
        stores.append(
            pltpu.make_async_copy(gathered.at[:, columns], out.at[:, columns], store_sem.at[n])
        )
        stores[-1].start()

    waiting = [chunk(n) for n in range(len(REDUCE_PLAN))]
    running = []
    while waiting or running:
        if waiting:
            running.append(waiting.pop(0))
        for member in running[::-1]:
            if next(member, "end") == "end":
                running.remove(member)
    for copy in stores:
        copy.wait()
    copies.finish()


def reduce_grads(*operands):
    chunks = len(REDUCE_PLAN)
    widest = max(chunk_width(plan) for plan in REDUCE_PLAN)
    landing = []
    for plan in REDUCE_PLAN:
        for stage in (0, 1):
            blocks, height, width = stage_shape(plan, stage)
            landing.append(pltpu.VMEM((3 * blocks, height, width), jnp.bfloat16))
    far = pl.BlockSpec(memory_space=pl.ANY)
    return pl.pallas_call(
        reduce_kernel,
        out_shape=jax.ShapeDtypeStruct((TILE, PAYLOAD), jnp.bfloat16),
        in_specs=[far] * len(operands),
        out_specs=far,
        scratch_shapes=[
            *[pltpu.VMEM(operand.shape, operand.dtype) for operand in operands],
            pltpu.VMEM((2, 4, 2, TILE, widest), jnp.bfloat16),
            pltpu.VMEM((4, TILE, PAYLOAD), jnp.bfloat16),
            pltpu.VMEM((1, 32, PAYLOAD), jnp.bfloat16),
            pltpu.VMEM((TILE, PAYLOAD), jnp.bfloat16),
            *landing,
            pltpu.SemaphoreType.DMA((len(operands),)),
            pltpu.SemaphoreType.DMA((chunks,)),
            pltpu.SemaphoreType.DMA((chunks * 18,)),
            pltpu.SemaphoreType.DMA((chunks * 18,)),
        ],
        compiler_params=pltpu.CompilerParams(
            collective_id=1, has_side_effects=True, vmem_limit_bytes=VMEM_CAP
        ),
        name="reduce_grads",
    )(*operands)


def widen_kernel(low, qkv, out, into, down, bias, gain, hidden):
    total = low[...].astype(jnp.float32)
    qkv[...] = total[:, :3072]
    out[...] = total[:, 3072:4096]
    into[...] = total[:, 4096:8192]
    for j in range(4):
        down[j] = total[:, 8192 + j * WIDTH : 8192 + (j + 1) * WIDTH]

    @pl.when(pl.program_id(0) == 0)
    def _():
        bias[...] = total[0:6, 12288:]
        gain[...] = total[6:8, 12288:]
        hidden[...] = total[8:12, 12288:]


def widen_outputs(total):
    step = 32
    shapes = [(TILE, 3072), (TILE, WIDTH), (TILE, 4096), (4, TILE, WIDTH), (6, TILE), (2, TILE), (4, TILE)]
    specs = [pl.BlockSpec((step, shape[1]), lambda i: (i, 0)) for shape in shapes[:3]]
    specs.append(pl.BlockSpec((4, step, WIDTH), lambda i: (0, i, 0)))
    specs += [pl.BlockSpec(shape, lambda i: (0, 0)) for shape in shapes[4:]]
    outs = pl.pallas_call(
        widen_kernel,
        grid=(TILE // step,),
        out_shape=[jax.ShapeDtypeStruct(shape, jnp.float32) for shape in shapes],
        in_specs=[pl.BlockSpec((step, PAYLOAD), lambda i: (i, 0))],
        out_specs=specs,
        name="widen_outputs",
    )(total)
    return (*outs[:3], outs[3].reshape(512, WIDTH), outs[4], outs[5], outs[6].reshape(512))


def row_mean(rows):
    return jnp.mean(rows, axis=-1, keepdims=True)


def norm_forward(summed):
    center = summed - row_mean(summed)
    inverse = lax.rsqrt(row_mean(center * center) + EPSILON)
    return center * inverse, inverse


def norm_backward(grad_rows, normed, inverse, gain_row):
    scaled = grad_rows * gain_row
    return inverse * (scaled - row_mean(scaled) - normed * row_mean(scaled * normed))


def strips(body, first):
    def one(n, carry):
        body(pl.ds(pl.multiple_of(first + n * STRIP, STRIP), STRIP))
        return carry

    lax.fori_loop(0, HALF // STRIP, one, 0)


def halves(body):
    def one(n, carry):
        body(n, pl.multiple_of(n * HALF, HALF))
        return carry

    lax.fori_loop(0, 2, one, 0)


def layer_kernel(
    ends,
    id_column,
    id_row,
    w_qkv_shard,
    w_out_shard,
    w_in_shard,
    w_down_shard,
    small_shard,
    ends_out,
    rows_in_far,
    context_far,
    normed_low_far,
    activated_far,
    joined_far,
    first_low_far,
    pre_low_far,
    second_low_far,
    small_far,
    w_qkv,
    w_out,
    w_in,
    w_down,
    small,
    vec,
    sums,
    rows_in,
    cotangent,
    leaving,
    qkv,
    context,
    first_normed,
    first_inverse,
    normed_out,
    normed_low,
    activated,
    slope,
    second_normed,
    second_inverse,
    chances,
    second_low,
    pre_low,
    first_low,
    joined,
    total,
    small_rows,
    small_tile,
    load_sem,
    store_sem,
    send_sem,
    recv_sem,
    gather_send_sem,
    gather_recv_sem,
):
    section = lax.axis_index("section")
    other = {"section": 1 - section}
    copies = Copies(gather_send_sem, gather_recv_sem)
    arrived = gather_into(
        (w_qkv_shard, w_out_shard, w_in_shard, w_down_shard, small_shard),
        (w_qkv, w_out, w_in, w_down, small),
        copies,
        load_sem,
        (other,),
    )
    stores = []

    def store(near, far):
        copy = pltpu.make_async_copy(near, far, store_sem.at[len(stores)])
        copy.start()
        stores.append(copy)

    def passing(first, landing, number):
        rows = pl.ds(first, HALF)
        return pltpu.make_async_remote_copy(
            src_ref=leaving.at[rows, :],
            dst_ref=landing.at[rows, :],
            send_sem=send_sem.at[number],
            recv_sem=recv_sem.at[number],
            device_id=other,
            device_id_type=MESH,
        )

    arrived(4)
    for f in range(N_F):
        shard = small[f * SMALL_ROWS : (f + 1) * SMALL_ROWS, :TILE].astype(jnp.float32)
        vec[0:8, f * TILE : (f + 1) * TILE] = shard[0:8]
        for i in range(4):
            first = (f % 2) * 512 + i * TILE
            vec[8 + f // 2 : 9 + f // 2, first : first + TILE] = shard[8 + i : 9 + i]
    sums[...] = jnp.zeros_like(sums)
    lane = lax.broadcasted_iota(jnp.int32, (1, TILE), 1)
    head_masks = [
        jnp.where((lane < HEAD_DIM) == (h == 0), 1.0, 0.0).astype(jnp.bfloat16) for h in (0, 1)
    ]

    @pl.when(section == 0)
    def _():
        rows_in[...] = ends[...]

    @pl.when(section == 1)
    def _():
        cotangent[...] = ends[...]

    for k in range(4):
        arrived(k)
    def head_columns(p, part):
        return pl.ds(pl.multiple_of(part * WIDTH + p * TILE, TILE), TILE)

    def forward(number, first_row):
        rows = pl.ds(first_row, HALF)

        @pl.when(section == 1)
        def _():
            passing(first_row, rows_in, number).wait_recv()

        for j in range(6):
            columns = slice(j * 512, (j + 1) * 512)
            projected = dot(rows_in[rows, :], w_qkv[:, columns])
            if j // 2 != 1:
                row = 0 if j < 2 else 1
                first = (j % 2) * 512
                projected = projected + vec[row : row + 1, first : first + 512]
            qkv[rows, columns] = projected.astype(jnp.bfloat16)

        def attend(p, carry):
            query = qkv[rows, head_columns(p, 0)]
            key = qkv[rows, head_columns(p, 1)]
            value = qkv[rows, head_columns(p, 2)]
            same = id_column[rows, :] == id_row[:, rows]
            mixed = None
            for h in (0, 1):
                scores = dot_last(query * head_masks[h], key) * HEAD_DIM ** (-0.5)
                scores = jnp.where(same, scores, -1e30)
                exponent = jnp.exp(scores - jnp.max(scores, axis=-1, keepdims=True))
                share = exponent / jnp.sum(exponent, axis=-1, keepdims=True)
                low = share.astype(jnp.bfloat16)
                chances[p * 4 + number * 2 + h] = low
                part = dot(low, value * head_masks[h])
                mixed = part if mixed is None else mixed + part
            context[rows, head_columns(p, 0)] = mixed.astype(jnp.bfloat16)
            return carry

        lax.fori_loop(0, HEADS // 2, attend, 0)
        total[rows, :] = dot(context[rows, :], w_out[...])

        def first_norm(rows):
            summed = rows_in[rows, :].astype(jnp.float32) + total[rows, :] + vec[2:3, :]
            normed, inverse = norm_forward(summed)
            first_normed[rows, :] = normed
            first_inverse[rows, :] = jnp.broadcast_to(inverse, (STRIP, TILE))
            shifted = normed * vec[6:7, :] + vec[3:4, :]
            normed_out[rows, :] = shifted
            normed_low[rows, :] = shifted.astype(jnp.bfloat16)

        strips(first_norm, first_row)

        def widen(j):
            columns = slice(j * FF_STEP, (j + 1) * FF_STEP)
            row, first = j * FF_STEP // WIDTH, j * FF_STEP % WIDTH
            pre_act = dot(normed_low[rows, :], w_in[:, columns])
            pre_act = pre_act + vec[8 + row : 9 + row, first : first + FF_STEP]
            phi = 0.5 * (1.0 + lax.erf(pre_act * 0.7071067811865476))
            activated[rows, columns] = (pre_act * phi).astype(jnp.bfloat16)
            density = jnp.exp(-0.5 * pre_act * pre_act) * 0.3989422804014327
            slope[rows, columns] = (phi + pre_act * density).astype(jnp.bfloat16)

        for j in range(FF_WIDTH // FF_STEP):
            widen(j)
        for n in range(2):
            columns = slice(n * 512, (n + 1) * 512)
            total[rows, columns] = dot(activated[rows, :], w_down[:, columns])


        def second_norm(rows):
            summed = normed_out[rows, :] + total[rows, :] + vec[4:5, :]
            normed, inverse = norm_forward(summed)
            second_normed[rows, :] = normed
            second_inverse[rows, :] = jnp.broadcast_to(inverse, (STRIP, TILE))
            leaving[rows, :] = (normed * vec[7:8, :] + vec[5:6, :]).astype(jnp.bfloat16)

        strips(second_norm, first_row)

        @pl.when(section == 0)
        def _():
            passing(first_row, rows_in, number).start()

        @pl.when(section == 1)
        def _():
            ends_out[rows, :] = leaving[rows, :]

    halves(forward)
    store(rows_in, rows_in_far)
    store(context, context_far)
    store(normed_low, normed_low_far)
    store(activated, activated_far)

    @pl.when(section == 0)
    def _():
        for n in range(2):
            passing(n * HALF, rows_in, n).wait_send()

    def add_sum(row, values):
        sums[row : row + 1, :] += jnp.sum(values, axis=0, keepdims=True)

    def backward(number, first_row):
        rows = pl.ds(first_row, HALF)

        @pl.when(section == 0)
        def _():
            passing(first_row, cotangent, 2 + number).wait_recv()

        def second_back(rows):
            grad = cotangent[rows, :].astype(jnp.float32)
            normed = second_normed[rows, :]
            add_sum(5, grad)
            add_sum(7, grad * normed)
            grad = norm_backward(grad, normed, second_inverse[rows, 0:1], vec[7:8, :])
            add_sum(4, grad)
            normed_out[rows, :] = grad
            second_low[rows, :] = grad.astype(jnp.bfloat16)

        strips(second_back, first_row)
        for j in range(FF_WIDTH // FF_STEP):
            columns = slice(j * FF_STEP, (j + 1) * FF_STEP)
            row, first = j * FF_STEP // WIDTH, j * FF_STEP % WIDTH
            grad = dot_last(second_low[rows, :], w_down[columns, :]) * slope[rows, columns].astype(jnp.float32)
            sums[8 + row : 9 + row, first : first + FF_STEP] += jnp.sum(grad, axis=0, keepdims=True)
            pre_low[rows, columns] = grad.astype(jnp.bfloat16)
        for n in range(2):
            columns = slice(n * 512, (n + 1) * 512)
            total[rows, columns] = dot_last(pre_low[rows, :], w_in[columns, :])


        def first_back(rows):
            grad = normed_out[rows, :] + total[rows, :]
            normed = first_normed[rows, :]
            add_sum(3, grad)
            add_sum(6, grad * normed)
            grad = norm_backward(grad, normed, first_inverse[rows, 0:1], vec[6:7, :])
            add_sum(2, grad)
            normed_out[rows, :] = grad
            first_low[rows, :] = grad.astype(jnp.bfloat16)

        strips(first_back, first_row)
        context_grad = leaving
        for n in range(2):
            columns = slice(n * 512, (n + 1) * 512)
            context_grad[rows, columns] = dot_last(first_low[rows, :], w_out[columns, :]).astype(jnp.bfloat16)

        def attend_back(p, carry):
            query = qkv[rows, head_columns(p, 0)]
            key = qkv[rows, head_columns(p, 1)]
            value = qkv[rows, head_columns(p, 2)]
            grads = context_grad[rows, head_columns(p, 0)]
            results = [0.0, 0.0, 0.0]
            for h in (0, 1):
                own = grads * head_masks[h]
                low = chances[p * 4 + number * 2 + h]
                share = low.astype(jnp.float32)
                weight_grad = dot_last(own, value)
                inner = jnp.sum(share * weight_grad, axis=-1, keepdims=True)
                score = (share * (weight_grad - inner) * HEAD_DIM ** (-0.5)).astype(jnp.bfloat16)
                results[0] += dot(score, key * head_masks[h])
                results[1] += dot_first(score, query * head_masks[h])
                results[2] += dot_first(low, own)
            for part in range(3):
                joined[rows, head_columns(p, part)] = results[part].astype(jnp.bfloat16)
            for row, part in ((0, 0), (1, 2)):
                here = head_columns(p, 0)
                sums[row : row + 1, here] += jnp.sum(results[part], axis=0, keepdims=True)
            return carry

        lax.fori_loop(0, HEADS // 2, attend_back, 0)
        for n in range(2):
            columns = slice(n * 512, (n + 1) * 512)
            grad = normed_out[rows, columns] + dot_last(joined[rows, :], w_qkv[columns, :])
            leaving[rows, columns] = grad.astype(jnp.bfloat16)

        @pl.when(section == 1)
        def _():
            passing(first_row, cotangent, 2 + number).start()

        @pl.when(section == 0)
        def _():
            ends_out[rows, :] = leaving[rows, :]

    halves(backward)
    store(joined, joined_far)
    store(first_low, first_low_far)
    store(pre_low, pre_low_far)
    store(second_low, second_low_far)
    for f in range(N_F):
        small_rows[f, 0:8, :] = sums[0:8, f * TILE : (f + 1) * TILE]
        for i in range(4):
            first = (f % 2) * 512 + i * TILE
            small_rows[f, 8 + i : 9 + i, :] = sums[8 + f // 2 : 9 + f // 2, first : first + TILE]
        small_rows[f, 12:16, :] = jnp.zeros((4, TILE), jnp.float32)
    small_tile[...] = jnp.zeros_like(small_tile)
    for f in range(N_F):
        small_tile[f // 2, f % 2, 0:16, :] = small_rows[f].astype(jnp.bfloat16)
    store(small_tile, small_far)
    for copy in stores:
        copy.wait()
    copies.finish()

    @pl.when(section == 1)
    def _():
        for n in range(2):
            passing(n * HALF, cotangent, 2 + n).wait_send()


def run_layer(ends, ids, shards):
    low, full = jnp.bfloat16, jnp.float32
    scratch = [
        ((1024, 3072), low),
        ((1024, 1024), low),
        ((1024, 4096), low),
        ((4096, 1024), low),
        ((N_F * SMALL_ROWS, 2 * TILE), low),
        ((16, WIDTH), full),
        ((16, WIDTH), full),
        ((ROWS, WIDTH), low),
        ((ROWS, WIDTH), low),
        ((ROWS, WIDTH), low),
        ((ROWS, 3 * WIDTH), low),
        ((ROWS, WIDTH), low),
        ((ROWS, WIDTH), full),
        ((ROWS, TILE), full),
        ((ROWS, WIDTH), full),
        ((ROWS, WIDTH), low),
        ((ROWS, FF_WIDTH), low),
        ((ROWS, FF_WIDTH), low),
        ((ROWS, WIDTH), full),
        ((ROWS, TILE), full),
        ((2 * HEADS, TILE, TILE), low),
        ((ROWS, WIDTH), low),
        ((ROWS, FF_WIDTH), low),
        ((ROWS, WIDTH), low),
        ((ROWS, 3 * WIDTH), low),
        ((ROWS, WIDTH), full),
        ((N_F, SMALL_ROWS, TILE), full),
        ((4, 2, TILE, TILE), low),
    ]
    near = pl.BlockSpec(memory_space=pltpu.VMEM)
    far = pl.BlockSpec(memory_space=pl.ANY)
    return pl.pallas_call(
        layer_kernel,
        out_shape=[
            jax.ShapeDtypeStruct((ROWS, WIDTH), low),
            *[jax.ShapeDtypeStruct((ROWS, columns * WIDTH), low) for columns in (1, 1, 1, 4, 3, 1, 4, 1)],
            jax.ShapeDtypeStruct((4, 2, TILE, TILE), low),
        ],
        in_specs=[near, near, near, far, far, far, far, far],
        out_specs=[near, *[far] * 9],
        scratch_shapes=[
            *[pltpu.VMEM(shape, kind) for shape, kind in scratch],
            pltpu.SemaphoreType.DMA((5,)),
            pltpu.SemaphoreType.DMA((9,)),
            pltpu.SemaphoreType.DMA((4,)),
            pltpu.SemaphoreType.DMA((4,)),
            pltpu.SemaphoreType.DMA((GATHER_COPIES,)),
            pltpu.SemaphoreType.DMA((GATHER_COPIES,)),
        ],
        compiler_params=pltpu.CompilerParams(
            collective_id=2, has_side_effects=True, vmem_limit_bytes=VMEM_CAP
        ),
        name="run_layer",
    )(ends, ids[:, None], ids[None, :], *shards)


def pack_small(biases, gains, bias_in):
    rows = jnp.concatenate([biases, gains, bias_in.reshape(4, TILE)], axis=0)
    return jnp.pad(rows, ((0, 4), (0, TILE)))


def body(ends_in, segment_ids, w_qkv, w_out, w_in, w_down, biases, gains, bias_in):
    shards = (w_qkv[0], w_out[0], w_in[0], w_down[0], pack_small(biases[0], gains[0], bias_in[0]))
    ids = segment_ids + (lax.iota(jnp.int32, ROWS) // SEQ) * 16
    ends_out, *operands = run_layer(ends_in[0], ids, shards)
    outs = widen_outputs(reduce_grads(*operands))
    return tuple(member[None] for member in (ends_out, *outs))


def solution(mesh):
    in_specs = (
        P("section", ("fsdp", "replica"), None),
        P(("fsdp", "replica")),
        P("section", "fsdp", None),
        P("section", "fsdp", None),
        P("section", "fsdp", None),
        P("section", "fsdp", None),
        P("section", None, "fsdp"),
        P("section", None, "fsdp"),
        P("section", "fsdp"),
    )
    out_specs = (
        P("section", ("fsdp", "replica"), None),
        P("section", "fsdp", None),
        P("section", "fsdp", None),
        P("section", "fsdp", None),
        P("section", "fsdp", None),
        P("section", None, "fsdp"),
        P("section", None, "fsdp"),
        P("section", "fsdp"),
    )
    return jax.shard_map(body, mesh=mesh, in_specs=in_specs, out_specs=out_specs, check_vma=False)
```

```python
import jax
import jax.numpy as jnp
from jax import lax
from jax.experimental import pallas as pl
from jax.experimental.pallas import tpu as pltpu
from jax.sharding import PartitionSpec as P

HEADS = 16
HEAD_DIM = 64
SEQ = 64
EPSILON = 1e-05
ROWS = 256
WIDTH = 1024
FF_WIDTH = 4096
STRIP = 32
HALF = 128
FF_STEP = 512


def dot(a, b):
    return jnp.dot(a, b, preferred_element_type=jnp.float32)


def dot_last(a, b):
    return lax.dot_general(a, b, (((1,), (1,)), ((), ())), preferred_element_type=jnp.float32)


def dot_first(a, b):
    return lax.dot_general(a, b, (((0,), (0,)), ((), ())), preferred_element_type=jnp.float32)


MESH = pl.DeviceIdType.MESH
N_F = 8
TILE = 128
SMALL_ROWS = 16
GATHER_COPIES = 112
PAYLOAD = 97 * TILE
VMEM_CAP = 60 * 1024 * 1024

GATHER_PLAN = ((128, 3072, 16), (128, 1024, 16), (128, 4096, 16), (512, 1024, 128), (16, 256, 0))


def place():
    f = lax.axis_index("fsdp")
    r = lax.axis_index("replica")
    return f // 2, lax.rem(f, 2), r // 2, lax.rem(r, 2)


def device(y, c, x, z):
    return {"fsdp": y * 2 + c, "replica": x * 2 + z}


def step_on(index, distance):
    return lax.rem(index + distance + 4, 4)


def greet(peers):
    barrier = pltpu.get_barrier_semaphore()
    for peer in peers:
        pl.semaphore_signal(barrier, inc=1, device_id=peer, device_id_type=MESH)
    pl.semaphore_wait(barrier, len(peers))


class Copies:
    def __init__(self, send_sem, recv_sem):
        self.send_sem, self.recv_sem, self.count, self.unsent = send_sem, recv_sem, 0, []

    def start(self, src, dst, peer):
        copy = pltpu.make_async_remote_copy(
            src_ref=src,
            dst_ref=dst,
            send_sem=self.send_sem.at[self.count],
            recv_sem=self.recv_sem.at[self.count],
            device_id=peer,
            device_id_type=MESH,
        )
        copy.start()
        self.count += 1
        self.unsent.append(copy)
        return copy

    def sent(self, copy):
        copy.wait_send()
        self.unsent = [member for member in self.unsent if member is not copy]

    def finish(self):
        for copy in self.unsent:
            copy.wait_send()


def gather_into(ins, outs, copies, local_sem, others):
    count = len(GATHER_PLAN)
    y, c, x, z = place()
    right_y, left_y = device(step_on(y, 1), c, x, z), device(step_on(y, -1), c, x, z)
    right_x, left_x = device(y, c, step_on(x, 1), z), device(y, c, step_on(x, -1), z)
    sibling = device(y, 1 - c, x, z)
    own = []
    for k in range(count):
        start = pl.multiple_of((y * 2 + c) * GATHER_PLAN[k][0], 16)
        here = outs[k].at[pl.ds(start, GATHER_PLAN[k][0]), :]
        own.append(pltpu.make_async_copy(ins[k], here, local_sem.at[k]))
        own[-1].start()
    greet((right_y, left_y, right_x, left_x, sibling, *others))

    def span(k, owner_y, first, rows, part=None):
        shard_rows, columns, _ = GATHER_PLAN[k]
        start = pl.multiple_of((owner_y * 2 + c) * shard_rows + first, 16)
        if part is None:
            return outs[k].at[pl.ds(start, rows), :]
        half = columns // 2
        return outs[k].at[pl.ds(start, rows), pl.ds(part * half, half)]

    def quarter(k, owner_x):
        return pl.multiple_of(owner_x * GATHER_PLAN[k][2], 16)

    relayed = [k for k in range(count) if GATHER_PLAN[k][2]]
    direct = [k for k in range(count) if GATHER_PLAN[k][0] > 4 * GATHER_PLAN[k][2]]
    first_right, first_left, second_right, second_left = {}, {}, {}, {}
    along_right, along_left, sibling_copies, further = {}, {}, {}, {}
    before, after, across = owners = (step_on(y, -1), step_on(y, 1), step_on(y, 2))

    def extent(kind, k):
        shard_rows, _, piece = GATHER_PLAN[k]
        return (quarter(k, x), piece) if kind == "relay" else (4 * piece, shard_rows - 4 * piece)

    def send_own(kind, k):
        block = span(k, y, *extent(kind, k))
        first_right[kind, k] = copies.start(block, block, right_y)
        first_left[kind, k] = copies.start(block, block, left_y)

    def send_on(kind, k):
        first_right[kind, k].wait_recv()
        block = span(k, before, *extent(kind, k), 0)
        second_right[kind, k] = copies.start(block, block, right_y)
        first_left[kind, k].wait_recv()
        block = span(k, after, *extent(kind, k), 1)
        second_left[kind, k] = copies.start(block, block, left_y)

    def send_along(n, k):
        block = span(k, owners[n], *extent("relay", k))
        along_right[n, k] = copies.start(block, block, right_x)
        along_left[n, k] = copies.start(block, block, left_x)

    def send_further(n, k):
        piece = GATHER_PLAN[k][2]
        along_right[n, k].wait_recv()
        block = span(k, owners[n], quarter(k, step_on(x, -1)), piece, 0)
        further[n, k, 0] = copies.start(block, block, right_x)
        along_left[n, k].wait_recv()
        block = span(k, owners[n], quarter(k, step_on(x, 1)), piece, 1)
        further[n, k, 1] = copies.start(block, block, left_x)

    for k in relayed:
        own[k].wait()
        send_own("relay", k)
    for k in range(count):
        if k not in relayed:
            own[k].wait()
        block = span(k, y, 0, GATHER_PLAN[k][0])
        sibling_copies[3, k] = copies.start(block, block, sibling)
    for k in relayed:
        send_on("relay", k)
        send_along(0, k)
        send_along(1, k)
    for k in direct[::-1]:
        send_own("direct", k)
    for k in relayed:
        second_right["relay", k].wait_recv()
        second_left["relay", k].wait_recv()
        send_along(2, k)
    for n in (0, 1):
        for k in relayed:
            send_further(n, k)
    for k in direct[::-1]:
        send_on("direct", k)
    for k in relayed:
        send_further(2, k)
    def pass_on(n, k):
        if n == 2 and k in direct:
            second_right["direct", k].wait_recv()
            second_left["direct", k].wait_recv()
        if k in relayed:
            further[n, k, 0].wait_recv()
            further[n, k, 1].wait_recv()
        block = span(k, owners[n], 0, GATHER_PLAN[k][0])
        sibling_copies[n, k] = copies.start(block, block, sibling)

    order = (4, 0, 1, 2, 3)
    for n in (0, 1):
        for k in order:
            pass_on(n, k)
    pass_on(2, 4)
    pass_on(2, 0)

    def finish():
        for k in order[2:]:
            pass_on(2, k)

    def arrived(k):
        for n in range(4):
            sibling_copies[n, k].wait_recv()

    return arrived, finish


REDUCE_PLAN = tuple(
    (unit, 1, "yxy"[n % 3]) for n, unit in enumerate((4, 5, 6, 7, 0, 1, 2, 3, 8, 9, 10, 11))
)
UNITS = 12


def chunk_width(plan):
    first, units, _ = plan
    return units * WIDTH + (TILE if first + units == UNITS else 0)


def stage_shape(plan, stage):
    shapes = {("y", 0): (1, 128), ("x", 0): (4, 32), ("y", 1): (1, 32), ("x", 1): (1, 32)}
    blocks, height = shapes[plan[2], stage]
    return blocks, height, chunk_width(plan)


def add_rows(blocks, height, reads, write):
    def one(step, carry):
        block = step // (height // 16)
        row = pl.multiple_of(lax.rem(step, height // 16) * 16, 16)
        total = reads[0](block, row).astype(jnp.float32)
        for read in reads[1:]:
            total = total + read(block, row).astype(jnp.float32)
        write(block, row, total.astype(jnp.bfloat16))
        return carry

    lax.fori_loop(0, blocks * (height // 16), one, 0)


def reduce_kernel(*refs):
    far, out = refs[:9], refs[9]
    near, (staged, held, crossed, gathered) = refs[10:19], refs[19:23]
    stage_refs, (load_sem, store_sem, send_sem, recv_sem) = refs[23:-4], refs[-4:]
    rows_in, context, normed_low, activated, joined, first_low, pre_low, second_low, small = near
    loads = [pltpu.make_async_copy(a, b, load_sem.at[n]) for n, (a, b) in enumerate(zip(far, near))]
    needs = {0: (0, 4), 3: (1, 5), 4: (2, 6), 8: (3, 7), 12: (8,)}
    sources = lambda unit: needs[max(key for key in needs if key <= unit)]
    pending = []
    for first, units, _ in REDUCE_PLAN:
        for unit in (first, first + units - 1):
            pending += [n for n in sources(unit) if n not in pending]
    pending.append(8)
    for n in pending:
        loads[n].start()
    y, c, x, z = place()
    ring = {
        "y": (y, device(step_on(y, 1), c, x, z), device(step_on(y, -1), c, x, z)),
        "x": (x, device(y, c, step_on(x, 1), z), device(y, c, step_on(x, -1), z)),
    }
    sibling = device(y, 1 - c, x, z)
    partner = device(y, c, x, 1 - z)
    greet((ring["y"][1], ring["y"][2], ring["x"][1], ring["x"][2], sibling, partner))
    copies = Copies(send_sem, recv_sem)
    to_sibling, stores = [], []

    def ready(numbers):
        for n in numbers:
            if n in pending:
                loads[n].wait()
                pending.remove(n)

    def produce(n):
        first, units, _ = REDUCE_PLAN[n]
        slot = n % 2
        for unit in range(first, first + units):
            ready(sources(unit))

        def block_rows(at, carry):
            for unit in range(first, min(first + units, 8)):
                if unit < 3:
                    left, right, column = rows_in, joined, unit
                elif unit == 3:
                    left, right, column = context, first_low, 0
                else:
                    left, right, column = normed_low, pre_low, unit - 4
                tile = dot_first(
                    left[:, pl.ds(pl.multiple_of(at * 256, 256), 256)],
                    right[:, column * WIDTH : (column + 1) * WIDTH],
                ).astype(jnp.bfloat16)
                place_at = slice((unit - first) * WIDTH, (unit - first + 1) * WIDTH)
                staged[slot, at, :, :, place_at] = tile.reshape(2, TILE, WIDTH)
            if first >= 8:
                for core in (0, 1):
                    start = at * WIDTH + core * 512 + (first - 8) * TILE
                    rows = activated[:, pl.ds(pl.multiple_of(start, TILE), units * TILE)]
                    tile = dot_first(rows, second_low[...]).astype(jnp.bfloat16)
                    for unit in range(units):
                        place_at = slice(unit * WIDTH, (unit + 1) * WIDTH)
                        staged[slot, at, core, :, place_at] = tile[unit * TILE : (unit + 1) * TILE]
            return carry

        lax.fori_loop(0, 4, block_rows, 0)
        if first + units == UNITS:
            ready((8,))
            for at in range(4):
                for core in (0, 1):
                    staged[slot, at, core, :, units * WIDTH : units * WIDTH + TILE] = small[at, core]

    def along(n, stage):
        first, _, leading = REDUCE_PLAN[n]
        offset, wide_a = first * WIDTH, REDUCE_PLAN[n][1] * WIDTH // 2
        wide_b = chunk_width(REDUCE_PLAN[n]) - wide_a
        start_a, start_b = offset, offset + wide_a
        axis = leading if stage == 0 else ("x" if leading == "y" else "y")
        index, right, left = ring[axis]
        blocks, height, _ = stage_shape(REDUCE_PLAN[n], stage)
        landing = stage_refs[2 * n + stage]

        def origin(at):
            if axis == "y":
                return at, (0 if stage == 0 else x * 32)
            return (0 if stage == 0 else y), at * 32

        def take(at, start, wide):
            block, row = origin(at)
            return held.at[
                pl.ds(block, blocks), pl.ds(pl.multiple_of(row, 16), height), pl.ds(start, wide)
            ]

        def land(slot, start, wide):
            return landing.at[pl.ds(slot * blocks, blocks), :, pl.ds(start - offset, wide)]

        def add(at, start, wide, slots):
            first_block, first_row = origin(at)

            def own(block, row):
                return first_block + block, pl.ds(
                    pl.multiple_of(first_row + row, 16), 16
                ), pl.ds(start, wide)

            def write(block, row, total):
                held[own(block, row)] = total

            def landed(slot):
                return lambda block, row: landing[
                    slot * blocks + block, pl.ds(row, 16), pl.ds(start - offset, wide)
                ]

            reads = [lambda block, row: held[own(block, row)], *[landed(slot) for slot in slots]]
            add_rows(blocks, height, reads, write)

        ahead, behind, across = step_on(index, 1), step_on(index, -1), step_on(index, 2)
        far_right = copies.start(take(across, start_a, wide_a), land(0, start_a, wide_a), right)
        far_left = copies.start(take(across, start_b, wide_b), land(0, start_b, wide_b), left)
        near_copies = [
            copies.start(take(ahead, start_b, wide_b), land(1, start_b, wide_b), right),
            copies.start(take(behind, start_a, wide_a), land(2, start_a, wide_a), left),
        ]
        yield
        far_right.wait_recv()
        add(ahead, start_a, wide_a, (0,))
        near_copies.append(
            copies.start(take(ahead, start_a, wide_a), land(1, start_a, wide_a), right)
        )
        far_left.wait_recv()
        add(behind, start_b, wide_b, (0,))
        near_copies.append(
            copies.start(take(behind, start_b, wide_b), land(2, start_b, wide_b), left)
        )
        yield
        for copy in near_copies:
            copy.wait_recv()
        add(index, start_a, wide_a + wide_b, (1, 2))

    def chunk(n):
        plan = REDUCE_PLAN[n]
        start, wide, slot = plan[0] * WIDTH, chunk_width(plan), n % 2
        wide_a = plan[1] * WIDTH // 2
        columns = pl.ds(start, wide)
        if n >= 2:
            copies.sent(to_sibling[n - 2])
        produce(n)
        to_sibling.append(
            copies.start(
                staged.at[slot, :, 1 - c, :, pl.ds(0, wide)], held.at[:, :, columns], sibling
            )
        )
        yield
        to_sibling[n].wait_recv()

        def write(block, row, total):
            held[block, pl.ds(row, 16), columns] = total

        add_rows(
            4,
            128,
            [
                lambda block, row: held[block, pl.ds(row, 16), columns],
                lambda block, row: staged[slot, block, c, pl.ds(row, 16), pl.ds(0, wide)],
            ],
            write,
        )
        yield from along(n, 0)
        yield from along(n, 1)

        def rows_of(at, first=start, width=wide):
            return gathered.at[pl.ds(pl.multiple_of(at * 32, 16), 32), pl.ds(first, width)]

        swap = copies.start(
            held.at[pl.ds(y, 1), pl.ds(pl.multiple_of(x * 32, 16), 32), columns],
            crossed.at[:, :, columns],
            partner,
        )
        yield
        swap.wait_recv()

        def finish(block, row, total):
            gathered[pl.ds(pl.multiple_of(x * 32 + row, 16), 16), columns] = total

        add_rows(
            1,
            32,
            [
                lambda block, row: held[y, pl.ds(pl.multiple_of(x * 32 + row, 16), 16), columns],
                lambda block, row: crossed[0, pl.ds(row, 16), columns],
            ],
            finish,
        )
        _, right, left = ring["x"]
        to_right = copies.start(rows_of(x), rows_of(x), right)
        to_left = copies.start(rows_of(x), rows_of(x), left)
        yield
        to_right.wait_recv()
        block = rows_of(step_on(x, -1), start, wide_a)
        last = [copies.start(block, block, right)]
        to_left.wait_recv()
        block = rows_of(step_on(x, 1), start + wide_a, wide - wide_a)
        last.append(copies.start(block, block, left))
        yield
        for copy in last:
            copy.wait_recv()
        stores.append(
            pltpu.make_async_copy(gathered.at[:, columns], out.at[:, columns], store_sem.at[n])
        )
        stores[-1].start()

    waiting = [chunk(n) for n in range(len(REDUCE_PLAN))]
    running = []
    while waiting or running:
        if waiting:
            running.append(waiting.pop(0))
        for member in running[::-1]:
            if next(member, "end") == "end":
                running.remove(member)
    for copy in stores:
        copy.wait()
    copies.finish()


def reduce_grads(*operands):
    chunks = len(REDUCE_PLAN)
    widest = max(chunk_width(plan) for plan in REDUCE_PLAN)
    landing = []
    for plan in REDUCE_PLAN:
        for stage in (0, 1):
            blocks, height, width = stage_shape(plan, stage)
            landing.append(pltpu.VMEM((3 * blocks, height, width), jnp.bfloat16))
    far = pl.BlockSpec(memory_space=pl.ANY)
    return pl.pallas_call(
        reduce_kernel,
        out_shape=jax.ShapeDtypeStruct((TILE, PAYLOAD), jnp.bfloat16),
        in_specs=[far] * len(operands),
        out_specs=far,
        scratch_shapes=[
            *[pltpu.VMEM(operand.shape, operand.dtype) for operand in operands],
            pltpu.VMEM((2, 4, 2, TILE, widest), jnp.bfloat16),
            pltpu.VMEM((4, TILE, PAYLOAD), jnp.bfloat16),
            pltpu.VMEM((1, 32, PAYLOAD), jnp.bfloat16),
            pltpu.VMEM((TILE, PAYLOAD), jnp.bfloat16),
            *landing,
            pltpu.SemaphoreType.DMA((len(operands),)),
            pltpu.SemaphoreType.DMA((chunks,)),
            pltpu.SemaphoreType.DMA((chunks * 18,)),
            pltpu.SemaphoreType.DMA((chunks * 18,)),
        ],
        compiler_params=pltpu.CompilerParams(
            collective_id=1, has_side_effects=True, vmem_limit_bytes=VMEM_CAP
        ),
        name="reduce_grads",
    )(*operands)


def widen_kernel(low, qkv, out, into, down, bias, gain, hidden):
    total = low[...].astype(jnp.float32)
    qkv[...] = total[:, :3072]
    out[...] = total[:, 3072:4096]
    into[...] = total[:, 4096:8192]
    for j in range(4):
        down[j] = total[:, 8192 + j * WIDTH : 8192 + (j + 1) * WIDTH]

    @pl.when(pl.program_id(0) == 0)
    def _():
        bias[...] = total[0:6, 12288:]
        gain[...] = total[6:8, 12288:]
        hidden[...] = total[8:12, 12288:]


def widen_outputs(total):
    step = 32
    shapes = [(TILE, 3072), (TILE, WIDTH), (TILE, 4096), (4, TILE, WIDTH), (6, TILE), (2, TILE), (4, TILE)]
    specs = [pl.BlockSpec((step, shape[1]), lambda i: (i, 0)) for shape in shapes[:3]]
    specs.append(pl.BlockSpec((4, step, WIDTH), lambda i: (0, i, 0)))
    specs += [pl.BlockSpec(shape, lambda i: (0, 0)) for shape in shapes[4:]]
    outs = pl.pallas_call(
        widen_kernel,
        grid=(TILE // step,),
        out_shape=[jax.ShapeDtypeStruct(shape, jnp.float32) for shape in shapes],
        in_specs=[pl.BlockSpec((step, PAYLOAD), lambda i: (i, 0))],
        out_specs=specs,
        name="widen_outputs",
    )(total)
    return (*outs[:3], outs[3].reshape(512, WIDTH), outs[4], outs[5], outs[6].reshape(512))


def row_mean(rows):
    return jnp.mean(rows, axis=-1, keepdims=True)


def norm_forward(summed):
    center = summed - row_mean(summed)
    inverse = lax.rsqrt(row_mean(center * center) + EPSILON)
    return center * inverse, inverse


def norm_backward(grad_rows, normed, inverse, gain_row):
    scaled = grad_rows * gain_row
    return inverse * (scaled - row_mean(scaled) - normed * row_mean(scaled * normed))


def strips(body, first):
    def one(n, carry):
        body(pl.ds(pl.multiple_of(first + n * STRIP, STRIP), STRIP))
        return carry

    lax.fori_loop(0, HALF // STRIP, one, 0)


def halves(body):
    def one(n, carry):
        body(n, pl.multiple_of(n * HALF, HALF))
        return carry

    lax.fori_loop(0, 2, one, 0)


def layer_kernel(
    ends,
    id_column,
    id_row,
    w_qkv_shard,
    w_out_shard,
    w_in_shard,
    w_down_shard,
    small_shard,
    ends_out,
    rows_in_far,
    context_far,
    normed_low_far,
    activated_far,
    joined_far,
    first_low_far,
    pre_low_far,
    second_low_far,
    small_far,
    w_qkv,
    w_out,
    w_in,
    w_down,
    small,
    vec,
    sums,
    rows_in,
    cotangent,
    leaving,
    qkv,
    context,
    first_normed,
    first_inverse,
    normed_out,
    normed_low,
    activated,
    slope,
    second_normed,
    second_inverse,
    chances,
    second_low,
    pre_low,
    first_low,
    joined,
    total,
    small_rows,
    small_tile,
    load_sem,
    store_sem,
    send_sem,
    recv_sem,
    gather_send_sem,
    gather_recv_sem,
):
    section = lax.axis_index("section")
    other = {"section": 1 - section}
    copies = Copies(gather_send_sem, gather_recv_sem)
    arrived, finish = gather_into(
        (w_qkv_shard, w_out_shard, w_in_shard, w_down_shard, small_shard),
        (w_qkv, w_out, w_in, w_down, small),
        copies,
        load_sem,
        (other,),
    )
    stores = []

    def store(near, far):
        copy = pltpu.make_async_copy(near, far, store_sem.at[len(stores)])
        copy.start()
        stores.append(copy)

    def passing(first, landing, number):
        rows = pl.ds(first, HALF)
        return pltpu.make_async_remote_copy(
            src_ref=leaving.at[rows, :],
            dst_ref=landing.at[rows, :],
            send_sem=send_sem.at[number],
            recv_sem=recv_sem.at[number],
            device_id=other,
            device_id_type=MESH,
        )

    arrived(4)
    for f in range(N_F):
        shard = small[f * SMALL_ROWS : (f + 1) * SMALL_ROWS, :TILE].astype(jnp.float32)
        vec[0:8, f * TILE : (f + 1) * TILE] = shard[0:8]
        for i in range(4):
            first = (f % 2) * 512 + i * TILE
            vec[8 + f // 2 : 9 + f // 2, first : first + TILE] = shard[8 + i : 9 + i]
    sums[...] = jnp.zeros_like(sums)
    lane = lax.broadcasted_iota(jnp.int32, (1, TILE), 1)
    head_masks = [
        jnp.where((lane < HEAD_DIM) == (h == 0), 1.0, 0.0).astype(jnp.bfloat16) for h in (0, 1)
    ]

    @pl.when(section == 0)
    def _():
        rows_in[...] = ends[...]

    @pl.when(section == 1)
    def _():
        cotangent[...] = ends[...]

    arrived(0)
    def head_columns(p, part):
        return pl.ds(pl.multiple_of(part * WIDTH + p * TILE, TILE), TILE)

    def project(rows):
        for j in range(6):
            columns = slice(j * 512, (j + 1) * 512)
            projected = dot(rows_in[rows, :], w_qkv[:, columns])
            if j // 2 != 1:
                row = 0 if j < 2 else 1
                first = (j % 2) * 512
                projected = projected + vec[row : row + 1, first : first + 512]
            qkv[rows, columns] = projected.astype(jnp.bfloat16)

    def mix(number, rows):
        def attend(p, carry):
            query = qkv[rows, head_columns(p, 0)]
            key = qkv[rows, head_columns(p, 1)]
            value = qkv[rows, head_columns(p, 2)]
            same = id_column[rows, :] == id_row[:, rows]
            mixed = None
            for h in (0, 1):
                scores = dot_last(query * head_masks[h], key) * HEAD_DIM ** (-0.5)
                scores = jnp.where(same, scores, -1e30)
                exponent = jnp.exp(scores - jnp.max(scores, axis=-1, keepdims=True))
                share = exponent / jnp.sum(exponent, axis=-1, keepdims=True)
                low = share.astype(jnp.bfloat16)
                chances[p * 4 + number * 2 + h] = low
                part = dot(low, value * head_masks[h])
                mixed = part if mixed is None else mixed + part
            context[rows, head_columns(p, 0)] = mixed.astype(jnp.bfloat16)
            return carry

        lax.fori_loop(0, HEADS // 2, attend, 0)

    @pl.when(section == 0)
    def _():
        project(slice(0, ROWS))

    finish()

    @pl.when(section == 0)
    def _():
        halves(lambda number, first_row: mix(number, pl.ds(first_row, HALF)))

    for k in (1, 2, 3):
        arrived(k)

    def forward(number, first_row):
        rows = pl.ds(first_row, HALF)

        @pl.when(section == 1)
        def _():
            passing(first_row, rows_in, number).wait_recv()
            project(rows)
            mix(number, rows)

        total[rows, :] = dot(context[rows, :], w_out[...])

        def first_norm(rows):
            summed = rows_in[rows, :].astype(jnp.float32) + total[rows, :] + vec[2:3, :]
            normed, inverse = norm_forward(summed)
            first_normed[rows, :] = normed
            first_inverse[rows, :] = jnp.broadcast_to(inverse, (STRIP, TILE))
            shifted = normed * vec[6:7, :] + vec[3:4, :]
            normed_out[rows, :] = shifted
            normed_low[rows, :] = shifted.astype(jnp.bfloat16)

        strips(first_norm, first_row)

        def widen(j):
            columns = slice(j * FF_STEP, (j + 1) * FF_STEP)
            row, first = j * FF_STEP // WIDTH, j * FF_STEP % WIDTH
            pre_act = dot(normed_low[rows, :], w_in[:, columns])
            pre_act = pre_act + vec[8 + row : 9 + row, first : first + FF_STEP]
            phi = 0.5 * (1.0 + lax.erf(pre_act * 0.7071067811865476))
            activated[rows, columns] = (pre_act * phi).astype(jnp.bfloat16)
            density = jnp.exp(-0.5 * pre_act * pre_act) * 0.3989422804014327
            slope[rows, columns] = (phi + pre_act * density).astype(jnp.bfloat16)

        for j in range(FF_WIDTH // FF_STEP):
            widen(j)
        for n in range(2):
            columns = slice(n * 512, (n + 1) * 512)
            total[rows, columns] = dot(activated[rows, :], w_down[:, columns])


        def second_norm(rows):
            summed = normed_out[rows, :] + total[rows, :] + vec[4:5, :]
            normed, inverse = norm_forward(summed)
            second_normed[rows, :] = normed
            second_inverse[rows, :] = jnp.broadcast_to(inverse, (STRIP, TILE))
            leaving[rows, :] = (normed * vec[7:8, :] + vec[5:6, :]).astype(jnp.bfloat16)

        strips(second_norm, first_row)

        @pl.when(section == 0)
        def _():
            passing(first_row, rows_in, number).start()

        @pl.when(section == 1)
        def _():
            ends_out[rows, :] = leaving[rows, :]

    halves(forward)
    store(rows_in, rows_in_far)
    store(context, context_far)
    store(normed_low, normed_low_far)
    store(activated, activated_far)

    @pl.when(section == 0)
    def _():
        for n in range(2):
            passing(n * HALF, rows_in, n).wait_send()

    def add_sum(row, values):
        sums[row : row + 1, :] += jnp.sum(values, axis=0, keepdims=True)

    def backward(number, first_row):
        rows = pl.ds(first_row, HALF)

        @pl.when(section == 0)
        def _():
            passing(first_row, cotangent, 2 + number).wait_recv()

        def second_back(rows):
            grad = cotangent[rows, :].astype(jnp.float32)
            normed = second_normed[rows, :]
            add_sum(5, grad)
            add_sum(7, grad * normed)
            grad = norm_backward(grad, normed, second_inverse[rows, 0:1], vec[7:8, :])
            add_sum(4, grad)
            normed_out[rows, :] = grad
            second_low[rows, :] = grad.astype(jnp.bfloat16)

        strips(second_back, first_row)
        for j in range(FF_WIDTH // FF_STEP):
            columns = slice(j * FF_STEP, (j + 1) * FF_STEP)
            row, first = j * FF_STEP // WIDTH, j * FF_STEP % WIDTH
            grad = dot_last(second_low[rows, :], w_down[columns, :]) * slope[rows, columns].astype(jnp.float32)
            sums[8 + row : 9 + row, first : first + FF_STEP] += jnp.sum(grad, axis=0, keepdims=True)
            pre_low[rows, columns] = grad.astype(jnp.bfloat16)
        for n in range(2):
            columns = slice(n * 512, (n + 1) * 512)
            total[rows, columns] = dot_last(pre_low[rows, :], w_in[columns, :])


        def first_back(rows):
            grad = normed_out[rows, :] + total[rows, :]
            normed = first_normed[rows, :]
            add_sum(3, grad)
            add_sum(6, grad * normed)
            grad = norm_backward(grad, normed, first_inverse[rows, 0:1], vec[6:7, :])
            add_sum(2, grad)
            normed_out[rows, :] = grad
            first_low[rows, :] = grad.astype(jnp.bfloat16)

        strips(first_back, first_row)
        context_grad = leaving
        for n in range(2):
            columns = slice(n * 512, (n + 1) * 512)
            context_grad[rows, columns] = dot_last(first_low[rows, :], w_out[columns, :]).astype(jnp.bfloat16)

        def attend_back(p, carry):
            query = qkv[rows, head_columns(p, 0)]
            key = qkv[rows, head_columns(p, 1)]
            value = qkv[rows, head_columns(p, 2)]
            grads = context_grad[rows, head_columns(p, 0)]
            results = [0.0, 0.0, 0.0]
            for h in (0, 1):
                own = grads * head_masks[h]
                low = chances[p * 4 + number * 2 + h]
                share = low.astype(jnp.float32)
                weight_grad = dot_last(own, value)
                inner = jnp.sum(share * weight_grad, axis=-1, keepdims=True)
                score = (share * (weight_grad - inner) * HEAD_DIM ** (-0.5)).astype(jnp.bfloat16)
                results[0] += dot(score, key * head_masks[h])
                results[1] += dot_first(score, query * head_masks[h])
                results[2] += dot_first(low, own)
            for part in range(3):
                joined[rows, head_columns(p, part)] = results[part].astype(jnp.bfloat16)
            for row, part in ((0, 0), (1, 2)):
                here = head_columns(p, 0)
                sums[row : row + 1, here] += jnp.sum(results[part], axis=0, keepdims=True)
            return carry

        lax.fori_loop(0, HEADS // 2, attend_back, 0)
        for n in range(2):
            columns = slice(n * 512, (n + 1) * 512)
            grad = normed_out[rows, columns] + dot_last(joined[rows, :], w_qkv[columns, :])
            leaving[rows, columns] = grad.astype(jnp.bfloat16)

        @pl.when(section == 1)
        def _():
            passing(first_row, cotangent, 2 + number).start()

        @pl.when(section == 0)
        def _():
            ends_out[rows, :] = leaving[rows, :]

    halves(backward)
    store(joined, joined_far)
    store(first_low, first_low_far)
    store(pre_low, pre_low_far)
    store(second_low, second_low_far)
    for f in range(N_F):
        small_rows[f, 0:8, :] = sums[0:8, f * TILE : (f + 1) * TILE]
        for i in range(4):
            first = (f % 2) * 512 + i * TILE
            small_rows[f, 8 + i : 9 + i, :] = sums[8 + f // 2 : 9 + f // 2, first : first + TILE]
        small_rows[f, 12:16, :] = jnp.zeros((4, TILE), jnp.float32)
    small_tile[...] = jnp.zeros_like(small_tile)
    for f in range(N_F):
        small_tile[f // 2, f % 2, 0:16, :] = small_rows[f].astype(jnp.bfloat16)
    store(small_tile, small_far)
    for copy in stores:
        copy.wait()
    copies.finish()

    @pl.when(section == 1)
    def _():
        for n in range(2):
            passing(n * HALF, cotangent, 2 + n).wait_send()


def run_layer(ends, ids, shards):
    low, full = jnp.bfloat16, jnp.float32
    scratch = [
        ((1024, 3072), low),
        ((1024, 1024), low),
        ((1024, 4096), low),
        ((4096, 1024), low),
        ((N_F * SMALL_ROWS, 2 * TILE), low),
        ((16, WIDTH), full),
        ((16, WIDTH), full),
        ((ROWS, WIDTH), low),
        ((ROWS, WIDTH), low),
        ((ROWS, WIDTH), low),
        ((ROWS, 3 * WIDTH), low),
        ((ROWS, WIDTH), low),
        ((ROWS, WIDTH), full),
        ((ROWS, TILE), full),
        ((ROWS, WIDTH), full),
        ((ROWS, WIDTH), low),
        ((ROWS, FF_WIDTH), low),
        ((ROWS, FF_WIDTH), low),
        ((ROWS, WIDTH), full),
        ((ROWS, TILE), full),
        ((2 * HEADS, TILE, TILE), low),
        ((ROWS, WIDTH), low),
        ((ROWS, FF_WIDTH), low),
        ((ROWS, WIDTH), low),
        ((ROWS, 3 * WIDTH), low),
        ((ROWS, WIDTH), full),
        ((N_F, SMALL_ROWS, TILE), full),
        ((4, 2, TILE, TILE), low),
    ]
    near = pl.BlockSpec(memory_space=pltpu.VMEM)
    far = pl.BlockSpec(memory_space=pl.ANY)
    return pl.pallas_call(
        layer_kernel,
        out_shape=[
            jax.ShapeDtypeStruct((ROWS, WIDTH), low),
            *[jax.ShapeDtypeStruct((ROWS, columns * WIDTH), low) for columns in (1, 1, 1, 4, 3, 1, 4, 1)],
            jax.ShapeDtypeStruct((4, 2, TILE, TILE), low),
        ],
        in_specs=[near, near, near, far, far, far, far, far],
        out_specs=[near, *[far] * 9],
        scratch_shapes=[
            *[pltpu.VMEM(shape, kind) for shape, kind in scratch],
            pltpu.SemaphoreType.DMA((5,)),
            pltpu.SemaphoreType.DMA((9,)),
            pltpu.SemaphoreType.DMA((4,)),
            pltpu.SemaphoreType.DMA((4,)),
            pltpu.SemaphoreType.DMA((GATHER_COPIES,)),
            pltpu.SemaphoreType.DMA((GATHER_COPIES,)),
        ],
        compiler_params=pltpu.CompilerParams(
            collective_id=2, has_side_effects=True, vmem_limit_bytes=VMEM_CAP
        ),
        name="run_layer",
    )(ends, ids[:, None], ids[None, :], *shards)


def pack_small(biases, gains, bias_in):
    rows = jnp.concatenate([biases, gains, bias_in.reshape(4, TILE)], axis=0)
    return jnp.pad(rows, ((0, 4), (0, TILE)))


def body(ends_in, segment_ids, w_qkv, w_out, w_in, w_down, biases, gains, bias_in):
    shards = (w_qkv[0], w_out[0], w_in[0], w_down[0], pack_small(biases[0], gains[0], bias_in[0]))
    ids = segment_ids + (lax.iota(jnp.int32, ROWS) // SEQ) * 16
    ends_out, *operands = run_layer(ends_in[0], ids, shards)
    outs = widen_outputs(reduce_grads(*operands))
    return tuple(member[None] for member in (ends_out, *outs))


def solution(mesh):
    in_specs = (
        P("section", ("fsdp", "replica"), None),
        P(("fsdp", "replica")),
        P("section", "fsdp", None),
        P("section", "fsdp", None),
        P("section", "fsdp", None),
        P("section", "fsdp", None),
        P("section", None, "fsdp"),
        P("section", None, "fsdp"),
        P("section", "fsdp"),
    )
    out_specs = (
        P("section", ("fsdp", "replica"), None),
        P("section", "fsdp", None),
        P("section", "fsdp", None),
        P("section", "fsdp", None),
        P("section", "fsdp", None),
        P("section", None, "fsdp"),
        P("section", None, "fsdp"),
        P("section", "fsdp"),
    )
    return jax.shard_map(body, mesh=mesh, in_specs=in_specs, out_specs=out_specs, check_vma=False)
```

```python
import jax
import jax.numpy as jnp
from jax import lax
from jax.experimental import pallas as pl
from jax.experimental.pallas import tpu as pltpu
from jax.sharding import PartitionSpec as P

HEADS = 16
HEAD_DIM = 64
SEQ = 64
EPSILON = 1e-05
ROWS = 256
WIDTH = 1024
FF_WIDTH = 4096
STRIP = 32
HALF = 128
FF_STEP = 512


def dot(a, b):
    return jnp.dot(a, b, preferred_element_type=jnp.float32)


def dot_last(a, b):
    return lax.dot_general(a, b, (((1,), (1,)), ((), ())), preferred_element_type=jnp.float32)


def dot_first(a, b):
    return lax.dot_general(a, b, (((0,), (0,)), ((), ())), preferred_element_type=jnp.float32)


MESH = pl.DeviceIdType.MESH
N_F = 8
TILE = 128
SMALL_ROWS = 16
GATHER_COPIES = 112
PAYLOAD = 97 * TILE
VMEM_CAP = 60 * 1024 * 1024

GATHER_PLAN = ((128, 3072, 16), (128, 1024, 16), (128, 4096, 16), (512, 1024, 128), (16, 256, 0))


def place():
    f = lax.axis_index("fsdp")
    r = lax.axis_index("replica")
    return f // 2, lax.rem(f, 2), r // 2, lax.rem(r, 2)


def device(y, c, x, z):
    return {"fsdp": y * 2 + c, "replica": x * 2 + z}


def step_on(index, distance):
    return lax.rem(index + distance + 4, 4)


def greet(peers):
    barrier = pltpu.get_barrier_semaphore()
    for peer in peers:
        pl.semaphore_signal(barrier, inc=1, device_id=peer, device_id_type=MESH)
    pl.semaphore_wait(barrier, len(peers))


class Copies:
    def __init__(self, send_sem, recv_sem):
        self.send_sem, self.recv_sem, self.count, self.unsent = send_sem, recv_sem, 0, []

    def start(self, src, dst, peer):
        copy = pltpu.make_async_remote_copy(
            src_ref=src,
            dst_ref=dst,
            send_sem=self.send_sem.at[self.count],
            recv_sem=self.recv_sem.at[self.count],
            device_id=peer,
            device_id_type=MESH,
        )
        copy.start()
        self.count += 1
        self.unsent.append(copy)
        return copy

    def sent(self, copy):
        copy.wait_send()
        self.unsent = [member for member in self.unsent if member is not copy]

    def finish(self):
        for copy in self.unsent:
            copy.wait_send()


def gather_into(ins, outs, copies, local_sem, others):
    count = len(GATHER_PLAN)
    y, c, x, z = place()
    right_y, left_y = device(step_on(y, 1), c, x, z), device(step_on(y, -1), c, x, z)
    right_x, left_x = device(y, c, step_on(x, 1), z), device(y, c, step_on(x, -1), z)
    sibling = device(y, 1 - c, x, z)
    own = []
    for k in range(count):
        start = pl.multiple_of((y * 2 + c) * GATHER_PLAN[k][0], 16)
        here = outs[k].at[pl.ds(start, GATHER_PLAN[k][0]), :]
        own.append(pltpu.make_async_copy(ins[k], here, local_sem.at[k]))
        own[-1].start()
    greet((right_y, left_y, right_x, left_x, sibling, *others))

    def span(k, owner_y, first, rows, part=None):
        shard_rows, columns, _ = GATHER_PLAN[k]
        start = pl.multiple_of((owner_y * 2 + c) * shard_rows + first, 16)
        if part is None:
            return outs[k].at[pl.ds(start, rows), :]
        half = columns // 2
        return outs[k].at[pl.ds(start, rows), pl.ds(part * half, half)]

    def quarter(k, owner_x):
        return pl.multiple_of(owner_x * GATHER_PLAN[k][2], 16)

    relayed = [k for k in range(count) if GATHER_PLAN[k][2]]
    direct = [k for k in range(count) if GATHER_PLAN[k][0] > 4 * GATHER_PLAN[k][2]]
    first_right, first_left, second_right, second_left = {}, {}, {}, {}
    along_right, along_left, sibling_copies, further = {}, {}, {}, {}
    before, after, across = owners = (step_on(y, -1), step_on(y, 1), step_on(y, 2))

    def extent(kind, k):
        shard_rows, _, piece = GATHER_PLAN[k]
        return (quarter(k, x), piece) if kind == "relay" else (4 * piece, shard_rows - 4 * piece)

    def send_own(kind, k):
        block = span(k, y, *extent(kind, k))
        first_right[kind, k] = copies.start(block, block, right_y)
        first_left[kind, k] = copies.start(block, block, left_y)

    def send_on(kind, k):
        first_right[kind, k].wait_recv()
        block = span(k, before, *extent(kind, k), 0)
        second_right[kind, k] = copies.start(block, block, right_y)
        first_left[kind, k].wait_recv()
        block = span(k, after, *extent(kind, k), 1)
        second_left[kind, k] = copies.start(block, block, left_y)

    def send_along(n, k):
        block = span(k, owners[n], *extent("relay", k))
        along_right[n, k] = copies.start(block, block, right_x)
        along_left[n, k] = copies.start(block, block, left_x)

    def send_further(n, k):
        piece = GATHER_PLAN[k][2]
        along_right[n, k].wait_recv()
        block = span(k, owners[n], quarter(k, step_on(x, -1)), piece, 0)
        further[n, k, 0] = copies.start(block, block, right_x)
        along_left[n, k].wait_recv()
        block = span(k, owners[n], quarter(k, step_on(x, 1)), piece, 1)
        further[n, k, 1] = copies.start(block, block, left_x)

    for k in relayed:
        own[k].wait()
        send_own("relay", k)
    for k in range(count):
        if k not in relayed:
            own[k].wait()
        block = span(k, y, 0, GATHER_PLAN[k][0])
        sibling_copies[3, k] = copies.start(block, block, sibling)
    for k in relayed:
        send_on("relay", k)
        send_along(0, k)
        send_along(1, k)
    for k in (4, 0, 1, 2):
        send_own("direct", k)
    for k in relayed:
        second_right["relay", k].wait_recv()
        second_left["relay", k].wait_recv()
        send_along(2, k)
    for n in (0, 1):
        for k in relayed:
            send_further(n, k)
    for k in (4, 0, 1, 2):
        send_on("direct", k)
    for k in relayed:
        send_further(2, k)
    def pass_on(n, k):
        if n == 2 and k in direct:
            second_right["direct", k].wait_recv()
            second_left["direct", k].wait_recv()
        if k in relayed:
            further[n, k, 0].wait_recv()
            further[n, k, 1].wait_recv()
        block = span(k, owners[n], 0, GATHER_PLAN[k][0])
        sibling_copies[n, k] = copies.start(block, block, sibling)

    order = (4, 0, 1, 2, 3)
    for n in (0, 1):
        for k in order:
            pass_on(n, k)
    pass_on(2, 4)
    pass_on(2, 0)

    def finish():
        for k in order[2:]:
            pass_on(2, k)

    def arrived(k):
        for n in range(4):
            sibling_copies[n, k].wait_recv()

    return arrived, finish


REDUCE_PLAN = tuple(
    (unit, 1, "yxy"[n % 3]) for n, unit in enumerate((4, 5, 6, 7, 0, 1, 2, 3, 8, 9, 10, 11))
)
UNITS = 12


def chunk_width(plan):
    first, units, _ = plan
    return units * WIDTH + (TILE if first + units == UNITS else 0)


def stage_shape(plan, stage):
    shapes = {("y", 0): (1, 128), ("x", 0): (4, 32), ("y", 1): (1, 32), ("x", 1): (1, 32)}
    blocks, height = shapes[plan[2], stage]
    return blocks, height, chunk_width(plan)


def add_rows(blocks, height, reads, write):
    def one(step, carry):
        block = step // (height // 16)
        row = pl.multiple_of(lax.rem(step, height // 16) * 16, 16)
        total = reads[0](block, row).astype(jnp.float32)
        for read in reads[1:]:
            total = total + read(block, row).astype(jnp.float32)
        write(block, row, total.astype(jnp.bfloat16))
        return carry

    lax.fori_loop(0, blocks * (height // 16), one, 0)


def reduce_kernel(*refs):
    far, out = refs[:9], refs[9]
    near, (staged, held, crossed, gathered) = refs[10:19], refs[19:23]
    stage_refs, (load_sem, store_sem, send_sem, recv_sem) = refs[23:-4], refs[-4:]
    rows_in, context, normed_low, activated, joined, first_low, pre_low, second_low, small = near
    loads = [pltpu.make_async_copy(a, b, load_sem.at[n]) for n, (a, b) in enumerate(zip(far, near))]
    needs = {0: (0, 4), 3: (1, 5), 4: (2, 6), 8: (3, 7), 12: (8,)}
    sources = lambda unit: needs[max(key for key in needs if key <= unit)]
    pending = []
    for first, units, _ in REDUCE_PLAN:
        for unit in (first, first + units - 1):
            pending += [n for n in sources(unit) if n not in pending]
    pending.append(8)
    for n in pending:
        loads[n].start()
    y, c, x, z = place()
    ring = {
        "y": (y, device(step_on(y, 1), c, x, z), device(step_on(y, -1), c, x, z)),
        "x": (x, device(y, c, step_on(x, 1), z), device(y, c, step_on(x, -1), z)),
    }
    sibling = device(y, 1 - c, x, z)
    partner = device(y, c, x, 1 - z)
    greet((ring["y"][1], ring["y"][2], ring["x"][1], ring["x"][2], sibling, partner))
    copies = Copies(send_sem, recv_sem)
    to_sibling, stores = [], []

    def ready(numbers):
        for n in numbers:
            if n in pending:
                loads[n].wait()
                pending.remove(n)

    def produce(n):
        first, units, _ = REDUCE_PLAN[n]
        slot = n % 2
        for unit in range(first, first + units):
            ready(sources(unit))

        def block_rows(at, carry):
            for unit in range(first, min(first + units, 8)):
                if unit < 3:
                    left, right, column = rows_in, joined, unit
                elif unit == 3:
                    left, right, column = context, first_low, 0
                else:
                    left, right, column = normed_low, pre_low, unit - 4
                tile = dot_first(
                    left[:, pl.ds(pl.multiple_of(at * 256, 256), 256)],
                    right[:, column * WIDTH : (column + 1) * WIDTH],
                ).astype(jnp.bfloat16)
                place_at = slice((unit - first) * WIDTH, (unit - first + 1) * WIDTH)
                staged[slot, at, :, :, place_at] = tile.reshape(2, TILE, WIDTH)
            if first >= 8:
                for core in (0, 1):
                    start = at * WIDTH + core * 512 + (first - 8) * TILE
                    rows = activated[:, pl.ds(pl.multiple_of(start, TILE), units * TILE)]
                    tile = dot_first(rows, second_low[...]).astype(jnp.bfloat16)
                    for unit in range(units):
                        place_at = slice(unit * WIDTH, (unit + 1) * WIDTH)
                        staged[slot, at, core, :, place_at] = tile[unit * TILE : (unit + 1) * TILE]
            return carry

        lax.fori_loop(0, 4, block_rows, 0)
        if first + units == UNITS:
            ready((8,))
            for at in range(4):
                for core in (0, 1):
                    staged[slot, at, core, :, units * WIDTH : units * WIDTH + TILE] = small[at, core]

    def along(n, stage):
        first, _, leading = REDUCE_PLAN[n]
        offset, wide_a = first * WIDTH, REDUCE_PLAN[n][1] * WIDTH // 2
        wide_b = chunk_width(REDUCE_PLAN[n]) - wide_a
        start_a, start_b = offset, offset + wide_a
        axis = leading if stage == 0 else ("x" if leading == "y" else "y")
        index, right, left = ring[axis]
        blocks, height, _ = stage_shape(REDUCE_PLAN[n], stage)
        landing = stage_refs[2 * n + stage]

        def origin(at):
            if axis == "y":
                return at, (0 if stage == 0 else x * 32)
            return (0 if stage == 0 else y), at * 32

        def take(at, start, wide):
            block, row = origin(at)
            return held.at[
                pl.ds(block, blocks), pl.ds(pl.multiple_of(row, 16), height), pl.ds(start, wide)
            ]

        def land(slot, start, wide):
            return landing.at[pl.ds(slot * blocks, blocks), :, pl.ds(start - offset, wide)]

        def add(at, start, wide, slots):
            first_block, first_row = origin(at)

            def own(block, row):
                return first_block + block, pl.ds(
                    pl.multiple_of(first_row + row, 16), 16
                ), pl.ds(start, wide)

            def write(block, row, total):
                held[own(block, row)] = total

            def landed(slot):
                return lambda block, row: landing[
                    slot * blocks + block, pl.ds(row, 16), pl.ds(start - offset, wide)
                ]

            reads = [lambda block, row: held[own(block, row)], *[landed(slot) for slot in slots]]
            add_rows(blocks, height, reads, write)

        ahead, behind, across = step_on(index, 1), step_on(index, -1), step_on(index, 2)
        far_right = copies.start(take(across, start_a, wide_a), land(0, start_a, wide_a), right)
        far_left = copies.start(take(across, start_b, wide_b), land(0, start_b, wide_b), left)
        near_copies = [
            copies.start(take(ahead, start_b, wide_b), land(1, start_b, wide_b), right),
            copies.start(take(behind, start_a, wide_a), land(2, start_a, wide_a), left),
        ]
        yield
        far_right.wait_recv()
        add(ahead, start_a, wide_a, (0,))
        near_copies.append(
            copies.start(take(ahead, start_a, wide_a), land(1, start_a, wide_a), right)
        )
        far_left.wait_recv()
        add(behind, start_b, wide_b, (0,))
        near_copies.append(
            copies.start(take(behind, start_b, wide_b), land(2, start_b, wide_b), left)
        )
        yield
        for copy in near_copies:
            copy.wait_recv()
        add(index, start_a, wide_a + wide_b, (1, 2))

    def chunk(n):
        plan = REDUCE_PLAN[n]
        start, wide, slot = plan[0] * WIDTH, chunk_width(plan), n % 2
        wide_a = plan[1] * WIDTH // 2
        columns = pl.ds(start, wide)
        if n >= 2:
            copies.sent(to_sibling[n - 2])
        produce(n)
        to_sibling.append(
            copies.start(
                staged.at[slot, :, 1 - c, :, pl.ds(0, wide)], held.at[:, :, columns], sibling
            )
        )
        yield
        to_sibling[n].wait_recv()

        def write(block, row, total):
            held[block, pl.ds(row, 16), columns] = total

        add_rows(
            4,
            128,
            [
                lambda block, row: held[block, pl.ds(row, 16), columns],
                lambda block, row: staged[slot, block, c, pl.ds(row, 16), pl.ds(0, wide)],
            ],
            write,
        )
        yield from along(n, 0)
        yield from along(n, 1)

        def rows_of(at, first=start, width=wide):
            return gathered.at[pl.ds(pl.multiple_of(at * 32, 16), 32), pl.ds(first, width)]

        swap = copies.start(
            held.at[pl.ds(y, 1), pl.ds(pl.multiple_of(x * 32, 16), 32), columns],
            crossed.at[:, :, columns],
            partner,
        )
        yield
        swap.wait_recv()

        def finish(block, row, total):
            gathered[pl.ds(pl.multiple_of(x * 32 + row, 16), 16), columns] = total

        add_rows(
            1,
            32,
            [
                lambda block, row: held[y, pl.ds(pl.multiple_of(x * 32 + row, 16), 16), columns],
                lambda block, row: crossed[0, pl.ds(row, 16), columns],
            ],
            finish,
        )
        _, right, left = ring["x"]
        to_right = copies.start(rows_of(x), rows_of(x), right)
        to_left = copies.start(rows_of(x), rows_of(x), left)
        yield
        to_right.wait_recv()
        block = rows_of(step_on(x, -1), start, wide_a)
        last = [copies.start(block, block, right)]
        to_left.wait_recv()
        block = rows_of(step_on(x, 1), start + wide_a, wide - wide_a)
        last.append(copies.start(block, block, left))
        yield
        for copy in last:
            copy.wait_recv()
        stores.append(
            pltpu.make_async_copy(gathered.at[:, columns], out.at[:, columns], store_sem.at[n])
        )
        stores[-1].start()

    waiting = [chunk(n) for n in range(len(REDUCE_PLAN))]
    running = []
    while waiting or running:
        if waiting:
            running.append(waiting.pop(0))
        for member in running[::-1]:
            if next(member, "end") == "end":
                running.remove(member)
    for copy in stores:
        copy.wait()
    copies.finish()


def reduce_grads(*operands):
    chunks = len(REDUCE_PLAN)
    widest = max(chunk_width(plan) for plan in REDUCE_PLAN)
    landing = []
    for plan in REDUCE_PLAN:
        for stage in (0, 1):
            blocks, height, width = stage_shape(plan, stage)
            landing.append(pltpu.VMEM((3 * blocks, height, width), jnp.bfloat16))
    far = pl.BlockSpec(memory_space=pl.ANY)
    return pl.pallas_call(
        reduce_kernel,
        out_shape=jax.ShapeDtypeStruct((TILE, PAYLOAD), jnp.bfloat16),
        in_specs=[far] * len(operands),
        out_specs=far,
        scratch_shapes=[
            *[pltpu.VMEM(operand.shape, operand.dtype) for operand in operands],
            pltpu.VMEM((2, 4, 2, TILE, widest), jnp.bfloat16),
            pltpu.VMEM((4, TILE, PAYLOAD), jnp.bfloat16),
            pltpu.VMEM((1, 32, PAYLOAD), jnp.bfloat16),
            pltpu.VMEM((TILE, PAYLOAD), jnp.bfloat16),
            *landing,
            pltpu.SemaphoreType.DMA((len(operands),)),
            pltpu.SemaphoreType.DMA((chunks,)),
            pltpu.SemaphoreType.DMA((chunks * 18,)),
            pltpu.SemaphoreType.DMA((chunks * 18,)),
        ],
        compiler_params=pltpu.CompilerParams(
            collective_id=1, has_side_effects=True, vmem_limit_bytes=VMEM_CAP
        ),
        name="reduce_grads",
    )(*operands)


def widen_kernel(low, qkv, out, into, down, bias, gain, hidden):
    total = low[...].astype(jnp.float32)
    qkv[...] = total[:, :3072]
    out[...] = total[:, 3072:4096]
    into[...] = total[:, 4096:8192]
    for j in range(4):
        down[j] = total[:, 8192 + j * WIDTH : 8192 + (j + 1) * WIDTH]

    @pl.when(pl.program_id(0) == 0)
    def _():
        bias[...] = total[0:6, 12288:]
        gain[...] = total[6:8, 12288:]
        hidden[...] = total[8:12, 12288:]


def widen_outputs(total):
    step = 32
    shapes = [(TILE, 3072), (TILE, WIDTH), (TILE, 4096), (4, TILE, WIDTH), (6, TILE), (2, TILE), (4, TILE)]
    specs = [pl.BlockSpec((step, shape[1]), lambda i: (i, 0)) for shape in shapes[:3]]
    specs.append(pl.BlockSpec((4, step, WIDTH), lambda i: (0, i, 0)))
    specs += [pl.BlockSpec(shape, lambda i: (0, 0)) for shape in shapes[4:]]
    outs = pl.pallas_call(
        widen_kernel,
        grid=(TILE // step,),
        out_shape=[jax.ShapeDtypeStruct(shape, jnp.float32) for shape in shapes],
        in_specs=[pl.BlockSpec((step, PAYLOAD), lambda i: (i, 0))],
        out_specs=specs,
        name="widen_outputs",
    )(total)
    return (*outs[:3], outs[3].reshape(512, WIDTH), outs[4], outs[5], outs[6].reshape(512))


def row_mean(rows):
    return jnp.mean(rows, axis=-1, keepdims=True)


def norm_forward(summed):
    center = summed - row_mean(summed)
    inverse = lax.rsqrt(row_mean(center * center) + EPSILON)
    return center * inverse, inverse


def norm_backward(grad_rows, normed, inverse, gain_row):
    scaled = grad_rows * gain_row
    return inverse * (scaled - row_mean(scaled) - normed * row_mean(scaled * normed))


def strips(body, first):
    def one(n, carry):
        body(pl.ds(pl.multiple_of(first + n * STRIP, STRIP), STRIP))
        return carry

    lax.fori_loop(0, HALF // STRIP, one, 0)


def halves(body):
    def one(n, carry):
        body(n, pl.multiple_of(n * HALF, HALF))
        return carry

    lax.fori_loop(0, 2, one, 0)


def layer_kernel(
    ends,
    id_column,
    id_row,
    w_qkv_shard,
    w_out_shard,
    w_in_shard,
    w_down_shard,
    small_shard,
    ends_out,
    rows_in_far,
    context_far,
    normed_low_far,
    activated_far,
    joined_far,
    first_low_far,
    pre_low_far,
    second_low_far,
    small_far,
    w_qkv,
    w_out,
    w_in,
    w_down,
    small,
    vec,
    sums,
    rows_in,
    cotangent,
    leaving,
    qkv,
    context,
    first_normed,
    first_inverse,
    normed_out,
    normed_low,
    activated,
    slope,
    second_normed,
    second_inverse,
    chances,
    second_low,
    pre_low,
    first_low,
    joined,
    total,
    small_rows,
    small_tile,
    load_sem,
    store_sem,
    send_sem,
    recv_sem,
    gather_send_sem,
    gather_recv_sem,
):
    section = lax.axis_index("section")
    other = {"section": 1 - section}
    copies = Copies(gather_send_sem, gather_recv_sem)
    arrived, finish = gather_into(
        (w_qkv_shard, w_out_shard, w_in_shard, w_down_shard, small_shard),
        (w_qkv, w_out, w_in, w_down, small),
        copies,
        load_sem,
        (other,),
    )
    stores = []

    def store(near, far):
        copy = pltpu.make_async_copy(near, far, store_sem.at[len(stores)])
        copy.start()
        stores.append(copy)

    def passing(first, landing, number):
        rows = pl.ds(first, HALF)
        return pltpu.make_async_remote_copy(
            src_ref=leaving.at[rows, :],
            dst_ref=landing.at[rows, :],
            send_sem=send_sem.at[number],
            recv_sem=recv_sem.at[number],
            device_id=other,
            device_id_type=MESH,
        )

    arrived(4)
    for f in range(N_F):
        shard = small[f * SMALL_ROWS : (f + 1) * SMALL_ROWS, :TILE].astype(jnp.float32)
        vec[0:8, f * TILE : (f + 1) * TILE] = shard[0:8]
        for i in range(4):
            first = (f % 2) * 512 + i * TILE
            vec[8 + f // 2 : 9 + f // 2, first : first + TILE] = shard[8 + i : 9 + i]
    sums[...] = jnp.zeros_like(sums)
    lane = lax.broadcasted_iota(jnp.int32, (1, TILE), 1)
    head_masks = [
        jnp.where((lane < HEAD_DIM) == (h == 0), 1.0, 0.0).astype(jnp.bfloat16) for h in (0, 1)
    ]

    @pl.when(section == 0)
    def _():
        rows_in[...] = ends[...]

    @pl.when(section == 1)
    def _():
        cotangent[...] = ends[...]

    arrived(0)
    def head_columns(p, part):
        return pl.ds(pl.multiple_of(part * WIDTH + p * TILE, TILE), TILE)

    def project(rows):
        for j in range(6):
            columns = slice(j * 512, (j + 1) * 512)
            projected = dot(rows_in[rows, :], w_qkv[:, columns])
            if j // 2 != 1:
                row = 0 if j < 2 else 1
                first = (j % 2) * 512
                projected = projected + vec[row : row + 1, first : first + 512]
            qkv[rows, columns] = projected.astype(jnp.bfloat16)

    def mix(number, rows):
        def attend(p, carry):
            query = qkv[rows, head_columns(p, 0)]
            key = qkv[rows, head_columns(p, 1)]
            value = qkv[rows, head_columns(p, 2)]
            same = id_column[rows, :] == id_row[:, rows]
            mixed = None
            for h in (0, 1):
                scores = dot_last(query * head_masks[h], key) * HEAD_DIM ** (-0.5)
                scores = jnp.where(same, scores, -1e30)
                exponent = jnp.exp(scores - jnp.max(scores, axis=-1, keepdims=True))
                share = exponent / jnp.sum(exponent, axis=-1, keepdims=True)
                low = share.astype(jnp.bfloat16)
                chances[p * 4 + number * 2 + h] = low
                part = dot(low, value * head_masks[h])
                mixed = part if mixed is None else mixed + part
            context[rows, head_columns(p, 0)] = mixed.astype(jnp.bfloat16)
            return carry

        lax.fori_loop(0, HEADS // 2, attend, 0)

    @pl.when(section == 0)
    def _():
        project(slice(0, ROWS))

    finish()

    @pl.when(section == 0)
    def _():
        halves(lambda number, first_row: mix(number, pl.ds(first_row, HALF)))

    for k in (1, 2, 3):
        arrived(k)

    def forward(number, first_row):
        rows = pl.ds(first_row, HALF)

        @pl.when(section == 1)
        def _():
            passing(first_row, rows_in, number).wait_recv()
            project(rows)
            mix(number, rows)

        total[rows, :] = dot(context[rows, :], w_out[...])

        def first_norm(rows):
            summed = rows_in[rows, :].astype(jnp.float32) + total[rows, :] + vec[2:3, :]
            normed, inverse = norm_forward(summed)
            first_normed[rows, :] = normed
            first_inverse[rows, :] = jnp.broadcast_to(inverse, (STRIP, TILE))
            shifted = normed * vec[6:7, :] + vec[3:4, :]
            normed_out[rows, :] = shifted
            normed_low[rows, :] = shifted.astype(jnp.bfloat16)

        strips(first_norm, first_row)

        def widen(j):
            columns = slice(j * FF_STEP, (j + 1) * FF_STEP)
            row, first = j * FF_STEP // WIDTH, j * FF_STEP % WIDTH
            pre_act = dot(normed_low[rows, :], w_in[:, columns])
            pre_act = pre_act + vec[8 + row : 9 + row, first : first + FF_STEP]
            phi = 0.5 * (1.0 + lax.erf(pre_act * 0.7071067811865476))
            activated[rows, columns] = (pre_act * phi).astype(jnp.bfloat16)
            density = jnp.exp(-0.5 * pre_act * pre_act) * 0.3989422804014327
            slope[rows, columns] = (phi + pre_act * density).astype(jnp.bfloat16)

        for j in range(FF_WIDTH // FF_STEP):
            widen(j)
        for n in range(2):
            columns = slice(n * 512, (n + 1) * 512)
            total[rows, columns] = dot(activated[rows, :], w_down[:, columns])


        def second_norm(rows):
            summed = normed_out[rows, :] + total[rows, :] + vec[4:5, :]
            normed, inverse = norm_forward(summed)
            second_normed[rows, :] = normed
            second_inverse[rows, :] = jnp.broadcast_to(inverse, (STRIP, TILE))
            leaving[rows, :] = (normed * vec[7:8, :] + vec[5:6, :]).astype(jnp.bfloat16)

        strips(second_norm, first_row)

        @pl.when(section == 0)
        def _():
            passing(first_row, rows_in, number).start()

        @pl.when(section == 1)
        def _():
            ends_out[rows, :] = leaving[rows, :]

    halves(forward)
    store(rows_in, rows_in_far)
    store(context, context_far)
    store(normed_low, normed_low_far)
    store(activated, activated_far)

    @pl.when(section == 0)
    def _():
        for n in range(2):
            passing(n * HALF, rows_in, n).wait_send()

    def add_sum(row, values):
        sums[row : row + 1, :] += jnp.sum(values, axis=0, keepdims=True)

    def backward(number, first_row):
        rows = pl.ds(first_row, HALF)

        @pl.when(section == 0)
        def _():
            passing(first_row, cotangent, 2 + number).wait_recv()

        def second_back(rows):
            grad = cotangent[rows, :].astype(jnp.float32)
            normed = second_normed[rows, :]
            add_sum(5, grad)
            add_sum(7, grad * normed)
            grad = norm_backward(grad, normed, second_inverse[rows, 0:1], vec[7:8, :])
            add_sum(4, grad)
            normed_out[rows, :] = grad
            second_low[rows, :] = grad.astype(jnp.bfloat16)

        strips(second_back, first_row)
        for j in range(FF_WIDTH // FF_STEP):
            columns = slice(j * FF_STEP, (j + 1) * FF_STEP)
            row, first = j * FF_STEP // WIDTH, j * FF_STEP % WIDTH
            grad = dot_last(second_low[rows, :], w_down[columns, :]) * slope[rows, columns].astype(jnp.float32)
            sums[8 + row : 9 + row, first : first + FF_STEP] += jnp.sum(grad, axis=0, keepdims=True)
            pre_low[rows, columns] = grad.astype(jnp.bfloat16)
        for n in range(2):
            columns = slice(n * 512, (n + 1) * 512)
            total[rows, columns] = dot_last(pre_low[rows, :], w_in[columns, :])


        def first_back(rows):
            grad = normed_out[rows, :] + total[rows, :]
            normed = first_normed[rows, :]
            add_sum(3, grad)
            add_sum(6, grad * normed)
            grad = norm_backward(grad, normed, first_inverse[rows, 0:1], vec[6:7, :])
            add_sum(2, grad)
            normed_out[rows, :] = grad
            first_low[rows, :] = grad.astype(jnp.bfloat16)

        strips(first_back, first_row)
        context_grad = leaving
        for n in range(2):
            columns = slice(n * 512, (n + 1) * 512)
            context_grad[rows, columns] = dot_last(first_low[rows, :], w_out[columns, :]).astype(jnp.bfloat16)

        def attend_back(p, carry):
            query = qkv[rows, head_columns(p, 0)]
            key = qkv[rows, head_columns(p, 1)]
            value = qkv[rows, head_columns(p, 2)]
            grads = context_grad[rows, head_columns(p, 0)]
            results = [0.0, 0.0, 0.0]
            for h in (0, 1):
                own = grads * head_masks[h]
                low = chances[p * 4 + number * 2 + h]
                share = low.astype(jnp.float32)
                weight_grad = dot_last(own, value)
                inner = jnp.sum(share * weight_grad, axis=-1, keepdims=True)
                score = (share * (weight_grad - inner) * HEAD_DIM ** (-0.5)).astype(jnp.bfloat16)
                results[0] += dot(score, key * head_masks[h])
                results[1] += dot_first(score, query * head_masks[h])
                results[2] += dot_first(low, own)
            for part in range(3):
                joined[rows, head_columns(p, part)] = results[part].astype(jnp.bfloat16)
            for row, part in ((0, 0), (1, 2)):
                here = head_columns(p, 0)
                sums[row : row + 1, here] += jnp.sum(results[part], axis=0, keepdims=True)
            return carry

        lax.fori_loop(0, HEADS // 2, attend_back, 0)
        for n in range(2):
            columns = slice(n * 512, (n + 1) * 512)
            grad = normed_out[rows, columns] + dot_last(joined[rows, :], w_qkv[columns, :])
            leaving[rows, columns] = grad.astype(jnp.bfloat16)

        @pl.when(section == 1)
        def _():
            passing(first_row, cotangent, 2 + number).start()

        @pl.when(section == 0)
        def _():
            ends_out[rows, :] = leaving[rows, :]

    halves(backward)
    store(joined, joined_far)
    store(first_low, first_low_far)
    store(pre_low, pre_low_far)
    store(second_low, second_low_far)
    for f in range(N_F):
        small_rows[f, 0:8, :] = sums[0:8, f * TILE : (f + 1) * TILE]
        for i in range(4):
            first = (f % 2) * 512 + i * TILE
            small_rows[f, 8 + i : 9 + i, :] = sums[8 + f // 2 : 9 + f // 2, first : first + TILE]
        small_rows[f, 12:16, :] = jnp.zeros((4, TILE), jnp.float32)
    small_tile[...] = jnp.zeros_like(small_tile)
    for f in range(N_F):
        small_tile[f // 2, f % 2, 0:16, :] = small_rows[f].astype(jnp.bfloat16)
    store(small_tile, small_far)
    for copy in stores:
        copy.wait()
    copies.finish()

    @pl.when(section == 1)
    def _():
        for n in range(2):
            passing(n * HALF, cotangent, 2 + n).wait_send()


def run_layer(ends, ids, shards):
    low, full = jnp.bfloat16, jnp.float32
    scratch = [
        ((1024, 3072), low),
        ((1024, 1024), low),
        ((1024, 4096), low),
        ((4096, 1024), low),
        ((N_F * SMALL_ROWS, 2 * TILE), low),
        ((16, WIDTH), full),
        ((16, WIDTH), full),
        ((ROWS, WIDTH), low),
        ((ROWS, WIDTH), low),
        ((ROWS, WIDTH), low),
        ((ROWS, 3 * WIDTH), low),
        ((ROWS, WIDTH), low),
        ((ROWS, WIDTH), full),
        ((ROWS, TILE), full),
        ((ROWS, WIDTH), full),
        ((ROWS, WIDTH), low),
        ((ROWS, FF_WIDTH), low),
        ((ROWS, FF_WIDTH), low),
        ((ROWS, WIDTH), full),
        ((ROWS, TILE), full),
        ((2 * HEADS, TILE, TILE), low),
        ((ROWS, WIDTH), low),
        ((ROWS, FF_WIDTH), low),
        ((ROWS, WIDTH), low),
        ((ROWS, 3 * WIDTH), low),
        ((ROWS, WIDTH), full),
        ((N_F, SMALL_ROWS, TILE), full),
        ((4, 2, TILE, TILE), low),
    ]
    near = pl.BlockSpec(memory_space=pltpu.VMEM)
    far = pl.BlockSpec(memory_space=pl.ANY)
    return pl.pallas_call(
        layer_kernel,
        out_shape=[
            jax.ShapeDtypeStruct((ROWS, WIDTH), low),
            *[jax.ShapeDtypeStruct((ROWS, columns * WIDTH), low) for columns in (1, 1, 1, 4, 3, 1, 4, 1)],
            jax.ShapeDtypeStruct((4, 2, TILE, TILE), low),
        ],
        in_specs=[near, near, near, far, far, far, far, far],
        out_specs=[near, *[far] * 9],
        scratch_shapes=[
            *[pltpu.VMEM(shape, kind) for shape, kind in scratch],
            pltpu.SemaphoreType.DMA((5,)),
            pltpu.SemaphoreType.DMA((9,)),
            pltpu.SemaphoreType.DMA((4,)),
            pltpu.SemaphoreType.DMA((4,)),
            pltpu.SemaphoreType.DMA((GATHER_COPIES,)),
            pltpu.SemaphoreType.DMA((GATHER_COPIES,)),
        ],
        compiler_params=pltpu.CompilerParams(
            collective_id=2, has_side_effects=True, vmem_limit_bytes=VMEM_CAP
        ),
        name="run_layer",
    )(ends, ids[:, None], ids[None, :], *shards)


def pack_small(biases, gains, bias_in):
    rows = jnp.concatenate([biases, gains, bias_in.reshape(4, TILE)], axis=0)
    return jnp.pad(rows, ((0, 4), (0, TILE)))


def body(ends_in, segment_ids, w_qkv, w_out, w_in, w_down, biases, gains, bias_in):
    shards = (w_qkv[0], w_out[0], w_in[0], w_down[0], pack_small(biases[0], gains[0], bias_in[0]))
    ids = segment_ids + (lax.iota(jnp.int32, ROWS) // SEQ) * 16
    ends_out, *operands = run_layer(ends_in[0], ids, shards)
    outs = widen_outputs(reduce_grads(*operands))
    return tuple(member[None] for member in (ends_out, *outs))


def solution(mesh):
    in_specs = (
        P("section", ("fsdp", "replica"), None),
        P(("fsdp", "replica")),
        P("section", "fsdp", None),
        P("section", "fsdp", None),
        P("section", "fsdp", None),
        P("section", "fsdp", None),
        P("section", None, "fsdp"),
        P("section", None, "fsdp"),
        P("section", "fsdp"),
    )
    out_specs = (
        P("section", ("fsdp", "replica"), None),
        P("section", "fsdp", None),
        P("section", "fsdp", None),
        P("section", "fsdp", None),
        P("section", "fsdp", None),
        P("section", None, "fsdp"),
        P("section", None, "fsdp"),
        P("section", "fsdp"),
    )
    return jax.shard_map(body, mesh=mesh, in_specs=in_specs, out_specs=out_specs, check_vma=False)
```
